32 devices in a mesh: seq: 8 (over y, x, core), dp: 4 (over z).
Axes of the slice: x: 2, y: 2, z: 4, core: 2. Of those that a mesh axis runs over, the one named last changes fastest.
Arguments:
- tokens: bfloat16 [12, 1024, 1024], P('dp', 'seq'), may hold values from -6 to 6
- first_values: bfloat16 [12, 1024, 1024], P('dp', 'seq'), may hold values from -6 to 6
- out_grad: bfloat16 [12, 1024, 1024], P('dp', 'seq'), may hold values from -6 to 6
- lengths: int32 [12], P('dp'), may hold values from 1 to 1024, as said below
- norm1_gain: bfloat16 [1024], P(('seq', 'dp')), may hold values from 0.099609375 to 1.8984375
- qkv_weight: bfloat16 [1024, 3072], P(('seq', 'dp')), may hold values from -0.1875 to 0.1875
- out_weight: bfloat16 [1024, 1024], P(('seq', 'dp')), may hold values from -1.5 to 1.5
- norm2_gain: bfloat16 [1024], P(('seq', 'dp')), may hold values from 0.099609375 to 1.8984375
- gate_weight: bfloat16 [1024, 2816], P(('seq', 'dp')), may hold values from -0.1875 to 0.1875
- up_weight: bfloat16 [1024, 2816], P(('seq', 'dp')), may hold values from -0.1875 to 0.1875
- down_weight: bfloat16 [2816, 1024], P(('seq', 'dp')), may hold values from -0.109375 to 0.109375
Outputs:
- output: bfloat16 [12, 1024, 1024], P('dp', 'seq')
- tokens_grad: float32 [12, 1024, 1024], P('dp', 'seq')
- first_values_grad: float32 [12, 1024, 1024], P('dp', 'seq')
- norm1_gain_grad: float32 [1024], P(('seq', 'dp'))
- qkv_weight_grad: float32 [1024, 3072], P(('seq', 'dp'))
- out_weight_grad: float32 [1024, 1024], P(('seq', 'dp'))
- norm2_gain_grad: float32 [1024], P(('seq', 'dp'))
- gate_weight_grad: float32 [1024, 2816], P(('seq', 'dp'))
- up_weight_grad: float32 [1024, 2816], P(('seq', 'dp'))
- down_weight_grad: float32 [2816, 1024], P(('seq', 'dp'))
The draws below stay inside these ranges and needn't reach their ends.
Inputs may be any that keep to these rules, and one draw needn't show every extreme that they name: `lengths`: real tokens of a slot; within each index of dp one of its 3 slots, drawn from the seed, is full.
All inputs are finite; a program needn't handle non-finite values.
Results may differ from the reference program's by a relative error of at most 0.025.
Values may be sent and summed in bfloat16 or wider, within the bound.
No kernel may reach another device: no remote copies, remote signals or barrier semaphores. Data moves between devices by JAX's collectives and lax.ppermute only.
A program may use at most 320 MiB of HBM per device.

```python
import jax
import jax.numpy as jnp
from jax import lax

D = 1024
HEADS = 16
HEAD_DIM = 64
FF = 2816
MB = 3
SLOT = 1024
SLOTS = 12


def draw_lengths(key, part):
    key = jax.random.fold_in(key, 7)
    first_key, second_key = jax.random.split(key)
    ragged = jax.random.randint(first_key, (SLOTS,), 1, SLOT + 1)
    chosen = jax.random.randint(second_key, (SLOTS // MB,), 0, MB)
    selected = jnp.arange(SLOTS) % MB == jnp.repeat(chosen, MB)
    return jnp.where(selected, SLOT, ragged).astype(jnp.int32)


def shard_levels(key, dims, pieces, smallest, largest):
    gain = 1.0
    for axis_at, blocks in pieces:
        heights = jax.random.uniform(jax.random.fold_in(jax.random.fold_in(key, 6), axis_at), (blocks,), jnp.float32, smallest / len(pieces), largest / len(pieces))
        gain = gain * jnp.repeat(jnp.exp(heights), dims[axis_at] // blocks).reshape((-1,) + (1,) * (len(dims) - 1 - axis_at))
    return gain


def centred(stream_key, extent, deviation, bound, pieces=(), held_as=jnp.bfloat16):
    drawn = jax.random.normal(stream_key, extent, jnp.float32) * deviation
    if len(pieces) > 0:
        drawn = shard_levels(stream_key, extent, pieces, -0.22, 0.18) * drawn
    return jnp.clip(drawn, min=-bound, max=bound).astype(held_as)


def setup_inputs(seed: int = 0) -> dict:
    splits = jax.random.split(jax.random.key(seed), 12)
    tokens = centred(splits[0], (SLOTS, SLOT, D), 1.0, 6.0, ((0, 4), (1, 8)))
    first_values = centred(splits[1], (SLOTS, SLOT, D), 1.0, 6.0, ((0, 4), (1, 8)))
    out_grad = centred(splits[2], (SLOTS, SLOT, D), 1.0, 6.0, ((0, 4), (1, 8)))
    lengths = draw_lengths(jax.random.fold_in(splits[11], 71), 0)
    norm1_gain = jnp.clip(1.0 + 0.18 * jax.random.normal(splits[4], (D,), jnp.float32), 0.099609375, 1.8984375).astype(jnp.bfloat16)
    qkv_weight = centred(splits[5], (D, 3 * D), D ** -0.5, 0.1875, ((0, 32),))
    out_weight = centred(splits[6], (D, D), (D // 64) ** -0.5, 1.5, ((0, 32),))
    norm2_gain = jnp.clip(1.0 + 0.18 * jax.random.normal(splits[7], (D,), jnp.float32), 0.099609375, 1.8984375).astype(jnp.bfloat16)
    gate_weight = centred(splits[8], (D, FF), D ** -0.5, 0.1875, ((0, 32),))
    up_weight = centred(splits[9], (D, FF), D ** -0.5, 0.1875, ((0, 32),))
    down_weight = centred(splits[10], (FF, D), FF ** -0.5, 0.109375, ((0, 32),))
    return {"tokens": tokens, "first_values": first_values, "out_grad": out_grad, "lengths": lengths, "norm1_gain": norm1_gain, "qkv_weight": qkv_weight, "out_weight": out_weight, "norm2_gain": norm2_gain, "gate_weight": gate_weight, "up_weight": up_weight, "down_weight": down_weight}


@jax.custom_vjp
def low(v):
    return lax.optimization_barrier(v.astype(jnp.bfloat16)).astype(jnp.float32)

@jax.custom_vjp
def low_back(v):
    return v

def low_keep(v):
    return (low(v), None)

def low_pass(kept, grad):
    return (grad,)

def back_keep(v):
    return (v, None)

def back_low(kept, grad):
    return (low(grad),)
low.defvjp(low_keep, low_pass)
low_back.defvjp(back_keep, back_low)
EPSILON = 1e-06

def product(left, right):
    return jnp.dot(left, right, precision=lax.Precision.HIGHEST)

def rotate_half(values):
    half_dim = values.shape[-1] // 2
    return jnp.concatenate([-values[..., half_dim:], values[..., :half_dim]], -1)

def rotate(values, cosine, sine_table):
    return values * cosine[:, None, :] + rotate_half(values) * sine_table[:, None, :]

def layer(param_set, inputs, value_rows, length):
    gain1, wqkv, wout, gain2, wgate, wup, wdown = param_set
    positions = jnp.arange(SLOT, dtype=jnp.int32)
    inverse = 10000.0 ** (-jnp.arange(0, HEAD_DIM, 2, dtype=jnp.float32) / HEAD_DIM)
    angles = positions.astype(jnp.float32)[:, None] * inverse[None, :]
    angles = jnp.concatenate([angles, angles], -1)
    cosine, sine_table = (jnp.cos(angles), jnp.sin(angles))
    inv1 = lax.rsqrt(lax.optimization_barrier(jnp.mean(inputs * inputs, -1, keepdims=True)) + EPSILON)
    normed = low(inputs * inv1 * gain1)
    projected = low_back(product(normed, wqkv))
    queries = projected[:, :D].reshape(SLOT, HEADS, HEAD_DIM)
    keys_raw = projected[:, D:2 * D].reshape(SLOT, HEADS, HEAD_DIM)
    values_raw = projected[:, 2 * D:].reshape(SLOT, HEADS, HEAD_DIM)
    query_rot = low(rotate(queries, cosine, sine_table))
    key_rot = low(rotate(keys_raw, cosine, sine_table))
    mixed = low(0.5 * values_raw + 0.5 * value_rows.reshape(SLOT, HEADS, HEAD_DIM))
    scores = low_back(jnp.einsum('qhd,khd->hqk', query_rot, key_rot, precision=lax.Precision.HIGHEST) * float(HEAD_DIM) ** (-0.5))
    allowed = (positions[None, :] <= positions[:, None]) & (positions[None, :] < length)
    scores = jnp.where(allowed[None], scores, -1e+30)
    weights = jax.nn.softmax(scores, -1)
    attended = jnp.einsum('hqk,khd->qhd', low(weights), mixed, precision=lax.Precision.HIGHEST).reshape(SLOT, D)
    attended = low_back(low(attended))
    middle = inputs + low_back(product(attended, wout))
    inv2 = lax.rsqrt(lax.optimization_barrier(jnp.mean(middle * middle, -1, keepdims=True)) + EPSILON)
    normed2 = low(middle * inv2 * gain2)
    gate = low_back(product(normed2, wgate))
    upward = low_back(product(normed2, wup))
    hidden = low(jax.nn.silu(gate) * upward)
    return middle + low_back(product(hidden, wdown))

def reference(tokens, first_values, out_grad, lengths, norm1_gain, qkv_weight, out_weight, norm2_gain, gate_weight, up_weight, down_weight):
    params = tuple((item.astype(jnp.float32) for item in (norm1_gain, qkv_weight, out_weight, norm2_gain, gate_weight, up_weight, down_weight)))
    initial = tuple((jnp.zeros(item.shape, jnp.float32) for item in params))

    def per_slot(running, slot_items):
        token_rows, value_rows, grad_rows, length = slot_items

        def forward(param_set, token_float, value_float):
            return layer(param_set, token_float, value_float, length)
        result, pull = jax.vjp(forward, params, token_rows.astype(jnp.float32), value_rows.astype(jnp.float32))
        grad_params, grad_tokens, grad_values = pull(grad_rows.astype(jnp.float32))
        running = tuple((first + second for first, second in zip(running, grad_params)))
        return (running, (result.astype(jnp.bfloat16), grad_tokens, grad_values))
    running, stacked = lax.scan(per_slot, initial, (tokens, first_values, out_grad, lengths))
    return (stacked[0], stacked[1], stacked[2], running[0], running[1], running[2], running[3], running[4], running[5], running[6])
```

```python
import functools

import jax
import jax.numpy as jnp
from jax import lax
from jax.experimental import pallas as pl
from jax.experimental.pallas import tpu as pltpu
from jax.sharding import PartitionSpec as P

HEADS = 16
HEAD_DIM = 64
EPSILON = 1e-06
CORES = 2
OUTER = 2
BLOCK = 256
NEG = -1e30
F32 = jnp.float32
BF16 = jnp.bfloat16
VMEM_LIMIT = 60 * 1024 * 1024


def dot_nn(a, b):
    return lax.dot_general(a, b, (((1,), (0,)), ((), ())), preferred_element_type=F32)


def dot_nt(a, b):
    return lax.dot_general(a, b, (((1,), (1,)), ((), ())), preferred_element_type=F32)


def dot_tn(a, b):
    return lax.dot_general(a, b, (((0,), (0,)), ((), ())), preferred_element_type=F32)


def turned(u):
    half = HEAD_DIM // 2
    width = u.shape[1]
    if width % 128:
        parts = []
        for h in range(width // HEAD_DIM):
            lo = h * HEAD_DIM
            parts += [u[:, lo + half : lo + HEAD_DIM], u[:, lo : lo + half]]
        return jnp.concatenate(parts, axis=1)
    lane = lax.broadcasted_iota(jnp.int32, u.shape, 1) % HEAD_DIM
    return jnp.where(lane < half, pltpu.roll(u, width - half, 1), pltpu.roll(u, half, 1))


def head_mask(shape, h):
    lane = lax.broadcasted_iota(jnp.int32, shape, 1)
    return (lane >= h * HEAD_DIM) & (lane < (h + 1) * HEAD_DIM)


def own_head(u, h):
    if u.shape[1] == HEAD_DIM:
        return u
    return jnp.where(head_mask(u.shape, h), u, jnp.zeros_like(u))


def join_heads(parts):
    out = parts[0]
    for h in range(1, len(parts)):
        out = jnp.where(head_mask(out.shape, h), parts[h], out)
    return out


def fill_rows(seat, refs, dest, rows):
    for ref, ms in refs:
        for j, m in enumerate(ms):
            at = pl.multiple_of((seat ^ m) * rows, rows)
            dest[pl.ds(at, rows), :] = ref[j, 0]


def attn_fwd_kernel(
    order, seat_ref, len_ref, xa0, xa1, xb0, xb1, w_ref, v1_ref, cos_ref, sin_ref,
    qkv_out, ot_out, send_out, lse_out, r1_out, xbuf, vt,
):
    slot = pl.program_id(0)
    seat = seat_ref[0]
    rows = xa0.shape[2]
    length = len_ref[slot]
    total = xbuf.shape[0]
    wide = w_ref.shape[1] // 3
    heads = wide // HEAD_DIM
    blocks = total // BLOCK
    per = BLOCK // rows
    fill_rows(seat, zip((xa0, xa1, xb0, xb1), order), xbuf, rows)
    for b in range(blocks):
        at = slice(b * BLOCK, (b + 1) * BLOCK)
        x = xbuf[at, :]
        xf = x.astype(F32)
        r1 = lax.rsqrt(jnp.mean(xf * xf, axis=1, keepdims=True) + EPSILON)
        qkv = dot_nn(x, w_ref[...]) * r1
        cosine = cos_ref[at, :]
        sine = sin_ref[at, :]
        q = qkv[:, :wide]
        k = qkv[:, wide : 2 * wide]
        v = qkv[:, 2 * wide :]
        q = (q * cosine + turned(q) * sine) * (HEAD_DIM**-0.5)
        k = k * cosine + turned(k) * sine
        v1 = v1_ref[b * per : (b + 1) * per, 0].reshape(BLOCK, wide).astype(F32)
        vm = 0.5 * v + 0.5 * v1
        qkv_out[0, at, :wide] = q.astype(BF16)
        qkv_out[0, at, wide : 2 * wide] = k.astype(BF16)
        qkv_out[0, at, 2 * wide :] = vm.astype(BF16)
        vt[:, at] = vm.T.astype(BF16)
        r1_out[0, at, :] = jnp.broadcast_to(r1, (BLOCK, r1_out.shape[2]))
    for b in range(blocks):
        at = slice(b * BLOCK, (b + 1) * BLOCK)
        count = (b + 1) * BLOCK
        q = qkv_out[0, at, :wide]
        query = b * BLOCK + lax.broadcasted_iota(jnp.int32, (1, BLOCK), 1)
        last = jnp.minimum(query, length - 1)
        key = lax.broadcasted_iota(jnp.int32, (count, BLOCK), 0)
        allowed = key <= last
        ots = []
        for h in range(heads):
            k = own_head(qkv_out[0, :count, wide : 2 * wide], h)
            scores = jnp.where(allowed, dot_nt(k, q), NEG)
            top = jnp.max(scores, axis=0, keepdims=True)
            weights = jnp.exp(scores - top)
            total_w = jnp.sum(weights, axis=0, keepdims=True)
            ot = dot_nn(vt[h * HEAD_DIM : (h + 1) * HEAD_DIM, :count], weights.astype(BF16))
            ots.append(ot / total_w)
            lse_out[0, h : h + 1, at] = top + jnp.log(total_w)
        ot = jnp.concatenate(ots, axis=0)
        ot_out[0, :, at] = ot
        o = ot.T.astype(BF16)
        half = total // OUTER
        spread = send_out.shape[0] // OUTER
        group = (b * BLOCK) // half
        start = b * BLOCK - group * half
        for j in range(spread):
            send_out[group * spread + j, 0, start : start + BLOCK, :] = o


def attn_fwd(seat, lengths, xs, w, v1, cosine, sine, order):
    xa0, xa1, xb0, xb1 = xs
    spread, micro, rows, width = xa0.shape
    total = rows * 4 * spread
    wide = w.shape[1] // 3
    heads = wide // HEAD_DIM
    smem = pl.BlockSpec(memory_space=pltpu.SMEM)
    whole = lambda a: pl.BlockSpec(a.shape, lambda i: (0,) * a.ndim)
    xspec = pl.BlockSpec((spread, 1, rows, width), lambda i: (0, i, 0, 0))
    pairs = total * total // 2 * micro * wide
    return pl.pallas_call(
        functools.partial(attn_fwd_kernel, order),
        grid=(micro,),
        in_specs=[
            smem, smem, xspec, xspec, xspec, xspec, whole(w),
            pl.BlockSpec((v1.shape[0], 1, rows, wide), lambda i: (0, i, 0, 0)),
            whole(cosine), whole(sine),
        ],
        out_specs=[
            pl.BlockSpec((1, total, 3 * wide), lambda i: (i, 0, 0)),
            pl.BlockSpec((1, wide, total), lambda i: (i, 0, 0)),
            pl.BlockSpec((OUTER * spread, 1, total // OUTER, wide), lambda i: (0, i, 0, 0)),
            pl.BlockSpec((1, heads, total), lambda i: (i, 0, 0)),
            pl.BlockSpec((1, total, 128), lambda i: (i, 0, 0)),
        ],
        out_shape=[
            jax.ShapeDtypeStruct((micro, total, 3 * wide), BF16),
            jax.ShapeDtypeStruct((micro, wide, total), F32),
            jax.ShapeDtypeStruct((OUTER * spread, micro, total // OUTER, wide), BF16),
            jax.ShapeDtypeStruct((micro, heads, total), F32),
            jax.ShapeDtypeStruct((micro, total, 128), F32),
        ],
        scratch_shapes=[pltpu.VMEM((total, width), BF16), pltpu.VMEM((wide, total), BF16)],
        compiler_params=pltpu.CompilerParams(vmem_limit_bytes=VMEM_LIMIT),
        cost_estimate=pl.CostEstimate(
            flops=2 * micro * total * width * 3 * wide + 16 * pairs,
            bytes_accessed=2 * micro * total * (width + 16 * wide),
            transcendentals=micro * heads * total * total // 2,
        ),
        name="attn_fwd",
    )(seat, lengths, xa0, xa1, xb0, xb1, w, v1, cosine, sine)


def attn_bwd_kernel(
    order, seat_ref, len_ref, xa0, xa1, xb0, xb1, w_ref, do_ref, cos_ref, sin_ref, qkv_ref, ot_ref,
    lse_ref, r1_ref, dv_out, za0, za1, zb0, zb1, dw_out, xbuf, dobuf, dqt, ebuf, zbuf, dw,
):
    slot = pl.program_id(0)
    seat = seat_ref[0]
    rows = xa0.shape[2]
    length = len_ref[slot]
    total = xbuf.shape[0]
    wide = w_ref.shape[1] // 3
    heads = wide // HEAD_DIM
    blocks = total // BLOCK
    per = BLOCK // rows
    fill_rows(seat, zip((xa0, xa1, xb0, xb1), order), xbuf, rows)
    for j in range(do_ref.shape[0]):
        dobuf[j * rows : (j + 1) * rows, :] = do_ref[j, 0]
    deltas = []
    for h in range(heads):
        part = slice(h * HEAD_DIM, (h + 1) * HEAD_DIM)
        deltas.append(None)
    dot_t = dobuf[...].astype(F32).T
    for h in range(heads):
        part = slice(h * HEAD_DIM, (h + 1) * HEAD_DIM)
        deltas[h] = jnp.sum(dot_t[part, :] * ot_ref[0, part, :], axis=0, keepdims=True)
    dqt[...] = jnp.zeros_like(dqt)
    for b in range(blocks):
        at = slice(b * BLOCK, (b + 1) * BLOCK)
        later = slice(b * BLOCK, total)
        count = total - b * BLOCK
        k = qkv_ref[0, at, wide : 2 * wide]
        v = qkv_ref[0, at, 2 * wide :]
        kt = k.astype(F32).T.astype(BF16)
        q = qkv_ref[0, later, :wide]
        d_o = dobuf[later, :]
        query = b * BLOCK + lax.broadcasted_iota(jnp.int32, (1, count), 1)
        last = jnp.minimum(query, length - 1)
        key = b * BLOCK + lax.broadcasted_iota(jnp.int32, (BLOCK, count), 0)
        allowed = key <= last
        dks, dvs = [], []
        for h in range(heads):
            part = slice(h * HEAD_DIM, (h + 1) * HEAD_DIM)
            scores = jnp.where(allowed, dot_nt(own_head(k, h), q), NEG)
            weights = jnp.exp(scores - lse_ref[0, h : h + 1, later])
            d_weights = dot_nt(own_head(v, h), d_o)
            ds = (weights * (d_weights - deltas[h][:, later])).astype(BF16)
            dvs.append(dot_nn(weights.astype(BF16), d_o))
            dks.append(dot_nn(ds, q))
            dqt[part, later] += dot_nn(kt[part, :], ds)
        cosine = cos_ref[at, :]
        sine = sin_ref[at, :]
        r1 = r1_ref[0, at, 0:1]
        dk = join_heads(dks)
        dk = dk * cosine - turned(dk) * sine
        dv = 0.5 * join_heads(dvs)
        dv_out[b * per : (b + 1) * per, 0] = dv.astype(BF16).reshape(per, rows, wide)
        ebuf[at, wide : 2 * wide] = (dk * r1).astype(BF16)
        ebuf[at, 2 * wide :] = (dv * r1).astype(BF16)
    for b in range(blocks):
        at = slice(b * BLOCK, (b + 1) * BLOCK)
        dq = dqt[:, at].T * (HEAD_DIM**-0.5)
        dq = dq * cos_ref[at, :] - turned(dq) * sin_ref[at, :]
        ebuf[at, :wide] = (dq * r1_ref[0, at, 0:1]).astype(BF16)
        zbuf[at, :] = dot_nt(ebuf[at, :], w_ref[...]).astype(BF16)
    for ref, ms in zip((za0, za1, zb0, zb1), order):
        for j, m in enumerate(ms):
            ref[j, 0] = zbuf[pl.ds(pl.multiple_of((seat ^ m) * rows, rows), rows), :]
    grown = dot_tn(xbuf[...], ebuf[...])

    @pl.when(slot == 0)
    def _():
        dw[...] = grown

    @pl.when(slot > 0)
    def _():
        dw[...] += grown

    @pl.when(slot == pl.num_programs(0) - 1)
    def _():
        dw_out[...] = dw[...].astype(BF16)


def attn_bwd(seat, lengths, xs, w, d_o, cosine, sine, qkv, ot, lse, r1, order):
    xa0 = xs[0]
    spread, micro, rows, width = xa0.shape
    total = rows * 4 * spread
    wide = w.shape[1] // 3
    heads = wide // HEAD_DIM
    smem = pl.BlockSpec(memory_space=pltpu.SMEM)
    whole = lambda a: pl.BlockSpec(a.shape, lambda i: (0,) * a.ndim)
    xspec = pl.BlockSpec((spread, 1, rows, width), lambda i: (0, i, 0, 0))
    vspec = pl.BlockSpec((d_o.shape[0], 1, rows, wide), lambda i: (0, i, 0, 0))
    zshape = jax.ShapeDtypeStruct(xa0.shape, BF16)
    pairs = total * total // 2 * micro * wide
    return pl.pallas_call(
        functools.partial(attn_bwd_kernel, order),
        grid=(micro,),
        in_specs=[
            smem, smem, xspec, xspec, xspec, xspec, whole(w), vspec, whole(cosine), whole(sine),
            pl.BlockSpec((1, total, 3 * wide), lambda i: (i, 0, 0)),
            pl.BlockSpec((1, wide, total), lambda i: (i, 0, 0)),
            pl.BlockSpec((1, heads, total), lambda i: (i, 0, 0)),
            pl.BlockSpec((1, total, 128), lambda i: (i, 0, 0)),
        ],
        out_specs=[vspec, xspec, xspec, xspec, xspec, pl.BlockSpec(w.shape, lambda i: (0, 0))],
        out_shape=[
            jax.ShapeDtypeStruct(d_o.shape, BF16), zshape, zshape, zshape, zshape,
            jax.ShapeDtypeStruct(w.shape, BF16),
        ],
        scratch_shapes=[
            pltpu.VMEM((total, width), BF16),
            pltpu.VMEM((total, wide), BF16),
            pltpu.VMEM((wide, total), F32),
            pltpu.VMEM((total, 3 * wide), BF16),
            pltpu.VMEM((total, width), BF16),
            pltpu.VMEM(w.shape, F32),
        ],
        compiler_params=pltpu.CompilerParams(vmem_limit_bytes=VMEM_LIMIT),
        cost_estimate=pl.CostEstimate(
            flops=4 * micro * total * width * 3 * wide + 40 * pairs,
            bytes_accessed=2 * micro * total * (2 * width + 24 * wide),
            transcendentals=micro * heads * total * total // 2,
        ),
        name="attn_bwd",
    )(seat, lengths, *xs, w, d_o, cosine, sine, qkv, ot, lse, r1)


def ff_kernel(
    seat_ref, xa, xb, ga, gb, oa_lo, ob_lo, oa_hi, ob_hi, wout_ref, wg_ref, wu_ref, wd_ref,
    za, zb, fa, fb, y_out, o_out, dwg_out, dwu_out, dwd_out, dwg, dwu, dwd,
):
    step = pl.program_id(0)
    core = seat_ref[0] % CORES
    micro, rows, width = xa.shape[1:]
    many = micro * rows

    def attended(mine, other):
        parts = []
        for j in range(mine.shape[0]):
            a = mine[j].reshape(many, mine.shape[3])
            b = other[j].reshape(many, other.shape[3])
            parts += [jnp.where(core == 0, a, b), jnp.where(core == 0, b, a)]
        return jnp.concatenate(parts, axis=1)

    @pl.when(step == 0)
    def _():
        dwg[...] = jnp.zeros_like(dwg)
        dwu[...] = jnp.zeros_like(dwu)
        dwd[...] = jnp.zeros_like(dwd)

    for x_ref, g_ref, mine, other, z_ref, f_ref, own in (
        (xa, ga, oa_lo, ob_lo, za, fa, True),
        (xb, gb, oa_hi, ob_hi, zb, fb, False),
    ):
        o = attended(mine, other)
        x = x_ref[0].reshape(many, width).astype(F32)
        g = g_ref[0].reshape(many, width)
        y = x + dot_nn(o, wout_ref[...])
        r2 = lax.rsqrt(jnp.mean(y * y, axis=1, keepdims=True) + EPSILON)
        hn = (y * r2).astype(BF16)
        if own:

            @pl.when(step == 0)
            def _():
                y_out[...] = y
                o_out[...] = o

        gate = dot_nn(hn, wg_ref[...])
        up = dot_nn(hn, wu_ref[...])
        sigma = jax.nn.sigmoid(gate)
        act = gate * sigma
        hid = (act * up).astype(BF16)
        dhid = dot_nt(g, wd_ref[...])
        dgate = (dhid * up * sigma * (1.0 + gate * (1.0 - sigma))).astype(BF16)
        dup = (dhid * act).astype(BF16)
        f_ref[0] = dot_nn(hid, wd_ref[...]).astype(BF16)
        z_ref[0] = (dot_nt(dgate, wg_ref[...]) + dot_nt(dup, wu_ref[...])).astype(BF16)
        dwg[...] += dot_tn(hn, dgate)
        dwu[...] += dot_tn(hn, dup)
        dwd[...] += dot_tn(hid, g)

    @pl.when(step == pl.num_programs(0) - 1)
    def _():
        dwg_out[...] = dwg[...].astype(BF16)
        dwu_out[...] = dwu[...].astype(BF16)
        dwd_out[...] = dwd[...].astype(BF16)


def feed_forward(seat, xa, xb, ga, gb, oa, ob, wout, wg, wu, wd):
    spread, micro, rows, width = xa.shape
    many = micro * rows
    group = spread * CORES
    wide = oa.shape[3]
    fan = wg.shape[1]
    whole = lambda a: pl.BlockSpec(a.shape, lambda i, s: (0,) * a.ndim)
    xspec = pl.BlockSpec((1, micro, rows, width), lambda i, s: (i, 0, 0, 0))

    def ospec(low):
        return pl.BlockSpec(
            (oa.shape[0], micro, rows, wide),
            lambda i, s: (0, 0, (s[0] % group) ^ (2 * i + low), 0),
        )

    zspec = pl.BlockSpec((1, many, width), lambda i, s: (i, 0, 0))
    zshape = jax.ShapeDtypeStruct((spread, many, width), BF16)
    fixed = lambda shape: pl.BlockSpec(shape, lambda i, s: (0,) * len(shape))
    tokens = group * many
    return pl.pallas_call(
        ff_kernel,
        grid_spec=pltpu.PrefetchScalarGridSpec(
            num_scalar_prefetch=1,
            grid=(spread,),
            in_specs=[
                xspec, xspec, xspec, xspec, ospec(0), ospec(0), ospec(1), ospec(1),
                whole(wout), whole(wg), whole(wu), whole(wd),
            ],
            out_specs=[
                zspec, zspec, zspec, zspec, fixed((many, width)), fixed((many, width)),
                fixed(wg.shape), fixed(wu.shape), fixed(wd.shape),
            ],
            scratch_shapes=[
                pltpu.VMEM(wg.shape, F32), pltpu.VMEM(wu.shape, F32), pltpu.VMEM(wd.shape, F32),
            ],
        ),
        out_shape=[
            zshape, zshape, zshape, zshape,
            jax.ShapeDtypeStruct((many, width), F32),
            jax.ShapeDtypeStruct((many, width), BF16),
            jax.ShapeDtypeStruct(wg.shape, BF16),
            jax.ShapeDtypeStruct(wu.shape, BF16),
            jax.ShapeDtypeStruct(wd.shape, BF16),
        ],
        compiler_params=pltpu.CompilerParams(vmem_limit_bytes=VMEM_LIMIT),
        cost_estimate=pl.CostEstimate(
            flops=2 * tokens * width * (width + 9 * fan),
            bytes_accessed=2 * tokens * width * 6 + 20 * width * fan,
            transcendentals=tokens * fan,
        ),
        name="feed_forward",
    )(seat, xa, xb, ga, gb, oa, ob, oa, ob, wout, wg, wu, wd)


def rope_tables(total, wide):
    positions = jnp.arange(total, dtype=jnp.int32).astype(F32)
    inverse = 10000.0 ** (-jnp.arange(0, HEAD_DIM, 2, dtype=F32) / HEAD_DIM)
    angles = positions[:, None] * inverse[None, :]
    cosine, sine = jnp.cos(angles), jnp.sin(angles)
    cosine = jnp.tile(cosine, (1, 2 * wide // HEAD_DIM))
    sine = jnp.tile(jnp.concatenate([-sine, sine], -1), (1, wide // HEAD_DIM))
    return cosine, sine


def local(
    tokens, first_values, out_grad, lengths, norm1_gain, qkv_weight, out_weight, norm2_gain,
    gate_weight, up_weight, down_weight,
):
    micro, rows, width = tokens.shape
    seats, depth = lax.axis_size("seq"), lax.axis_size("dp")
    devices = seats * depth
    seat = lax.axis_index("seq")
    group = seats // OUTER
    spread = group // CORES
    outer = seat // group
    total = seats * rows
    wide = width // seats
    held = qkv_weight.shape[0]
    fan_rows = down_weight.shape[0]
    fan = fan_rows * devices
    piece = fan // seats
    slab = OUTER * piece
    padded = -(-slab // 128) * 128
    many = micro * rows
    seat_arr = jnp.reshape(seat, (1,)).astype(jnp.int32)

    def swap(value, mask):
        return lax.ppermute(value, "seq", [(i, i ^ mask) for i in range(seats)])

    same_core = [[i for i in range(seats) if i % CORES == c] for c in range(CORES)]
    same_outer = [list(range(o * group, (o + 1) * group)) for o in range(OUTER)]
    every = ("seq", "dp")

    gain1 = norm1_gain.astype(F32)[:, None]
    gain2 = norm2_gain.astype(F32)[:, None]

    inner = [2 * j for j in range(spread)]
    across = [group + 2 * j for j in range(spread)]
    xa0 = jnp.stack([tokens] + [swap(tokens, m) for m in inner[1:]])
    xb0 = swap(xa0, 1)
    xa1 = jnp.stack([swap(tokens, m) for m in across])
    xb1 = swap(xa1, 1)
    order = (
        tuple(inner), tuple(across), tuple(m + 1 for m in inner), tuple(m + 1 for m in across),
    )
    xs = (xa0, xa1, xb0, xb1)

    wqkv = (qkv_weight.astype(F32) * gain1).astype(BF16)
    wqkv = wqkv.reshape(held, 3, seats, wide).transpose(2, 0, 1, 3).reshape(seats, 1, held, 3 * wide)
    wqkv = jnp.broadcast_to(wqkv, (seats, depth, held, 3 * wide)).reshape(devices, held, 3 * wide)
    wqkv = lax.all_to_all(wqkv, every, split_axis=0, concat_axis=0, tiled=True)
    wqkv = wqkv.reshape(width, 3 * wide)

    v1 = first_values.reshape(micro, rows, seats, wide).transpose(2, 0, 1, 3)
    v1 = lax.all_to_all(v1, "seq", split_axis=0, concat_axis=0, tiled=True)

    def columns(weight):
        scaled = (weight.astype(F32) * gain2).astype(BF16)
        return scaled.reshape(held, OUTER, group, piece).transpose(2, 0, 1, 3).reshape(group, held, slab)

    pair = jnp.concatenate([columns(gate_weight), columns(up_weight)], -1)
    pair = lax.all_to_all(
        pair, "seq", split_axis=0, concat_axis=0, tiled=True, axis_index_groups=same_outer
    )

    def both_outer(value):
        other = swap(value, group)
        return jnp.where(outer == 0, jnp.stack([value, other]), jnp.stack([other, value]))

    pair = lax.all_gather(both_outer(pair), "dp", axis=0)
    pair = pair.transpose(1, 2, 0, 3, 4).reshape(width, 2 * slab)
    grow = ((0, 0), (0, padded - slab))
    wg = jnp.pad(pair[:, :slab], grow)
    wu = jnp.pad(pair[:, slab:], grow)

    tail = jnp.concatenate([down_weight, out_weight], 0)
    tail = lax.all_gather(both_outer(tail), "dp", axis=0)
    wd = tail[:, :, :fan_rows].transpose(1, 0, 2, 3).reshape(slab, width)
    wd = jnp.pad(wd, ((0, padded - slab), (0, 0)))
    wout = tail[:, :, fan_rows:].transpose(1, 0, 2, 3)[:, None, None]
    inner_at = (seat % group) // CORES
    core = seat % CORES
    pieces = jnp.stack([wout] + [swap(wout, m) for m in inner[1:]])
    wout = jnp.concatenate([pieces[inner_at ^ j] for j in range(spread)], 1)
    other = swap(wout, 1)
    wout = jnp.where(
        core == 0, jnp.concatenate([wout, other], 2), jnp.concatenate([other, wout], 2)
    ).reshape(width, width)

    ga = jnp.stack([out_grad] + [swap(out_grad, m) for m in inner[1:]])
    gb = swap(ga, 1)

    cosine, sine = rope_tables(total, wide)
    qkv, ot, send, lse, r1 = attn_fwd(seat_arr, lengths, xs, wqkv, v1, cosine, sine, order)
    oa = lax.all_to_all(
        send, "seq", split_axis=0, concat_axis=0, tiled=True, axis_index_groups=same_core
    )
    ob = swap(oa, 1)
    za, zb, fa, fb, y, o_own, dwg, dwu, dwd = feed_forward(
        seat_arr, xa0, xb0, ga, gb, oa, ob, wout, wg, wu, wd
    )

    def gathered(mine, theirs):
        joined = (mine.astype(F32) + swap(theirs, 1).astype(F32)).astype(BF16)
        out = joined[0].astype(F32)
        for j in range(1, spread):
            out = out + swap(joined[j], inner[j]).astype(F32)
        return out

    z = gathered(za, zb)
    grad = out_grad.reshape(many, width).astype(F32)
    r2 = lax.rsqrt(jnp.mean(y * y, -1, keepdims=True) + EPSILON)
    dy = grad + r2 * z - y * (r2 * r2 * r2) * jnp.mean(z * y, -1, keepdims=True)
    dyb = dy.astype(BF16)
    d_o = dot_nt(dyb, wout).astype(BF16)
    d_o = d_o.reshape(micro, rows, seats, wide).transpose(2, 0, 1, 3)
    d_o = lax.all_to_all(d_o, "seq", split_axis=0, concat_axis=0, tiled=True)
    output = (y + gathered(fa, fb)).astype(BF16).reshape(tokens.shape)

    pair = jnp.concatenate([dwg[:, :slab], dwu[:, :slab]], -1)
    pair = pair.reshape(OUTER, group, depth, held, 2 * slab).transpose(2, 0, 1, 3, 4)
    dwd = dwd[:slab].reshape(OUTER, depth, fan_rows, width).transpose(1, 0, 2, 3)
    dwd = lax.psum_scatter(dwd, "dp", scatter_dimension=0)
    pair = lax.psum_scatter(pair, "dp", scatter_dimension=0)

    def own_outer(value):
        mine = jnp.where(outer == 0, value[0], value[1])
        theirs = jnp.where(outer == 0, value[1], value[0])
        return mine.astype(F32) + swap(theirs, group).astype(F32)

    down_grad = own_outer(dwd)
    pair = own_outer(pair).astype(BF16)
    pair = lax.all_to_all(
        pair, "seq", split_axis=0, concat_axis=0, tiled=True, axis_index_groups=same_outer
    )
    pair = pair.reshape(group, held, 2, OUTER, piece).transpose(2, 1, 3, 0, 4).reshape(2, held, fan)
    pair = pair.astype(F32)
    gate_grad, up_grad = pair[0] * gain2, pair[1] * gain2
    gain2_grad = jnp.sum(
        pair[0] * gate_weight.astype(F32) + pair[1] * up_weight.astype(F32), -1
    )

    d_wout = dot_tn(o_own, dyb).astype(BF16)
    out_grad_w = lax.psum_scatter(
        d_wout.reshape(devices, held, width), every, scatter_dimension=0
    ).astype(F32)

    dv, xz0, xz1, xw0, xw1, dwq = attn_bwd(
        seat_arr, lengths, xs, wqkv, d_o, cosine, sine, qkv, ot, lse, r1, order
    )
    dv = lax.all_to_all(dv, "seq", split_axis=0, concat_axis=0, tiled=True)
    d_first = dv.transpose(1, 2, 0, 3).reshape(tokens.shape).astype(F32)
    dwq = lax.all_to_all(
        dwq.reshape(devices, held, 3 * wide), every, split_axis=0, concat_axis=0, tiled=True
    )
    dwq = jnp.sum(dwq.reshape(seats, depth, held, 3, wide).astype(F32), 1)
    dwq = dwq.transpose(1, 2, 0, 3).reshape(held, 3 * width)
    gain1_grad = jnp.sum(dwq * qkv_weight.astype(F32), -1)
    qkv_grad = dwq * gain1

    near = (xz0.astype(F32) + swap(xw0, 1).astype(F32)).astype(BF16)
    far = (xz1.astype(F32) + swap(xw1, 1).astype(F32)).astype(BF16)
    z1 = near[0].astype(F32)
    for j in range(1, spread):
        z1 = z1 + swap(near[j], inner[j]).astype(F32)
    for j in range(spread):
        z1 = z1 + swap(far[j], across[j]).astype(F32)
    x = tokens.astype(F32)
    inv1 = lax.rsqrt(jnp.mean(x * x, -1, keepdims=True) + EPSILON)
    d_tokens = (
        dy.reshape(tokens.shape)
        + z1
        - x * (inv1 * inv1) * jnp.mean(z1 * x, -1, keepdims=True)
    )
    return (
        output, d_tokens, d_first, gain1_grad, qkv_grad, out_grad_w, gain2_grad, gate_grad, up_grad,
        down_grad,
    )


def solution(mesh):
    rows = P(("seq", "dp"), None)
    acts = P("dp", "seq", None)
    gains = P(("seq", "dp"))
    return jax.shard_map(
        local,
        mesh=mesh,
        in_specs=(acts, acts, acts, P("dp"), gains, rows, rows, gains, rows, rows, rows),
        out_specs=(acts, acts, acts, gains, rows, rows, gains, rows, rows, rows),
        check_vma=False,
    )
```

```python
import functools

import jax
import jax.numpy as jnp
import numpy as np
from jax import lax
from jax.experimental import pallas as pl
from jax.experimental.pallas import tpu as pltpu
from jax.sharding import PartitionSpec as P

HEADS = 16
HEAD_DIM = 64
EPSILON = 1e-06
CORES = 2
OUTER = 2
BLOCK = 256
NEG = -1e30
F32 = jnp.float32
BF16 = jnp.bfloat16
MIB = 1024 * 1024
FREE = pl.CostEstimate(flops=0, bytes_accessed=0, transcendentals=0)


def lasting(us):
    return pl.CostEstimate(flops=0, bytes_accessed=int(us * 3.69e6), transcendentals=0)


def vmem(mib, scale=1):
    return pltpu.CompilerParams(vmem_limit_bytes=int(min(60, mib * max(scale, 1))) * MIB)


def held_in_hbm(*arrays):
    return [pltpu.with_memory_space_constraint(a, pltpu.HBM) for a in arrays]


class Copies:
    def __init__(self, sems):
        self.sems, self.used, self.waiting = sems, 0, {}

    def start(self, name, src, dst):
        copy = pltpu.make_async_copy(src, dst, self.sems.at[self.used])
        self.used += 1
        copy.start()
        self.waiting.setdefault(name, []).append(copy)

    def wait(self, *names):
        for name in names or list(self.waiting):
            for copy in self.waiting.pop(name, []):
                copy.wait()


def corner(a):
    block = (1,) * (a.ndim - 2) + (min(16, a.shape[-2]), min(128, a.shape[-1]))
    return pl.BlockSpec(block, lambda *_: (0,) * a.ndim)


def dot_nn(a, b):
    return lax.dot_general(a, b, (((1,), (0,)), ((), ())), preferred_element_type=F32)


def dot_nt(a, b):
    return lax.dot_general(a, b, (((1,), (1,)), ((), ())), preferred_element_type=F32)


def dot_tn(a, b):
    return lax.dot_general(a, b, (((0,), (0,)), ((), ())), preferred_element_type=F32)


def turned(u):
    half = HEAD_DIM // 2
    width = u.shape[1]
    if width % 128:
        parts = []
        for h in range(width // HEAD_DIM):
            lo = h * HEAD_DIM
            parts += [u[:, lo + half : lo + HEAD_DIM], u[:, lo : lo + half]]
        return jnp.concatenate(parts, axis=1)
    lane = lax.broadcasted_iota(jnp.int32, u.shape, 1) % HEAD_DIM
    return jnp.where(lane < half, pltpu.roll(u, width - half, 1), pltpu.roll(u, half, 1))


def head_mask(shape, h):
    lane = lax.broadcasted_iota(jnp.int32, shape, 1)
    return (lane >= h * HEAD_DIM) & (lane < (h + 1) * HEAD_DIM)


def own_head(u, h):
    if u.shape[1] == HEAD_DIM:
        return u
    return jnp.where(head_mask(u.shape, h), u, jnp.zeros_like(u))


def join_heads(parts):
    out = parts[0]
    for h in range(1, len(parts)):
        out = jnp.where(head_mask(out.shape, h), parts[h], out)
    return out


def fill_rows(seat, refs, order, dest):
    rows = refs[0].shape[2]
    for ref, ms in zip(refs, order):
        for j, m in enumerate(ms):
            at = pl.multiple_of((seat ^ m) * rows, rows)
            dest[pl.ds(at, rows), :] = ref[j, 0]


def attn_fwd_kernel(
    order, seat_ref, len_ref, w_ref, cos_ref, sin_ref, *refs,
):
    xs = refs[: len(order)]
    qkv_out, ot_out, send_out, lse_out, r1_out, xbuf, vt = refs[-7:]
    slot = pl.program_id(0)
    seat = seat_ref[0]
    length = len_ref[slot]
    total = xbuf.shape[0]
    width = w_ref.shape[0]
    wide = w_ref.shape[1] // 3
    heads = wide // HEAD_DIM
    blocks = total // BLOCK
    fill_rows(seat, xs, order, xbuf)
    for b in range(blocks):
        at = slice(b * BLOCK, (b + 1) * BLOCK)
        x = xbuf[at, :width]
        xf = x.astype(F32)
        r1 = lax.rsqrt(jnp.mean(xf * xf, axis=1, keepdims=True) + EPSILON)
        qkv = dot_nn(x, w_ref[...]) * r1
        cosine = cos_ref[at, :]
        sine = sin_ref[at, :]
        q = qkv[:, :wide]
        k = qkv[:, wide : 2 * wide]
        v = qkv[:, 2 * wide :]
        q = (q * cosine + turned(q) * sine) * (HEAD_DIM**-0.5)
        k = k * cosine + turned(k) * sine
        first = xbuf[at, width : width + wide]
        second = xbuf[at, width + wide :]
        v1 = jnp.where(seat % CORES == 0, first, second).astype(F32)
        vm = 0.5 * v + 0.5 * v1
        qkv_out[0, at, :wide] = q.astype(BF16)
        qkv_out[0, at, wide : 2 * wide] = k.astype(BF16)
        qkv_out[0, at, 2 * wide :] = vm.astype(BF16)
        vt[:, at] = vm.T.astype(BF16)
        r1_out[0, at, :] = jnp.broadcast_to(r1, (BLOCK, r1_out.shape[2]))
    for b in range(blocks):
        at = slice(b * BLOCK, (b + 1) * BLOCK)
        count = (b + 1) * BLOCK
        q = qkv_out[0, at, :wide]
        query = b * BLOCK + lax.broadcasted_iota(jnp.int32, (1, BLOCK), 1)
        last = jnp.minimum(query, length - 1)
        key = lax.broadcasted_iota(jnp.int32, (count, BLOCK), 0)
        allowed = key <= last
        ots = []
        for h in range(heads):
            k = own_head(qkv_out[0, :count, wide : 2 * wide], h)
            scores = jnp.where(allowed, dot_nt(k, q), NEG)
            top = jnp.max(scores, axis=0, keepdims=True)
            weights = jnp.exp(scores - top)
            total_w = jnp.sum(weights, axis=0, keepdims=True)
            ot = dot_nn(vt[h * HEAD_DIM : (h + 1) * HEAD_DIM, :count], weights.astype(BF16))
            ots.append(ot / total_w)
            lse_out[0, h : h + 1, at] = top + jnp.log(total_w)
        ot = jnp.concatenate(ots, axis=0)
        ot_out[0, :, at] = ot
        o = ot.T.astype(BF16)
        half = total // OUTER
        spread = send_out.shape[0] // OUTER
        group = (b * BLOCK) // half
        start = b * BLOCK - group * half
        for j in range(spread):
            send_out[group * spread + j, 0, start : start + BLOCK, :] = o


def chunk_specs(xs, lanes=None):
    return [
        pl.BlockSpec((x.shape[0], 1, x.shape[2], lanes or x.shape[3]), lambda i: (0, i, 0, 0))
        for x in xs
    ]


def attn_fwd(seat, lengths, xs, w, cosine, sine, order, ready):
    micro, rows, lanes = xs[0].shape[1:]
    width = w.shape[0]
    total = cosine.shape[0]
    spread = total // rows // (OUTER * CORES)
    wide = w.shape[1] // 3
    heads = wide // HEAD_DIM
    smem = pl.BlockSpec(memory_space=pltpu.SMEM)
    whole = lambda a: pl.BlockSpec(a.shape, lambda i: (0,) * a.ndim)
    pairs = total * total // 2 * micro * wide
    return pl.pallas_call(
        functools.partial(attn_fwd_kernel, order),
        grid=(micro,),
        in_specs=[smem, smem, whole(w), whole(cosine), whole(sine)]
        + chunk_specs(xs)
        + [corner(a) for a in ready],
        out_specs=[
            pl.BlockSpec((1, total, 3 * wide), lambda i: (i, 0, 0)),
            pl.BlockSpec((1, wide, total), lambda i: (i, 0, 0)),
            pl.BlockSpec((OUTER * spread, 1, total // OUTER, wide), lambda i: (0, i, 0, 0)),
            pl.BlockSpec((1, heads, total), lambda i: (i, 0, 0)),
            pl.BlockSpec((1, total, 128), lambda i: (i, 0, 0)),
        ],
        out_shape=[
            pltpu.HBM((micro, total, 3 * wide), BF16),
            pltpu.HBM((micro, wide, total), F32),
            pltpu.HBM((OUTER * spread, micro, total // OUTER, wide), BF16),
            pltpu.HBM((micro, heads, total), F32),
            pltpu.HBM((micro, total, 128), F32),
        ],
        scratch_shapes=[pltpu.VMEM((total, lanes), BF16), pltpu.VMEM((wide, total), BF16)],
        compiler_params=vmem(30, total / 1024),
        cost_estimate=lasting(20),
        name="attn_fwd",
    )(seat, lengths, *held_in_hbm(w, cosine, sine, *xs), *ready)


def attn_bwd_kernel(
    order, sent, seat_ref, len_ref, do_ref, cos_ref, sin_ref, qkv_ref, ot_ref, lse_ref, r1_ref,
    *refs,
):
    xs = refs[: len(order)]
    outs = refs[-6 - len(sent) : -6]
    dw_out, xbuf, dobuf, dqt, ebuf, dw = refs[-6:]
    slot = pl.program_id(0)
    seat = seat_ref[0]
    rows = do_ref.shape[2]
    length = len_ref[slot]
    total = xbuf.shape[0]
    wide = do_ref.shape[3]
    heads = wide // HEAD_DIM
    blocks = total // BLOCK
    fill_rows(seat, xs, order, xbuf)
    for j in range(do_ref.shape[0]):
        dobuf[j * rows : (j + 1) * rows, :] = do_ref[j, 0]
    dot_t = dobuf[...].astype(F32).T
    deltas = []
    for h in range(heads):
        part = slice(h * HEAD_DIM, (h + 1) * HEAD_DIM)
        deltas.append(jnp.sum(dot_t[part, :] * ot_ref[0, part, :], axis=0, keepdims=True))
    dqt[...] = jnp.zeros_like(dqt)
    for b in range(blocks):
        at = slice(b * BLOCK, (b + 1) * BLOCK)
        later = slice(b * BLOCK, total)
        count = total - b * BLOCK
        k = qkv_ref[0, at, wide : 2 * wide]
        v = qkv_ref[0, at, 2 * wide :]
        kt = k.astype(F32).T.astype(BF16)
        q = qkv_ref[0, later, :wide]
        d_o = dobuf[later, :]
        query = b * BLOCK + lax.broadcasted_iota(jnp.int32, (1, count), 1)
        last = jnp.minimum(query, length - 1)
        key = b * BLOCK + lax.broadcasted_iota(jnp.int32, (BLOCK, count), 0)
        allowed = key <= last
        dks, dvs = [], []
        for h in range(heads):
            part = slice(h * HEAD_DIM, (h + 1) * HEAD_DIM)
            scores = jnp.where(allowed, dot_nt(own_head(k, h), q), NEG)
            weights = jnp.exp(scores - lse_ref[0, h : h + 1, later])
            d_weights = dot_nt(own_head(v, h), d_o)
            ds = (weights * (d_weights - deltas[h][:, later])).astype(BF16)
            dvs.append(dot_nn(weights.astype(BF16), d_o))
            dks.append(dot_nn(ds, q))
            dqt[part, later] += dot_nn(kt[part, :], ds)
        cosine = cos_ref[at, :]
        sine = sin_ref[at, :]
        r1 = r1_ref[0, at, 0:1]
        dk = join_heads(dks)
        dk = dk * cosine - turned(dk) * sine
        dv = 0.5 * join_heads(dvs)
        ebuf[at, 3 * wide :] = dv.astype(BF16)
        ebuf[at, wide : 2 * wide] = (dk * r1).astype(BF16)
        ebuf[at, 2 * wide : 3 * wide] = (dv * r1).astype(BF16)
    for b in range(blocks):
        at = slice(b * BLOCK, (b + 1) * BLOCK)
        dq = dqt[:, at].T * (HEAD_DIM**-0.5)
        dq = dq * cos_ref[at, :] - turned(dq) * sin_ref[at, :]
        ebuf[at, :wide] = (dq * r1_ref[0, at, 0:1]).astype(BF16)
    for ref, ms in zip(outs, sent):
        for j, m in enumerate(ms):
            ref[j, 0] = ebuf[pl.ds(pl.multiple_of((seat ^ m) * rows, rows), rows), :]
    grown = dot_tn(xbuf[...], ebuf[:, : 3 * wide])

    @pl.when(slot == 0)
    def _():
        dw[...] = grown

    @pl.when(slot > 0)
    def _():
        dw[...] += grown

    @pl.when(slot == pl.num_programs(0) - 1)
    def _():
        dw_out[...] = dw[...].astype(BF16)


def attn_bwd(seat, lengths, xs, wshape, d_o, cosine, sine, qkv, ot, lse, r1, order, sent, ready):
    micro, rows = xs[0].shape[1:3]
    width = wshape[0]
    total = cosine.shape[0]
    wide = wshape[1] // 3
    heads = wide // HEAD_DIM
    smem = pl.BlockSpec(memory_space=pltpu.SMEM)
    whole = lambda a: pl.BlockSpec(a.shape, lambda i: (0,) * a.ndim)
    vspec = pl.BlockSpec((d_o.shape[0], 1, rows, wide), lambda i: (0, i, 0, 0))
    zshapes = [pltpu.HBM((len(ms), micro, rows, 4 * wide), BF16) for ms in sent]
    pairs = total * total // 2 * micro * wide
    return pl.pallas_call(
        functools.partial(attn_bwd_kernel, order, sent),
        grid=(micro,),
        in_specs=[
            smem, smem, vspec, whole(cosine), whole(sine),
            pl.BlockSpec((1, total, 3 * wide), lambda i: (i, 0, 0)),
            pl.BlockSpec((1, wide, total), lambda i: (i, 0, 0)),
            pl.BlockSpec((1, heads, total), lambda i: (i, 0, 0)),
            pl.BlockSpec((1, total, 128), lambda i: (i, 0, 0)),
        ]
        + chunk_specs(xs, width)
        + [corner(a) for a in ready],
        out_specs=chunk_specs(zshapes) + [pl.BlockSpec(wshape, lambda i: (0, 0))],
        out_shape=zshapes + [pltpu.HBM(wshape, BF16)],
        scratch_shapes=[
            pltpu.VMEM((total, width), BF16),
            pltpu.VMEM((total, wide), BF16),
            pltpu.VMEM((wide, total), F32),
            pltpu.VMEM((total, 4 * wide), BF16),
            pltpu.VMEM(wshape, F32),
        ],
        compiler_params=vmem(40, total / 1024),
        cost_estimate=lasting(20),
        name="attn_bwd",
    )(seat, lengths, *held_in_hbm(d_o, cosine, sine, qkv, ot, lse, r1, *xs), *ready)


def ff_kernel(
    own, skip, at, seat_ref, xa, xb, ga, gb, oa, ob, pair, down_mine, down_far, wout_mine, wout_theirs, *refs,
):
    refs = refs[skip:]
    za, zb_lo, zb_hi, fa, fb, hn_out, hid_out, dgate_out, dup_out = refs[:9]
    refs = refs[9:]
    if own:
        y_out, o_out, wout_out = refs[:3]
        refs = refs[3:]
    x_buf, g_buf, oa_buf, ob_buf, wout, wg, wu, wd, z_buf, f_buf, hn, hid, dgate, dup, y_buf, o_buf, sems = refs
    seat = seat_ref[0]
    core = seat % CORES
    micro, rows, width = xa.shape[1:]
    width = wout.shape[0]
    many = micro * rows
    depth, outer, group, held, slab2 = pair.shape
    slab = slab2 // 2
    spread = group // CORES
    tall = down_mine.shape[1]
    half = seat // group
    copies = Copies(sems)

    for low in range(CORES):
        there = pl.ds(pl.multiple_of(((seat % group) ^ (2 * at + low)) * rows, rows), rows)
        copies.start("o", oa.at[:, :, there, :], oa_buf.at[low])
        copies.start("o", ob.at[:, :, there, :], ob_buf.at[low])
    for rc, ref in enumerate((wout_mine, wout_theirs)):
        for rx in range(spread):
            for ry in range(outer):
                other = seat ^ (ry * group + rx * CORES + rc)
                for d in range(depth):
                    to = pl.ds(pl.multiple_of((other * depth + d) * held, held), held)
                    copies.start("wout", ref.at[rx, ry, d], wout.at[to, :])
    copies.start("x", xa.at[at, :, :, :width], x_buf.at[0])
    copies.start("x", xb.at[at, :, :, :width], x_buf.at[1])
    for part, dest in ((0, wg), (1, wu)):
        for y in range(outer):
            for q in range(group):
                for d in range(depth):
                    to = ((y * group + q) * depth + d) * held
                    copies.start(
                        "wg" if part == 0 else "wu",
                        pair.at[d, y, q, :, pl.ds(part * slab, slab)],
                        dest.at[pl.ds(to, held), :],
                    )
    copies.start("g", ga.at[at], g_buf.at[0])
    copies.start("g", gb.at[at], g_buf.at[1])
    for ry, ref in enumerate((down_mine, down_far)):
        for d in range(depth):
            to = pl.ds(pl.multiple_of(((half ^ ry) * depth + d) * tall, tall), tall)
            copies.start("wd", ref.at[d], wd.at[to, :])

    copies.wait("o")
    for low in range(CORES):
        for j in range(oa_buf.shape[1]):
            a = oa_buf[low, j].reshape(many, oa_buf.shape[4])
            b = ob_buf[low, j].reshape(many, oa_buf.shape[4])
            wide = a.shape[1]
            here = slice(low * many, (low + 1) * many)
            o_buf[here, (2 * j) * wide : (2 * j + 1) * wide] = jnp.where(core == 0, a, b)
            o_buf[here, (2 * j + 1) * wide : (2 * j + 2) * wide] = jnp.where(core == 0, b, a)
    copies.wait("wout", "x")
    if own:
        copies.start("out", wout, wout_out)
        copies.start("out", o_buf, o_out)
    y = x_buf[...].reshape(2 * many, width).astype(F32) + dot_nn(o_buf[...], wout[...])
    r2 = lax.rsqrt(jnp.mean(y * y, axis=1, keepdims=True) + EPSILON)
    hn[...] = (y * r2).astype(BF16)
    if own:
        y_buf[...] = y[:many]
        copies.start("out", y_buf, y_out)
    copies.start("out", hn, hn_out)
    copies.wait("wg")
    gate = dot_nn(hn[...], wg[...])
    copies.wait("wu")
    up = dot_nn(hn[...], wu[...])
    sigma = jax.nn.sigmoid(gate)
    act = gate * sigma
    hid[...] = (act * up).astype(BF16)
    copies.start("out", hid, hid_out)
    copies.wait("g", "wd")
    dhid = dot_nt(g_buf[...].reshape(2 * many, width), wd[...])
    dgate[...] = (dhid * up * (sigma + act * (1.0 - sigma))).astype(BF16)
    dup[...] = (dhid * act).astype(BF16)
    copies.start("out", dgate, dgate_out)
    copies.start("out", dup, dup_out)
    z_buf[...] = (dot_nt(dgate[...], wg[...]) + dot_nt(dup[...], wu[...])).astype(BF16)
    copies.start("out", z_buf.at[pl.ds(0, many)], za)
    copies.start("out", z_buf.at[pl.ds(many, many // 2)], zb_lo)
    copies.start("out", z_buf.at[pl.ds(many + many // 2, many // 2)], zb_hi)
    f_buf[...] = dot_nn(hid[...], wd[...]).astype(BF16)
    copies.start("out", f_buf.at[pl.ds(0, many)], fa)
    copies.start("out", f_buf.at[pl.ds(many, many)], fb)
    copies.wait()


def feed_forward(seat, xa, xb, ga, gb, oa, ob, weights, at, own, ready=()):
    pair, down_mine, down_far, wout_mine, wout_theirs = weights
    spread, micro, rows, width = ga.shape
    many = micro * rows
    depth, outer, group, held, slab2 = pair.shape
    fan = slab2 // 2
    wide = oa.shape[3]
    outs = [(many, width), (many // 2, width), (many // 2, width), (many, width), (many, width)]
    outs = [pltpu.HBM(s, BF16) for s in outs + [(2 * many, width)] + [(2 * many, fan)] * 3]
    if own:
        outs += [
            pltpu.HBM((many, width), F32), pltpu.HBM((2 * many, width), BF16),
            pltpu.HBM((width, width), BF16),
        ]
    o_shape = (CORES, oa.shape[0], micro, rows, wide)
    scratch = [
        ((2, micro, rows, width), BF16), ((2, micro, rows, width), BF16), (o_shape, BF16),
        (o_shape, BF16), ((width, width), BF16), ((width, fan), BF16), ((width, fan), BF16),
        ((fan, width), BF16), ((2 * many, width), BF16), ((2 * many, width), BF16),
        ((2 * many, width), BF16), ((2 * many, fan), BF16), ((2 * many, fan), BF16),
        ((2 * many, fan), BF16), ((many, width), F32), ((2 * many, width), BF16),
    ]
    many_copies = 32 + 4 * outer * group * depth
    anywhere = pl.BlockSpec(memory_space=pl.ANY)
    return pl.pallas_call(
        functools.partial(ff_kernel, own, len(ready), at),
        grid=(1,),
        in_specs=[pl.BlockSpec(memory_space=pltpu.SMEM)]
        + [anywhere] * 11
        + [corner(a) for a in ready],
        out_specs=[anywhere] * len(outs),
        out_shape=outs,
        scratch_shapes=[pltpu.VMEM(s, t) for s, t in scratch]
        + [pltpu.SemaphoreType.DMA((many_copies,))],
        compiler_params=vmem(56),
        cost_estimate=lasting(16),
        name="ff_own" if own else "ff_near",
    )(seat, *held_in_hbm(xa, xb, ga, gb, oa, ob, *weights), *ready)


def ff_grads_kernel(sets, skip, group, spread, seat_ref, *refs):
    refs = refs[skip:]
    ins = refs[: 6 * sets]
    o_ref, dyb_ref, dyb_theirs = refs[6 * sets : 6 * sets + 3]
    fa, fb = refs[6 * sets + 3 : 6 * sets + 5]
    refs = refs[6 * sets + 5 :]
    pair_out, down_mine, wout_own = refs[:3]
    parcels = refs[3 : 2 + 2 * spread]
    dwg, dwu, dwd, dwo = refs[2 + 2 * spread :]
    seat = seat_ref[0]
    outer = seat // group
    core = seat % CORES
    chip = seat // CORES
    depth, blocks, held, slab2 = pair_out.shape
    slab = slab2 // 2
    tall = down_mine.shape[1]
    many, width = dyb_ref.shape
    for n in range(sets):
        hn, hid, dgate, dup, ga, gb = ins[6 * n : 6 * n + 6]
        g = jnp.concatenate([ga[0].reshape(many, width), gb[0].reshape(many, width)], axis=0)
        new = dot_tn(hn[...], dgate[...]), dot_tn(hn[...], dup[...]), dot_tn(hid[...], g)
        for scratch, value in zip((dwg, dwu, dwd), new):
            if n == 0:
                scratch[...] = value
            else:
                scratch[...] += value
    for k in range(blocks):
        for d in range(depth):
            at = slice((k * depth + d) * held, (k * depth + d + 1) * held)
            pair_out[d, k, :, :slab] = dwg[at, :].astype(BF16)
            pair_out[d, k, :, slab:] = dwu[at, :].astype(BF16)
    far = parcels[spread - 1]
    for d in range(depth):
        pieces = []
        for k in range(OUTER):
            at = slice((k * depth + d) * tall, (k * depth + d + 1) * tall)
            pieces.append(dwd[at, :].astype(BF16))
        down_mine[d] = jnp.where(outer == 0, pieces[0], pieces[1])
        far[d * tall : (d + 1) * tall, :] = jnp.where(outer == 0, pieces[1], pieces[0])
    dyb = jnp.concatenate([dyb_ref[...], dyb_theirs[...]], axis=0)
    rows = depth * held
    for c in range(2 * spread):
        a = o_ref[:, (2 * c) * rows : (2 * c + 1) * rows]
        b = o_ref[:, (2 * c + 1) * rows : (2 * c + 2) * rows]
        dwo[c * rows : (c + 1) * rows, :] = dot_tn(jnp.where(core == 0, a, b), dyb)
    for j in range(2 * spread):
        at = pl.ds(pl.multiple_of((chip ^ j) * rows, rows), rows)
        value = dwo[at, :].astype(BF16)
        if j == 0:
            wout_own[...] = value
        else:
            out = parcels[j - 1]
            out[out.shape[0] - rows :, :] = value
    for j in range(spread - 1):
        parcels[j][:many, :] = (fa[j].astype(F32) + fb[j].astype(F32)).astype(BF16)


def ff_grads(seat, ready, sets, ga, gb, o_both, dyb, dyb_theirs, fa, fb, pair_shape, tall, spread):
    once = pl.Buffered(1)

    def fixed(shape):
        return pl.BlockSpec(shape, lambda i: (0,) * len(shape), pipeline_mode=once)

    args, specs = [], []
    for chip, *arrays in sets:
        args += arrays
        specs += [fixed(a.shape) for a in arrays]
        for g in (ga, gb):
            args.append(g)
            specs.append(
                pl.BlockSpec((1,) + g.shape[1:], lambda i, c=chip: (c, 0, 0, 0), pipeline_mode=once)
            )
    last = [o_both, dyb, dyb_theirs, fa, fb]
    args += last
    specs += [fixed(a.shape) for a in last]
    depth, _, held, slab2 = pair_shape
    many, width = dyb.shape
    fan = slab2 // 2
    rows = depth * held
    parcels = [(many + rows, width)] * (spread - 1) + [(depth * tall + rows, width)]
    parcels += [(rows, width)] * (spread - 1)
    outs = [pair_shape, (depth, tall, width), (rows, width)] + parcels
    return pl.pallas_call(
        functools.partial(ff_grads_kernel, len(sets), len(ready), spread * CORES, spread),
        grid=(1,),
        in_specs=[pl.BlockSpec(memory_space=pltpu.SMEM)] + [corner(a) for a in ready] + specs,
        out_specs=[fixed(s) for s in outs],
        out_shape=[pltpu.HBM(s, BF16) for s in outs],
        scratch_shapes=[
            pltpu.VMEM((width, fan), F32), pltpu.VMEM((width, fan), F32),
            pltpu.VMEM((fan, width), F32), pltpu.VMEM((2 * spread * rows, width), F32),
        ],
        compiler_params=vmem(56),
        cost_estimate=lasting(14),
        name="ff_grads",
    )(seat, *ready, *args)


def pieces_at(values, index):
    step = 1
    while step < len(values):
        flip = (index // step) % 2 == 1
        values = [jnp.where(flip, values[k ^ step], values[k]) for k in range(len(values))]
        step *= 2
    return values


def payloads(seat, tokens, first_values, down_weight, out_weight, spread, wide, tall):
    micro, rows, width = tokens.shape
    lanes = CORES * wide
    short = down_weight.shape[0]
    held = out_weight.shape[0]

    def kernel(seat_ref, x_ref, d_ref, w_ref, *refs):
        firsts, outs = refs[: 2 * spread], refs[2 * spread : 3 * spread + 1]
        tail_out, zero_out = refs[3 * spread + 1 :]
        for out in outs:
            out[0, :, :width] = x_ref[0]
        outs[0][0, :, width:] = firsts[0][0]
        outs[1][0, :, width:] = firsts[spread][0]
        for j in range(1, spread):
            outs[1 + j][0, :, width : width + lanes] = firsts[j][0]
            outs[1 + j][0, :, width + lanes :] = firsts[spread + j][0]

        @pl.when(pl.program_id(0) == 0)
        def _():
            tail_out[...] = jnp.zeros_like(tail_out)
            tail_out[:short, :] = d_ref[...]
            tail_out[tall:, :] = w_ref[...]
            zero_out[...] = jnp.zeros_like(zero_out)

    def part(j):
        return pl.BlockSpec((1, rows, lanes), lambda i, s: (i, 0, (s[0] // CORES) ^ j))

    fixed = lambda *shape: pl.BlockSpec(shape, lambda i, s: (0,) * len(shape))
    sizes = [width + lanes, width + lanes] + [width + 2 * lanes] * (spread - 1)
    return pl.pallas_call(
        kernel,
        grid_spec=pltpu.PrefetchScalarGridSpec(
            num_scalar_prefetch=1,
            grid=(micro,),
            in_specs=[
                pl.BlockSpec((1, rows, width), lambda i, s: (i, 0, 0)),
                fixed(*down_weight.shape), fixed(*out_weight.shape),
            ]
            + [part(j) for j in range(2 * spread)],
            out_specs=[pl.BlockSpec((1, rows, n), lambda i, s: (i, 0, 0)) for n in sizes]
            + [fixed(tall + held, width), fixed(8, 128)],
        ),
        out_shape=[pltpu.HBM((micro, rows, n), BF16) for n in sizes]
        + [
            pltpu.HBM((tall + held, width), BF16),
            pltpu.HBM((8, 128), F32),
        ],
        cost_estimate=FREE,
        name="payloads",
    )(seat, *held_in_hbm(tokens, down_weight, out_weight, *([first_values] * (2 * spread))))


def middle_back(y, parts, pieces, grad, wout, wide):
    micro, rows, width = grad.shape
    seats = width // wide
    many = micro * rows

    def kernel(y_ref, g_ref, w_ref, *refs):
        zs = refs[: len(parts)]
        z = jnp.concatenate([r[...] for r in refs[len(parts) : len(parts) + len(pieces)]], axis=0)
        dy_out, dyb_out, do_out = refs[len(parts) + len(pieces) :]
        z = z.astype(F32)
        for ref in zs:
            z = z + ref[...].astype(F32)
        y = y_ref[...]
        r2 = lax.rsqrt(jnp.mean(y * y, axis=1, keepdims=True) + EPSILON)
        inner = jnp.mean(z * y, axis=1, keepdims=True)
        g = g_ref[...].reshape(many, width).astype(F32)
        dy = g + r2 * z - y * (r2 * r2 * r2 * inner)
        dy_out[...] = dy
        dyb = dy.astype(BF16)
        dyb_out[...] = dyb
        d_o = dot_nt(dyb, w_ref[...]).astype(BF16)
        for s in range(seats):
            do_out[s] = d_o[:, s * wide : (s + 1) * wide].reshape(micro, rows, wide)

    def fixed(shape):
        return pl.BlockSpec(shape, lambda i: (0,) * len(shape), pipeline_mode=pl.Buffered(1))

    given = [y, grad, wout, *parts, *pieces]
    return pl.pallas_call(
        kernel,
        grid=(1,),
        in_specs=[fixed(a.shape) for a in given],
        out_specs=[
            fixed((many, width)), fixed((many, width)), fixed((seats, micro, rows, wide)),
        ],
        out_shape=[
            pltpu.HBM((many, width), F32),
            pltpu.HBM((many, width), BF16),
            pltpu.HBM((seats, micro, rows, wide), BF16),
        ],
        compiler_params=vmem(24),
        cost_estimate=FREE,
        name="middle_back",
    )(*given)


def back_to_x(seat, mine, theirs, w_mine, w_theirs, along, sums):
    count, micro, rows, lanes = mine.shape
    width = w_mine.shape[0]
    wide = lanes // 4
    many = micro * rows
    down, wout, parcels = sums
    depth, tall = down.shape[:2]
    spread = (len(parcels) + 1) // 2
    held = wout.shape[0] // depth

    def kernel(seat_ref, a_ref, b_ref, wa, wb, _, down_ref, wout_ref, *refs):
        parts = refs[: len(parcels)]
        outs = refs[len(parcels) : len(parcels) + count]
        tail_out = refs[len(parcels) + count]
        buf, sems = refs[-2:]
        core = seat_ref[0] % CORES
        copies = Copies(sems)
        for j in range(count):
            a = a_ref[j].reshape(many, lanes)
            b = b_ref[j].reshape(many, lanes)
            z = dot_nt(a[:, : 3 * wide], wa[...]) + dot_nt(b[:, : 3 * wide], wb[...])
            buf[j, :, :, :width] = z.astype(BF16).reshape(micro, rows, width)
            first = jnp.where(core == 0, a[:, 3 * wide :], b[:, 3 * wide :])
            second = jnp.where(core == 0, b[:, 3 * wide :], a[:, 3 * wide :])
            buf[j, :, :, width : width + wide] = first.reshape(micro, rows, wide)
            buf[j, :, :, width + wide :] = second.reshape(micro, rows, wide)
            copies.start("out", buf.at[j], outs[j])
        total = wout_ref[...].astype(F32)
        for part in parts:
            total = total + part[part.shape[0] - depth * held :, :].astype(F32)
        far = parts[spread - 1]
        for d in range(depth):
            value = down_ref[d].astype(F32) + far[d * tall : (d + 1) * tall, :].astype(F32)
            tail_out[d, :tall, :] = value.astype(BF16)
            tail_out[d, tall:, :] = total[d * held : (d + 1) * held, :].astype(BF16)
        copies.wait()

    anywhere = pl.BlockSpec(memory_space=pl.ANY)
    out = pltpu.HBM((micro, rows, width + CORES * wide), BF16)
    fixed = lambda shape: pl.BlockSpec(
        shape, lambda i: (0,) * len(shape), pipeline_mode=pl.Buffered(1)
    )
    tail = (depth, tall + held, width)
    given = [mine, theirs, w_mine, w_theirs]
    sums = [down, wout, *parcels]
    return pl.pallas_call(
        kernel,
        grid=(1,),
        in_specs=[pl.BlockSpec(memory_space=pltpu.SMEM)]
        + [fixed(a.shape) for a in given]
        + [anywhere]
        + [fixed(a.shape) for a in sums],
        out_specs=[anywhere] * count + [fixed(tail), anywhere],
        out_shape=[out] * count
        + [pltpu.HBM(tail, BF16), pltpu.HBM(along.shape, along.dtype)],
        scratch_shapes=[
            pltpu.VMEM((count, micro, rows, width + CORES * wide), BF16),
            pltpu.SemaphoreType.DMA((count,)),
        ],
        input_output_aliases={5: count + 1},
        compiler_params=vmem(32),
        cost_estimate=FREE,
        name="back_to_x",
    )(seat, *given, along, *sums)


def add_parts(mine, theirs):
    def kernel(a_ref, *refs):
        b = jnp.concatenate([r[...] for r in refs[:-1]], axis=0)
        refs[-1][...] = (a_ref[...].astype(F32) + b.astype(F32)).astype(BF16)

    fixed = lambda shape: pl.BlockSpec(
        shape, lambda i: (0,) * len(shape), pipeline_mode=pl.Buffered(1)
    )
    return pl.pallas_call(
        kernel,
        grid=(1,),
        in_specs=[fixed(a.shape) for a in (mine, *theirs)],
        out_specs=fixed(mine.shape),
        out_shape=pltpu.HBM(mine.shape, BF16),
        compiler_params=vmem(16),
        cost_estimate=FREE,
        name="add_parts",
    )(mine, *theirs)


def tail_grads(tail, tall, short):
    rows, width = tail.shape

    def kernel(t_ref, down_out, wout_out):
        down_out[...] = t_ref[:short, :].astype(F32)
        wout_out[...] = t_ref[tall:, :].astype(F32)

    return pl.pallas_call(
        kernel,
        out_shape=[pltpu.HBM((short, width), F32), pltpu.HBM((rows - tall, width), F32)],
        cost_estimate=FREE,
        name="tail_grads",
    )(tail)


def onward(arrived, width, lanes, ready):
    count = len(arrived)
    micro, rows, held = arrived[0].shape

    def kernel(*refs):
        out = refs[-1]
        for j in range(count):
            out[j, 0, :, :width] = refs[j][0, :, :width]
            out[j, 0, :, width:] = refs[j][0, :, lanes:]

    return pl.pallas_call(
        kernel,
        grid=(micro,),
        in_specs=[pl.BlockSpec((1, rows, held), lambda i: (i, 0, 0))] * count
        + [corner(a) for a in ready],
        out_specs=pl.BlockSpec((count, 1, rows, lanes), lambda i: (0, i, 0, 0)),
        out_shape=pltpu.HBM((count, micro, rows, lanes), BF16),
        cost_estimate=lasting(40),
        name="onward",
    )(*arrived, *ready)


def fence(value, ready):
    def kernel(*_):
        pass

    return pl.pallas_call(
        kernel,
        grid=(1,),
        in_specs=[pl.BlockSpec(memory_space=pl.ANY)] + [corner(a) for a in ready],
        out_specs=pl.BlockSpec(memory_space=pl.ANY),
        out_shape=pltpu.HBM(value.shape, value.dtype),
        input_output_aliases={0: 0},
        cost_estimate=FREE,
        name="fence",
    )(value, *ready)


def token_grads(seat, tokens, dy, got, wide, ready):
    micro, rows, width = tokens.shape
    lanes = CORES * wide

    def kernel(seat_ref, x_ref, dy_ref, *refs):
        parts = refs[: len(got)]
        dx_out, dv_out = refs[-2:]
        z = parts[0][0, :, :width].astype(F32)
        for ref in parts[1:]:
            z = z + ref[0, :, :width].astype(F32)
        x = x_ref[0].astype(F32)
        inv = lax.rsqrt(jnp.mean(x * x, axis=1, keepdims=True) + EPSILON)
        inner = jnp.mean(z * x, axis=1, keepdims=True)
        dx_out[0] = dy_ref[...] + z - x * (inv * inv * inner)
        firsts = pieces_at([ref[0, :, width:].astype(F32) for ref in parts], seat_ref[0] // CORES)
        for k, value in enumerate(firsts):
            dv_out[0, :, k * lanes : (k + 1) * lanes] = value

    spec = pl.BlockSpec((1, rows, width), lambda i: (i, 0, 0))
    return pl.pallas_call(
        kernel,
        grid=(micro,),
        in_specs=[
            pl.BlockSpec(memory_space=pltpu.SMEM), spec, pl.BlockSpec((rows, width), lambda i: (i, 0)),
        ]
        + [pl.BlockSpec((1, rows, width + lanes), lambda i: (i, 0, 0))] * len(got)
        + [corner(a) for a in ready],
        out_specs=[spec, spec],
        out_shape=[pltpu.HBM(tokens.shape, F32)] * 2,
        cost_estimate=FREE,
        name="token_grads",
    )(seat, tokens, dy, *got, *ready)


def projection_grads(parts, weight, gain, wide):
    seats, depth, held, _ = parts.shape
    width = seats * wide

    def kernel(p_ref, w_ref, gain_ref, dw_out, dg_out):
        gain = gain_ref[...]
        grown = jnp.zeros((held, 1), F32)
        for s in range(seats):
            total = p_ref[s, 0].astype(F32)
            for d in range(1, depth):
                total = total + p_ref[s, d].astype(F32)
            for t in range(3):
                at = slice(t * width + s * wide, t * width + (s + 1) * wide)
                piece = total[:, t * wide : (t + 1) * wide]
                dw_out[:, at] = piece * gain
                grown = grown + jnp.sum(piece * w_ref[:, at].astype(F32), axis=1, keepdims=True)
        dg_out[...] = grown

    return pl.pallas_call(
        kernel,
        out_shape=[
            pltpu.HBM(weight.shape, F32), pltpu.HBM((held, 1), F32),
        ],
        cost_estimate=FREE,
        name="projection_grads",
    )(parts, weight, gain)


def pair_grads(parts, gate, up, gain, depth, short):
    outer, group, held, slab2 = parts.shape
    slab = slab2 // 2
    tall = slab // (OUTER * depth)
    fan = gate.shape[1]

    def kernel(p_ref, gate_ref, up_ref, gain_ref, dgate_out, dup_out, dg_out):
        for q in range(group):
            total = p_ref[0, q].astype(F32)
            for y in range(1, outer):
                total = total + p_ref[y, q].astype(F32)
            for m, out in enumerate((dgate_out, dup_out)):
                for y in range(OUTER):
                    for d in range(depth):
                        at = m * slab + (y * depth + d) * tall
                        to = ((y * group + q) * depth + d) * short
                        out[:, to : to + short] = total[:, at : at + short]
        dgate = dgate_out[...]
        dup = dup_out[...]
        dg_out[...] = jnp.sum(
            dgate * gate_ref[...].astype(F32) + dup * up_ref[...].astype(F32),
            axis=1,
            keepdims=True,
        )
        dgate_out[...] = dgate * gain_ref[...]
        dup_out[...] = dup * gain_ref[...]

    return pl.pallas_call(
        kernel,
        out_shape=[
            pltpu.HBM((held, fan), F32), pltpu.HBM((held, fan), F32), pltpu.HBM((held, 1), F32),
        ],
        cost_estimate=FREE,
        name="pair_grads",
    )(parts, gate, up, gain)


def rope_tables(total, wide):
    positions = np.arange(total, dtype=np.float32)
    inverse = np.float32(10000.0) ** (-np.arange(0, HEAD_DIM, 2, dtype=np.float32) / HEAD_DIM)
    angles = (positions[:, None] * inverse[None, :].astype(np.float32)).astype(np.float64)
    cosine, sine = np.cos(angles), np.sin(angles)
    cosine = np.tile(cosine, (1, 2 * wide // HEAD_DIM))
    sine = np.tile(np.concatenate([-sine, sine], -1), (1, wide // HEAD_DIM))
    return jnp.asarray(cosine.astype(np.float32)), jnp.asarray(sine.astype(np.float32))


def local(
    tokens, first_values, out_grad, lengths, norm1_gain, qkv_weight, out_weight, norm2_gain,
    gate_weight, up_weight, down_weight,
):
    micro, rows, width = tokens.shape
    seats, depth = lax.axis_size("seq"), lax.axis_size("dp")
    devices = seats * depth
    seat = lax.axis_index("seq")
    group = seats // OUTER
    spread = group // CORES
    outer = seat // group
    total = seats * rows
    wide = width // seats
    held = qkv_weight.shape[0]
    fan_rows = down_weight.shape[0]
    fan = fan_rows * devices
    tall = -(-fan_rows // 16) * 16
    slab = OUTER * depth * tall
    many = micro * rows
    seat_arr = jnp.reshape(seat, (1,)).astype(jnp.int32)

    def swap(value, mask):
        return lax.ppermute(value, "seq", [(i, i ^ mask) for i in range(seats)])

    def token(value):
        return value[(0,) * value.ndim].astype(F32) * 0.0

    same_core = [[i for i in range(seats) if i % CORES == c] for c in range(CORES)]
    every = ("seq", "dp")
    core = seat % CORES
    chip = seat // CORES
    inner = [2 * j for j in range(spread)]
    across = [group + 2 * j for j in range(spread)]

    gain1 = norm1_gain.astype(F32)[:, None]
    gain2 = norm2_gain.astype(F32)[:, None]

    lanes = width + CORES * wide
    own, far_own, *arrived, tail, zero = payloads(
        seat_arr, tokens, first_values, down_weight, out_weight, spread, wide, tall
    )
    first = zero[:1, :1]
    arrived = [swap(arrived[j - 1], 2 * j) for j in range(1, spread)]
    far_own = swap(far_own, group)
    near = jnp.stack([own] + [a[..., :lanes] for a in arrived])

    def columns(weight):
        scaled = (weight.astype(F32) * gain2 + first).astype(BF16)
        scaled = scaled.reshape(held, OUTER, group, depth, fan_rows).transpose(2, 0, 1, 3, 4)
        scaled = jnp.pad(scaled, ((0, 0),) * 4 + ((0, tall - fan_rows),))
        return scaled.reshape(group, held, slab)

    pair = jnp.concatenate([columns(gate_weight), columns(up_weight)], -1)
    pair = jnp.concatenate([pair] * OUTER, 0)
    pair = lax.all_to_all(pair, "seq", split_axis=0, concat_axis=0, tiled=True)
    far_rest = swap(onward(arrived, width, lanes, []), group)
    pair = lax.all_gather(pair, "dp", axis=0).reshape(depth, OUTER, group, held, 2 * slab)

    near_b = swap(near, 1)
    far_own = far_own[None]
    far_own_b = swap(far_own, 1)
    far_rest_b = swap(far_rest, 1)
    xs = (near, far_own, far_rest, near_b, far_own_b, far_rest_b)
    masks = (tuple(inner), tuple(across[:1]), tuple(across[1:]))
    order = masks + tuple(tuple(m + 1 for m in ms) for ms in masks)

    wqkv = (qkv_weight.astype(F32) * gain1 + first).astype(BF16)
    wqkv = wqkv.reshape(held, 3, seats, wide).transpose(2, 0, 1, 3).reshape(seats, 1, held, 3 * wide)
    wqkv = jnp.broadcast_to(wqkv, (seats, depth, held, 3 * wide)).reshape(devices, held, 3 * wide)
    wqkv = lax.all_to_all(wqkv, every, split_axis=0, concat_axis=0, tiled=True)
    wqkv = wqkv.reshape(width, 3 * wide)

    tail = lax.all_gather(tail, "dp", axis=0)
    down_mine = tail[:, :tall]
    down_far = swap(down_mine, group)
    wout_mine = tail[:, tall:]
    wout_far = swap(wout_mine, group)
    wout = jnp.stack([wout_mine, wout_far])
    wout_inner = [swap(wout, m) for m in inner[1:]]
    wout = jnp.stack([wout] + wout_inner)
    wout_theirs = swap(wout, 1)
    wqkv_theirs = swap(wqkv, 1)

    late_grad = (out_grad.astype(F32) + token(wqkv)).astype(BF16)
    grads = [swap(late_grad, m) for m in inner[1:]]
    ga = jnp.stack([out_grad] + grads)
    gb = swap(ga, 1)

    cosine, sine = rope_tables(total, wide)
    qkv, ot, send, lse, r1 = attn_fwd(
        seat_arr, lengths, xs, wqkv, cosine, sine, order,
        [wqkv_theirs, wout_far, gb],
    )
    send = fence(send, [down_far, *wout_inner])
    oa = lax.all_to_all(
        send, "seq", split_axis=0, concat_axis=0, tiled=True, axis_index_groups=same_core
    )
    ob = swap(oa, 1)
    ff_args = (
        seat_arr, near, near_b, ga, gb, oa, ob, (pair, down_mine, down_far, wout, wout_theirs)
    )
    near_z, sets, near_f = [], [], []
    for j in range(1, spread):
        za, zb_lo, zb_hi, fa, fb, *kept = feed_forward(*ff_args, j, False, near_z)
        near_z.append(add_parts(za, [swap(zb_lo, 1), swap(zb_hi, 1)]))
        sets.append((j, *kept))
        near_f.append((fa, swap(fb, 1)))
    za, zb_lo, zb_hi, fa, fb, *kept = feed_forward(*ff_args, 0, True, near_z)
    y, o_both, wout = kept[4:]
    sets.append((0, *kept[:4]))
    parts = [za] + [swap(v, m) for v, m in zip(near_z, inner[1:])]
    dy, dyb, d_o = middle_back(y, parts, [swap(zb_lo, 1), swap(zb_hi, 1)], out_grad, wout, wide)
    d_o = lax.all_to_all(d_o, "seq", split_axis=0, concat_axis=0, tiled=True)

    def scatter_depth(value):
        return lax.psum_scatter(value, "dp", scatter_dimension=0, tiled=True)

    near_fa = jnp.stack([v[0] for v in near_f])
    near_fb = jnp.stack([v[1] for v in near_f])
    pair_raw, down_mine, wout_own, *parcels = ff_grads(
        seat_arr, [dyb], sets, ga, gb, o_both, dyb, swap(dyb, 1), near_fa, near_fb,
        (depth, OUTER * group, held, 2 * slab), tall, spread,
    )
    pair = scatter_depth(pair_raw.reshape(-1, 2 * slab)).reshape(OUTER * group, held, 2 * slab)
    masks = inner[1:] + across
    landed = [swap(v, m) for v, m in zip(parcels, masks)]

    sent = (tuple(across + inner), tuple(m + 1 for m in across + inner))
    e_mine, e_theirs, dwq = attn_bwd(
        seat_arr, lengths, xs, wqkv.shape, d_o, cosine, sine, qkv, ot, lse, r1, order, sent,
        [pair_raw],
    )
    *both, tail, dwq = back_to_x(
        seat_arr, e_mine, swap(e_theirs, 1), wqkv, wqkv_theirs, dwq, (down_mine, wout_own, landed)
    )
    far, close = both[:spread], both[spread:]
    got = [close[0]]
    got += [swap(close[j], inner[j]) for j in range(1, spread)]
    got += [swap(far[j], across[j]) for j in range(spread)]
    output = y + fa.astype(F32) + swap(fb, 1).astype(F32)
    output = output + sum(v[:many].astype(F32) for v in landed[: spread - 1])
    output = output.astype(BF16).reshape(tokens.shape)
    dwq = lax.all_to_all(
        dwq.reshape(devices, held, 3 * wide), every, split_axis=0, concat_axis=0, tiled=True
    )
    qkv_grad, gain1_grad = projection_grads(
        dwq.reshape(seats, depth, held, 3 * wide), qkv_weight, gain1, wide
    )
    pair = lax.all_to_all(pair, "seq", split_axis=0, concat_axis=0, tiled=True)
    gate_grad, up_grad, gain2_grad = pair_grads(
        pair.reshape(OUTER, group, held, 2 * slab), gate_weight, up_weight, gain2, depth, fan_rows
    )
    down_grad, out_grad_w = tail_grads(
        scatter_depth(tail.reshape(-1, width)), tall, fan_rows
    )
    d_tokens, d_first = token_grads(
        seat_arr, tokens, dy, got, wide, [qkv_grad, gate_grad, down_grad, output]
    )
    gain1_grad, gain2_grad = gain1_grad[:, 0], gain2_grad[:, 0]
    return (
        output, d_tokens, d_first, gain1_grad, qkv_grad, out_grad_w, gain2_grad, gate_grad, up_grad,
        down_grad,
    )


def solution(mesh):
    rows = P(("seq", "dp"), None)
    acts = P("dp", "seq", None)
    gains = P(("seq", "dp"))
    return jax.shard_map(
        local,
        mesh=mesh,
        in_specs=(acts, acts, acts, P("dp"), gains, rows, rows, gains, rows, rows, rows),
        out_specs=(acts, acts, acts, gains, rows, rows, gains, rows, rows, rows),
        check_vma=False,
    )
```

```python
import functools

import jax
import jax.numpy as jnp
import numpy as np
from jax import lax
from jax.experimental import pallas as pl
from jax.experimental.pallas import tpu as pltpu
from jax.sharding import PartitionSpec as P

HEADS = 16
HEAD_DIM = 64
EPSILON = 1e-06
CORES = 2
OUTER = 2
BLOCK = 256
NEG = -1e30
F32 = jnp.float32
BF16 = jnp.bfloat16
MIB = 1024 * 1024
FREE = pl.CostEstimate(flops=0, bytes_accessed=0, transcendentals=0)


def lasting(us):
    return pl.CostEstimate(flops=0, bytes_accessed=int(us * 3.69e6), transcendentals=0)


def vmem(mib, scale=1):
    return pltpu.CompilerParams(vmem_limit_bytes=int(min(60, mib * max(scale, 1))) * MIB)


def held_in_hbm(*arrays):
    return [pltpu.with_memory_space_constraint(a, pltpu.HBM) for a in arrays]


class Copies:
    def __init__(self, sems):
        self.sems, self.used, self.waiting = sems, 0, {}

    def start(self, name, src, dst):
        copy = pltpu.make_async_copy(src, dst, self.sems.at[self.used])
        self.used += 1
        copy.start()
        self.waiting.setdefault(name, []).append(copy)

    def wait(self, *names):
        for name in names or list(self.waiting):
            for copy in self.waiting.pop(name, []):
                copy.wait()


def corner(a):
    block = (1,) * (a.ndim - 2) + (min(16, a.shape[-2]), min(128, a.shape[-1]))
    return pl.BlockSpec(block, lambda *_: (0,) * a.ndim)


def dot_nn(a, b):
    return lax.dot_general(a, b, (((1,), (0,)), ((), ())), preferred_element_type=F32)


def dot_nt(a, b):
    return lax.dot_general(a, b, (((1,), (1,)), ((), ())), preferred_element_type=F32)


def dot_tn(a, b):
    return lax.dot_general(a, b, (((0,), (0,)), ((), ())), preferred_element_type=F32)


def turned(u):
    half = HEAD_DIM // 2
    width = u.shape[1]
    if width % 128:
        parts = []
        for h in range(width // HEAD_DIM):
            lo = h * HEAD_DIM
            parts += [u[:, lo + half : lo + HEAD_DIM], u[:, lo : lo + half]]
        return jnp.concatenate(parts, axis=1)
    lane = lax.broadcasted_iota(jnp.int32, u.shape, 1) % HEAD_DIM
    return jnp.where(lane < half, pltpu.roll(u, width - half, 1), pltpu.roll(u, half, 1))


def head_mask(shape, h):
    lane = lax.broadcasted_iota(jnp.int32, shape, 1)
    return (lane >= h * HEAD_DIM) & (lane < (h + 1) * HEAD_DIM)


def own_head(u, h):
    if u.shape[1] == HEAD_DIM:
        return u
    return jnp.where(head_mask(u.shape, h), u, jnp.zeros_like(u))


def join_heads(parts):
    out = parts[0]
    for h in range(1, len(parts)):
        out = jnp.where(head_mask(out.shape, h), parts[h], out)
    return out


def fill_rows(seat, refs, order, dest):
    rows = refs[0].shape[1]
    for ref, (m, lane) in zip(refs, order):
        at = pl.multiple_of((seat ^ m) * rows, rows)
        dest[pl.ds(at, rows), lane : lane + ref.shape[2]] = ref[0]


def attn_fwd_kernel(
    order, seat_ref, len_ref, w_ref, cos_ref, sin_ref, *refs,
):
    xs = refs[: len(order)]
    spread = len(refs) - len(order) - 6
    qkv_out, ot_out = refs[len(order) : len(order) + 2]
    sends = refs[len(order) + 2 : len(order) + 2 + spread]
    lse_out, r1_out, xbuf, vt = refs[-4:]
    slot = pl.program_id(0)
    seat = seat_ref[0]
    length = len_ref[slot]
    total = xbuf.shape[0]
    width = w_ref.shape[0]
    wide = w_ref.shape[1] // 3
    heads = wide // HEAD_DIM
    blocks = total // BLOCK
    fill_rows(seat, xs, order, xbuf)
    for b in range(blocks):
        at = slice(b * BLOCK, (b + 1) * BLOCK)
        x = xbuf[at, :width]
        xf = x.astype(F32)
        r1 = lax.rsqrt(jnp.mean(xf * xf, axis=1, keepdims=True) + EPSILON)
        qkv = dot_nn(x, w_ref[...]) * r1
        cosine = cos_ref[at, :]
        sine = sin_ref[at, :]
        q = qkv[:, :wide]
        k = qkv[:, wide : 2 * wide]
        v = qkv[:, 2 * wide :]
        q = (q * cosine + turned(q) * sine) * (HEAD_DIM**-0.5)
        k = k * cosine + turned(k) * sine
        first = xbuf[at, width : width + wide]
        second = xbuf[at, width + wide :]
        v1 = jnp.where(seat % CORES == 0, first, second).astype(F32)
        vm = 0.5 * v + 0.5 * v1
        qkv_out[0, at, :wide] = q.astype(BF16)
        qkv_out[0, at, wide : 2 * wide] = k.astype(BF16)
        qkv_out[0, at, 2 * wide :] = vm.astype(BF16)
        vt[:, at] = vm.T.astype(BF16)
        r1_out[0, at, :] = jnp.broadcast_to(r1, (BLOCK, r1_out.shape[2]))
    for b in range(blocks):
        at = slice(b * BLOCK, (b + 1) * BLOCK)
        count = (b + 1) * BLOCK
        q = qkv_out[0, at, :wide]
        query = b * BLOCK + lax.broadcasted_iota(jnp.int32, (1, BLOCK), 1)
        last = jnp.minimum(query, length - 1)
        key = lax.broadcasted_iota(jnp.int32, (count, BLOCK), 0)
        allowed = key <= last
        ots = []
        for h in range(heads):
            k = own_head(qkv_out[0, :count, wide : 2 * wide], h)
            scores = jnp.where(allowed, dot_nt(k, q), NEG)
            top = jnp.max(scores, axis=0, keepdims=True)
            weights = jnp.exp(scores - top)
            total_w = jnp.sum(weights, axis=0, keepdims=True)
            ot = dot_nn(vt[h * HEAD_DIM : (h + 1) * HEAD_DIM, :count], weights.astype(BF16))
            ots.append(ot / total_w)
            lse_out[0, h : h + 1, at] = top + jnp.log(total_w)
        ot = jnp.concatenate(ots, axis=0)
        ot_out[0, :, at] = ot
        o = ot.T.astype(BF16)
        for x in range(spread):
            sends[x ^ (b % spread)][(b // spread) * spread + x, 0] = o


def chunk_specs(xs, order, lanes):
    return [
        pl.BlockSpec((1, x.shape[1], min(x.shape[2], lanes - lane)), lambda i: (i, 0, 0))
        for x, (_, lane) in zip(xs, order)
    ]


def attn_fwd(seat, lengths, xs, w, cosine, sine, order, ready):
    micro, rows, lanes = xs[0].shape
    width = w.shape[0]
    total = cosine.shape[0]
    spread = total // rows // (OUTER * CORES)
    wide = w.shape[1] // 3
    heads = wide // HEAD_DIM
    smem = pl.BlockSpec(memory_space=pltpu.SMEM)
    whole = lambda a: pl.BlockSpec(a.shape, lambda i: (0,) * a.ndim)
    pairs = total * total // 2 * micro * wide
    return pl.pallas_call(
        functools.partial(attn_fwd_kernel, order),
        grid=(micro,),
        in_specs=[smem, smem, whole(w), whole(cosine), whole(sine)]
        + chunk_specs(xs, order, lanes)
        + [corner(a) for a in ready],
        out_specs=[
            pl.BlockSpec((1, total, 3 * wide), lambda i: (i, 0, 0)),
            pl.BlockSpec((1, wide, total), lambda i: (i, 0, 0)),
        ]
        + [pl.BlockSpec((OUTER * spread, 1, BLOCK, wide), lambda i: (0, i, 0, 0))] * spread
        + [
            pl.BlockSpec((1, heads, total), lambda i: (i, 0, 0)),
            pl.BlockSpec((1, total, 128), lambda i: (i, 0, 0)),
        ],
        out_shape=[
            pltpu.HBM((micro, total, 3 * wide), BF16),
            pltpu.HBM((micro, wide, total), F32),
        ]
        + [pltpu.HBM((OUTER * spread, micro, BLOCK, wide), BF16)] * spread
        + [
            pltpu.HBM((micro, heads, total), F32),
            pltpu.HBM((micro, total, 128), F32),
        ],
        scratch_shapes=[pltpu.VMEM((total, lanes), BF16), pltpu.VMEM((wide, total), BF16)],
        compiler_params=vmem(30, total / 1024),
        cost_estimate=lasting(20),
        name="attn_fwd",
    )(seat, lengths, *held_in_hbm(w, cosine, sine, *xs), *ready)


def attn_bwd_kernel(
    order, sent, seat_ref, len_ref, do_ref, cos_ref, sin_ref, qkv_ref, ot_ref, lse_ref, r1_ref,
    *refs,
):
    xs = refs[: len(order)]
    outs = refs[-6 - CORES : -6]
    dw_out, xbuf, dobuf, dqt, ebuf, dw = refs[-6:]
    slot = pl.program_id(0)
    seat = seat_ref[0]
    rows = do_ref.shape[2]
    length = len_ref[slot]
    total = xbuf.shape[0]
    wide = do_ref.shape[3]
    heads = wide // HEAD_DIM
    blocks = total // BLOCK
    fill_rows(seat, xs, order, xbuf)
    for j in range(do_ref.shape[0]):
        dobuf[j * rows : (j + 1) * rows, :] = do_ref[j, 0]
    dot_t = dobuf[...].astype(F32).T
    deltas = []
    for h in range(heads):
        part = slice(h * HEAD_DIM, (h + 1) * HEAD_DIM)
        deltas.append(jnp.sum(dot_t[part, :] * ot_ref[0, part, :], axis=0, keepdims=True))
    dqt[...] = jnp.zeros_like(dqt)
    for b in range(blocks):
        at = slice(b * BLOCK, (b + 1) * BLOCK)
        later = slice(b * BLOCK, total)
        count = total - b * BLOCK
        k = qkv_ref[0, at, wide : 2 * wide]
        v = qkv_ref[0, at, 2 * wide :]
        kt = k.astype(F32).T.astype(BF16)
        q = qkv_ref[0, later, :wide]
        d_o = dobuf[later, :]
        query = b * BLOCK + lax.broadcasted_iota(jnp.int32, (1, count), 1)
        last = jnp.minimum(query, length - 1)
        key = b * BLOCK + lax.broadcasted_iota(jnp.int32, (BLOCK, count), 0)
        allowed = key <= last
        dks, dvs = [], []
        for h in range(heads):
            part = slice(h * HEAD_DIM, (h + 1) * HEAD_DIM)
            scores = jnp.where(allowed, dot_nt(own_head(k, h), q), NEG)
            weights = jnp.exp(scores - lse_ref[0, h : h + 1, later])
            d_weights = dot_nt(own_head(v, h), d_o)
            ds = (weights * (d_weights - deltas[h][:, later])).astype(BF16)
            dvs.append(dot_nn(weights.astype(BF16), d_o))
            dks.append(dot_nn(ds, q))
            dqt[part, later] += dot_nn(kt[part, :], ds)
        cosine = cos_ref[at, :]
        sine = sin_ref[at, :]
        r1 = r1_ref[0, at, 0:1]
        dk = join_heads(dks)
        dk = dk * cosine - turned(dk) * sine
        dv = 0.5 * join_heads(dvs)
        ebuf[at, 3 * wide :] = dv.astype(BF16)
        ebuf[at, wide : 2 * wide] = (dk * r1).astype(BF16)
        ebuf[at, 2 * wide : 3 * wide] = (dv * r1).astype(BF16)
    for b in range(blocks):
        at = slice(b * BLOCK, (b + 1) * BLOCK)
        dq = dqt[:, at].T * (HEAD_DIM**-0.5)
        dq = dq * cos_ref[at, :] - turned(dq) * sin_ref[at, :]
        ebuf[at, :wide] = (dq * r1_ref[0, at, 0:1]).astype(BF16)
    for low, out in enumerate(outs):
        for j, m in enumerate(sent):
            at = pl.multiple_of((seat ^ m ^ low) * rows, rows)
            out[j, 0] = ebuf[pl.ds(at, rows), :]
    grown = dot_tn(xbuf[...], ebuf[:, : 3 * wide])

    @pl.when(slot == 0)
    def _():
        dw[...] = grown

    @pl.when(slot > 0)
    def _():
        dw[...] += grown

    @pl.when(slot == pl.num_programs(0) - 1)
    def _():
        dw_out[...] = dw[...].astype(BF16)


def attn_bwd(seat, lengths, xs, wshape, d_o, cosine, sine, qkv, ot, lse, r1, order, sent, ready):
    micro, rows = xs[0].shape[:2]
    width = wshape[0]
    total = cosine.shape[0]
    wide = wshape[1] // 3
    heads = wide // HEAD_DIM
    smem = pl.BlockSpec(memory_space=pltpu.SMEM)
    whole = lambda a: pl.BlockSpec(a.shape, lambda i: (0,) * a.ndim)
    vspec = pl.BlockSpec((d_o.shape[0], 1, rows, wide), lambda i: (0, i, 0, 0))
    zshapes = [pltpu.HBM((len(sent), micro, rows, 4 * wide), BF16)] * CORES
    pairs = total * total // 2 * micro * wide
    return pl.pallas_call(
        functools.partial(attn_bwd_kernel, order, sent),
        grid=(micro,),
        in_specs=[
            smem, smem, vspec, whole(cosine), whole(sine),
            pl.BlockSpec((1, total, 3 * wide), lambda i: (i, 0, 0)),
            pl.BlockSpec((1, wide, total), lambda i: (i, 0, 0)),
            pl.BlockSpec((1, heads, total), lambda i: (i, 0, 0)),
            pl.BlockSpec((1, total, 128), lambda i: (i, 0, 0)),
        ]
        + chunk_specs(xs, order, width)
        + [corner(a) for a in ready],
        out_specs=[
            pl.BlockSpec((len(sent), 1, rows, 4 * wide), lambda i: (0, i, 0, 0))
        ]
        * CORES
        + [pl.BlockSpec(wshape, lambda i: (0, 0))],
        out_shape=zshapes + [pltpu.HBM(wshape, BF16)],
        scratch_shapes=[
            pltpu.VMEM((total, width), BF16),
            pltpu.VMEM((total, wide), BF16),
            pltpu.VMEM((wide, total), F32),
            pltpu.VMEM((total, 4 * wide), BF16),
            pltpu.VMEM(wshape, F32),
        ],
        compiler_params=vmem(40, total / 1024),
        cost_estimate=lasting(20),
        name="attn_bwd",
    )(seat, lengths, *held_in_hbm(d_o, cosine, sine, qkv, ot, lse, r1, *xs), *ready)


def ff_kernel(
    own, parts, seat_ref, xa, xb, oa, ob, pair, down_mine, down_far, wout_mine, wout_theirs, *refs,
):
    cotangents, refs = (refs[:parts], refs[parts : 2 * parts]), refs[2 * parts :]
    za, zb_lo, zb_hi, fa, fb, hn_out, hid_out, dgate_out, dup_out = refs[:9]
    refs = refs[9:]
    if own:
        y_out, o_out, wout_out = refs[:3]
        refs = refs[3:]
    x_buf, g_buf, oa_buf, ob_buf, wout, wg, wu, wd, z_buf, f_buf, hn, hid, dgate, dup, y_buf, o_buf, sems = refs
    seat = seat_ref[0]
    core = seat % CORES
    micro, rows = xa.shape[:2]
    width = wout.shape[0]
    many = micro * rows
    depth, outer, group, held, slab2 = pair.shape
    slab = slab2 // 2
    spread = group // CORES
    tall = down_mine.shape[1]
    half = seat // group
    copies = Copies(sems)

    for low in range(CORES):
        there = pl.ds(pl.multiple_of((core ^ low) * rows, rows), rows)
        copies.start("o", oa.at[:, :, there, :], oa_buf.at[low])
        copies.start("o", ob.at[:, :, there, :], ob_buf.at[low])
    for rc, ref in enumerate((wout_mine, wout_theirs)):
        for rx in range(spread):
            for ry in range(outer):
                other = seat ^ (ry * group + rx * CORES + rc)
                for d in range(depth):
                    to = pl.ds(pl.multiple_of((other * depth + d) * held, held), held)
                    copies.start("wout", ref.at[rx, ry, d], wout.at[to, :])
    copies.start("x", xa.at[:, :, pl.ds(0, width)], x_buf.at[0])
    copies.start("x", xb.at[:, :, pl.ds(0, width)], x_buf.at[1])
    for part, dest in ((0, wg), (1, wu)):
        for y in range(outer):
            for q in range(group):
                for d in range(depth):
                    to = ((y * group + q) * depth + d) * held
                    copies.start(
                        "wg" if part == 0 else "wu",
                        pair.at[d, y, q, :, pl.ds(part * slab, slab)],
                        dest.at[pl.ds(to, held), :],
                    )
    for low, some in enumerate(cotangents):
        base = 0
        for ref in some:
            copies.start("g", ref, g_buf.at[low, pl.ds(base, ref.shape[0])])
            base += ref.shape[0]
    for ry, ref in enumerate((down_mine, down_far)):
        for d in range(depth):
            to = pl.ds(pl.multiple_of(((half ^ ry) * depth + d) * tall, tall), tall)
            copies.start("wd", ref.at[d], wd.at[to, :])

    copies.wait("o")
    for low in range(CORES):
        for j in range(oa_buf.shape[1]):
            a = oa_buf[low, j].reshape(many, oa_buf.shape[4])
            b = ob_buf[low, j].reshape(many, oa_buf.shape[4])
            wide = a.shape[1]
            here = slice(low * many, (low + 1) * many)
            o_buf[here, (2 * j) * wide : (2 * j + 1) * wide] = jnp.where(core == 0, a, b)
            o_buf[here, (2 * j + 1) * wide : (2 * j + 2) * wide] = jnp.where(core == 0, b, a)
    copies.wait("wout", "x")
    if own:
        copies.start("out", wout, wout_out)
        copies.start("out", o_buf, o_out)
    y = x_buf[...].reshape(2 * many, width).astype(F32) + dot_nn(o_buf[...], wout[...])
    r2 = lax.rsqrt(jnp.mean(y * y, axis=1, keepdims=True) + EPSILON)
    hn[...] = (y * r2).astype(BF16)
    if own:
        y_buf[...] = y[:many]
        copies.start("out", y_buf, y_out)
    copies.start("out", hn, hn_out)
    copies.wait("wg")
    gate = dot_nn(hn[...], wg[...])
    copies.wait("wu")
    up = dot_nn(hn[...], wu[...])
    sigma = jax.nn.sigmoid(gate)
    act = gate * sigma
    hid[...] = (act * up).astype(BF16)
    copies.start("out", hid, hid_out)
    copies.wait("g", "wd")
    dhid = dot_nt(g_buf[...].reshape(2 * many, width), wd[...])
    dgate[...] = (dhid * up * (sigma + act * (1.0 - sigma))).astype(BF16)
    dup[...] = (dhid * act).astype(BF16)
    copies.start("out", dgate, dgate_out)
    copies.start("out", dup, dup_out)
    z_buf[...] = (dot_nt(dgate[...], wg[...]) + dot_nt(dup[...], wu[...])).astype(BF16)
    copies.start("out", z_buf.at[pl.ds(0, many)], za)
    copies.start("out", z_buf.at[pl.ds(many, many // 2)], zb_lo)
    copies.start("out", z_buf.at[pl.ds(many + many // 2, many // 2)], zb_hi)
    f_buf[...] = dot_nn(hid[...], wd[...]).astype(BF16)
    copies.start("out", f_buf.at[pl.ds(0, many)], fa)
    copies.start("out", f_buf.at[pl.ds(many, many)], fb)
    copies.wait()


def feed_forward(seat, xa, xb, ga, gb, oa, ob, weights, own):
    pair, down_mine, down_far, wout_mine, wout_theirs = weights
    micro, rows = xa.shape[:2]
    width = ga[0].shape[2]
    many = micro * rows
    depth, outer, group, held, slab2 = pair.shape
    fan = slab2 // 2
    wide = oa.shape[3]
    outs = [(many, width), (many // 2, width), (many // 2, width), (many, width), (many, width)]
    outs = [pltpu.HBM(s, BF16) for s in outs + [(2 * many, width)] + [(2 * many, fan)] * 3]
    if own:
        outs += [
            pltpu.HBM((many, width), F32), pltpu.HBM((2 * many, width), BF16),
            pltpu.HBM((width, width), BF16),
        ]
    o_shape = (CORES, oa.shape[0], micro, rows, wide)
    scratch = [
        ((2, micro, rows, width), BF16), ((2, micro, rows, width), BF16), (o_shape, BF16),
        (o_shape, BF16), ((width, width), BF16), ((width, fan), BF16), ((width, fan), BF16),
        ((fan, width), BF16), ((2 * many, width), BF16), ((2 * many, width), BF16),
        ((2 * many, width), BF16), ((2 * many, fan), BF16), ((2 * many, fan), BF16),
        ((2 * many, fan), BF16), ((many, width), F32), ((2 * many, width), BF16),
    ]
    many_copies = 32 + 4 * outer * group * depth
    anywhere = pl.BlockSpec(memory_space=pl.ANY)
    return pl.pallas_call(
        functools.partial(ff_kernel, own, len(ga)),
        grid=(1,),
        in_specs=[pl.BlockSpec(memory_space=pltpu.SMEM)]
        + [anywhere] * (9 + 2 * len(ga)),
        out_specs=[anywhere] * len(outs),
        out_shape=outs,
        scratch_shapes=[pltpu.VMEM(s, t) for s, t in scratch]
        + [pltpu.SemaphoreType.DMA((many_copies,))],
        compiler_params=vmem(56),
        cost_estimate=lasting(16),
        name="ff_own" if own else "ff_near",
    )(seat, *held_in_hbm(xa, xb, oa, ob, *weights, *ga, *gb))


def ff_grads_kernel(sizes, group, spread, seat_ref, *refs):
    sets = []
    for size in sizes:
        sets.append(refs[:size])
        refs = refs[size:]
    o_ref, dyb_ref, dyb_theirs, fa, fb = refs[:5]
    refs = refs[5:]
    pair_out, down_mine, wout_own = refs[:3]
    parcels = refs[3 : 2 + 2 * spread]
    dwg, dwu, dwd, dwo = refs[2 + 2 * spread :]
    seat = seat_ref[0]
    outer = seat // group
    core = seat % CORES
    chip = seat // CORES
    depth, blocks, held, slab2 = pair_out.shape
    slab = slab2 // 2
    tall = down_mine.shape[1]
    many, width = dyb_ref.shape
    for n, (hn, hid, dgate, dup, *gs) in enumerate(sets):
        g = jnp.concatenate([r[...].reshape(-1, width) for r in gs], axis=0)
        new = dot_tn(hn[...], dgate[...]), dot_tn(hn[...], dup[...]), dot_tn(hid[...], g)
        for scratch, value in zip((dwg, dwu, dwd), new):
            if n == 0:
                scratch[...] = value
            else:
                scratch[...] += value
    for k in range(blocks):
        for d in range(depth):
            at = slice((k * depth + d) * held, (k * depth + d + 1) * held)
            pair_out[d, k, :, :slab] = dwg[at, :].astype(BF16)
            pair_out[d, k, :, slab:] = dwu[at, :].astype(BF16)
    far = parcels[spread - 1]
    for d in range(depth):
        pieces = []
        for k in range(OUTER):
            at = slice((k * depth + d) * tall, (k * depth + d + 1) * tall)
            pieces.append(dwd[at, :].astype(BF16))
        down_mine[d] = jnp.where(outer == 0, pieces[0], pieces[1])
        far[d * tall : (d + 1) * tall, :] = jnp.where(outer == 0, pieces[1], pieces[0])
    dyb = jnp.concatenate([dyb_ref[...], dyb_theirs[...]], axis=0)
    rows = depth * held
    for c in range(2 * spread):
        a = o_ref[:, (2 * c) * rows : (2 * c + 1) * rows]
        b = o_ref[:, (2 * c + 1) * rows : (2 * c + 2) * rows]
        dwo[c * rows : (c + 1) * rows, :] = dot_tn(jnp.where(core == 0, a, b), dyb)
    for j in range(2 * spread):
        at = pl.ds(pl.multiple_of((chip ^ j) * rows, rows), rows)
        value = dwo[at, :].astype(BF16)
        if j == 0:
            wout_own[...] = value
        else:
            out = parcels[j - 1]
            out[out.shape[0] - rows :, :] = value
    for j in range(spread - 1):
        parcels[j][:many, :] = (fa[j].astype(F32) + fb[j].astype(F32)).astype(BF16)


def ff_grads(seat, sets, o_both, dyb, dyb_theirs, fa, fb, pair_shape, tall, spread):
    def fixed(shape):
        return pl.BlockSpec(shape, lambda i: (0,) * len(shape), pipeline_mode=pl.Buffered(1))

    args = [a for arrays in sets for a in arrays]
    last = [o_both, dyb, dyb_theirs, fa, fb]
    args += last
    specs = [fixed(a.shape) for a in args]
    depth, _, held, slab2 = pair_shape
    many, width = dyb.shape
    fan = slab2 // 2
    rows = depth * held
    parcels = [(many + rows, width)] * (spread - 1) + [(depth * tall + rows, width)]
    parcels += [(rows, width)] * (spread - 1)
    outs = [pair_shape, (depth, tall, width), (rows, width)] + parcels
    return pl.pallas_call(
        functools.partial(ff_grads_kernel, [len(s) for s in sets], spread * CORES, spread),
        grid=(1,),
        in_specs=[pl.BlockSpec(memory_space=pltpu.SMEM)] + specs,
        out_specs=[fixed(s) for s in outs],
        out_shape=[pltpu.HBM(s, BF16) for s in outs],
        scratch_shapes=[
            pltpu.VMEM((width, fan), F32), pltpu.VMEM((width, fan), F32),
            pltpu.VMEM((fan, width), F32), pltpu.VMEM((2 * spread * rows, width), F32),
        ],
        compiler_params=vmem(56),
        cost_estimate=lasting(14),
        name="ff_grads",
    )(seat, *args)


def pieces_at(values, index):
    step = 1
    while step < len(values):
        flip = (index // step) % 2 == 1
        values = [jnp.where(flip, values[k ^ step], values[k]) for k in range(len(values))]
        step *= 2
    return values


def payloads(seat, tokens, first_values, spread, wide):
    micro, rows, width = tokens.shape
    lanes = CORES * wide

    def kernel(seat_ref, x_ref, *refs):
        firsts, outs = refs[: 2 * spread], refs[2 * spread :]
        for out in outs:
            out[0, :, :width] = x_ref[0]
        for j in range(spread):
            outs[1][0, :, width + j * lanes : width + (j + 1) * lanes] = firsts[spread + j][0]
            outs[j and 1 + j][0, :, width:] = firsts[j][0]

    def part(j):
        return pl.BlockSpec((1, rows, lanes), lambda i, s: (i, 0, (s[0] // CORES) ^ j))

    sizes = [width + lanes, width + spread * lanes] + [width + lanes] * (spread - 1)
    return pl.pallas_call(
        kernel,
        grid_spec=pltpu.PrefetchScalarGridSpec(
            num_scalar_prefetch=1,
            grid=(micro,),
            in_specs=[pl.BlockSpec((1, rows, width), lambda i, s: (i, 0, 0))]
            + [part(j) for j in range(2 * spread)],
            out_specs=[pl.BlockSpec((1, rows, n), lambda i, s: (i, 0, 0)) for n in sizes],
        ),
        out_shape=[pltpu.HBM((micro, rows, n), BF16) for n in sizes],
        cost_estimate=lasting(4),
        name="payloads",
    )(seat, *held_in_hbm(tokens, *([first_values] * (2 * spread))))


def middle_back(y, parts, pieces, grad, wout, wide):
    micro, rows, width = grad.shape
    seats = width // wide
    many = micro * rows

    def kernel(y_ref, g_ref, w_ref, *refs):
        zs = refs[: len(parts)]
        z = jnp.concatenate([r[...] for r in refs[len(parts) : len(parts) + len(pieces)]], axis=0)
        dy_out, dyb_out, do_out = refs[len(parts) + len(pieces) :]
        z = z.astype(F32)
        for ref in zs:
            z = z + ref[...].astype(F32)
        y = y_ref[...]
        r2 = lax.rsqrt(jnp.mean(y * y, axis=1, keepdims=True) + EPSILON)
        inner = jnp.mean(z * y, axis=1, keepdims=True)
        g = g_ref[...].reshape(many, width).astype(F32)
        dy = g + r2 * z - y * (r2 * r2 * r2 * inner)
        dy_out[...] = dy
        dyb = dy.astype(BF16)
        dyb_out[...] = dyb
        d_o = dot_nt(dyb, w_ref[...]).astype(BF16)
        for s in range(seats):
            do_out[s] = d_o[:, s * wide : (s + 1) * wide].reshape(micro, rows, wide)

    def fixed(shape):
        return pl.BlockSpec(shape, lambda i: (0,) * len(shape), pipeline_mode=pl.Buffered(1))

    given = held_in_hbm(y, grad, wout, parts[0]) + [*parts[1:], *pieces]
    return pl.pallas_call(
        kernel,
        grid=(1,),
        in_specs=[fixed(a.shape) for a in given],
        out_specs=[
            fixed((many, width)), fixed((many, width)), fixed((seats, micro, rows, wide)),
        ],
        out_shape=[
            pltpu.HBM((many, width), F32),
            pltpu.HBM((many, width), BF16),
            pltpu.HBM((seats, micro, rows, wide), BF16),
        ],
        compiler_params=vmem(24),
        cost_estimate=FREE,
        name="middle_back",
    )(*given)


def back_to_x(seat, mine, theirs, w_mine, w_theirs):
    count, micro, rows, lanes = mine.shape
    width = w_mine.shape[0]
    wide = lanes // 4
    many = micro * rows

    def kernel(seat_ref, a_ref, b_ref, wa, wb, *refs):
        outs = refs[:count]
        buf, sems = refs[-2:]
        core = seat_ref[0] % CORES
        copies = Copies(sems)
        for j in range(count):
            a = a_ref[j].reshape(many, lanes)
            b = b_ref[j].reshape(many, lanes)
            z = dot_nt(a[:, : 3 * wide], wa[...]) + dot_nt(b[:, : 3 * wide], wb[...])
            buf[j, :, :, :width] = z.astype(BF16).reshape(micro, rows, width)
            first = jnp.where(core == 0, a[:, 3 * wide :], b[:, 3 * wide :])
            second = jnp.where(core == 0, b[:, 3 * wide :], a[:, 3 * wide :])
            buf[j, :, :, width : width + wide] = first.reshape(micro, rows, wide)
            buf[j, :, :, width + wide :] = second.reshape(micro, rows, wide)
            copies.start("out", buf.at[j], outs[j])
        copies.wait()

    anywhere = pl.BlockSpec(memory_space=pl.ANY)
    out = pltpu.HBM((micro, rows, width + CORES * wide), BF16)
    fixed = lambda shape: pl.BlockSpec(
        shape, lambda i: (0,) * len(shape), pipeline_mode=pl.Buffered(1)
    )
    given = held_in_hbm(mine) + [theirs, w_mine, w_theirs]
    return pl.pallas_call(
        kernel,
        grid=(1,),
        in_specs=[pl.BlockSpec(memory_space=pltpu.SMEM)] + [fixed(a.shape) for a in given],
        out_specs=[anywhere] * count,
        out_shape=[out] * count,
        scratch_shapes=[
            pltpu.VMEM((count, micro, rows, width + CORES * wide), BF16),
            pltpu.SemaphoreType.DMA((count,)),
        ],
        compiler_params=vmem(32),
        cost_estimate=lasting(5),
        name="back_to_x",
    )(seat, *given)


def plane_sums(level, down, wout, parcels):
    depth, tall, width = down.shape
    held = wout.shape[0] // depth
    spread = (len(parcels) + 1) // 2

    def kernel(level_ref, down_ref, wout_ref, *refs):
        parts, outs = refs[: len(parcels)], refs[len(parcels) :]
        far = parts[spread - 1]
        for k, out in enumerate(outs):
            d = level_ref[0] ^ k
            at = pl.ds(pl.multiple_of(d * tall, tall), tall)
            out[:tall, :] = (down_ref[d].astype(F32) + far[at, :].astype(F32)).astype(BF16)
            at = pl.ds(pl.multiple_of(d * held, held), held)
            total = wout_ref[at, :].astype(F32)
            for part in parts:
                base = part.shape[0] - depth * held
                at = pl.ds(pl.multiple_of(base + d * held, held), held)
                total = total + part[at, :].astype(F32)
            out[tall:, :] = total.astype(BF16)

    fixed = lambda shape: pl.BlockSpec(
        shape, lambda i: (0,) * len(shape), pipeline_mode=pl.Buffered(1)
    )
    given = [down, wout, *parcels]
    shape = (tall + held, width)
    return pl.pallas_call(
        kernel,
        grid=(1,),
        in_specs=[pl.BlockSpec(memory_space=pltpu.SMEM)] + [fixed(a.shape) for a in given],
        out_specs=[fixed(shape)] * depth,
        out_shape=[pltpu.HBM(shape, BF16)] * depth,
        compiler_params=vmem(24),
        cost_estimate=FREE,
        name="plane_sums",
    )(level, *given)


def add_parts(mine, theirs):
    def kernel(a_ref, *refs):
        b = jnp.concatenate([r[...] for r in refs[:-1]], axis=0)
        refs[-1][...] = (a_ref[...].astype(F32) + b.astype(F32)).astype(BF16)

    fixed = lambda shape: pl.BlockSpec(
        shape, lambda i: (0,) * len(shape), pipeline_mode=pl.Buffered(1)
    )
    return pl.pallas_call(
        kernel,
        grid=(1,),
        in_specs=[fixed(a.shape) for a in (mine, *theirs)],
        out_specs=fixed(mine.shape),
        out_shape=pltpu.HBM(mine.shape, BF16),
        compiler_params=vmem(16),
        cost_estimate=FREE,
        name="add_parts",
    )(mine, *theirs)


def tail_grads(parts, tall, short):
    rows, width = parts[0].shape

    def kernel(*refs):
        *ins, down_out, wout_out = refs
        total = ins[0][...].astype(F32)
        for ref in ins[1:]:
            total = total + ref[...].astype(F32)
        down_out[...] = total[:short, :]
        wout_out[...] = total[tall:, :]

    return pl.pallas_call(
        kernel,
        out_shape=[pltpu.HBM((short, width), F32), pltpu.HBM((rows - tall, width), F32)],
        cost_estimate=FREE,
        name="tail_grads",
    )(*parts)


def onward(arrived, far_own, width, lanes, split):
    count = len(arrived)
    micro, rows, _ = far_own.shape

    def kernel(*refs):
        blocks, far, outs = refs[:count], refs[count], refs[count + 1 :]
        for j in range(count):
            outs[j][0] = blocks[j][0, :, :split]
            outs[count + j][0, :, : width - split] = far[0, :, split:width]
            at = width + (j + 1) * lanes
            outs[count + j][0, :, width - split :] = far[0, :, at : at + lanes]

    spec = lambda n: pl.BlockSpec((1, rows, n), lambda i: (i, 0, 0))
    sizes = [split] * count + [width + lanes - split] * count
    out = pl.pallas_call(
        kernel,
        grid=(micro,),
        in_specs=[spec(a.shape[2]) for a in (*arrived, far_own)],
        out_specs=[spec(n) for n in sizes],
        out_shape=[pltpu.HBM((micro, rows, n), BF16) for n in sizes],
        cost_estimate=FREE,
        name="onward",
    )(*arrived, far_own)
    return out[:count], out[count:]


def fence(value, ready):
    def kernel(*_):
        pass

    return pl.pallas_call(
        kernel,
        grid=(1,),
        in_specs=[pl.BlockSpec(memory_space=pl.ANY)] + [corner(a) for a in ready],
        out_specs=pl.BlockSpec(memory_space=pl.ANY),
        out_shape=pltpu.HBM(value.shape, value.dtype),
        input_output_aliases={0: 0},
        cost_estimate=FREE,
        name="fence",
    )(value, *ready)


def token_grads(seat, tokens, dy, got, wide, ready):
    micro, rows, width = tokens.shape
    lanes = CORES * wide

    def kernel(seat_ref, x_ref, dy_ref, *refs):
        parts = refs[: len(got)]
        dx_out, dv_out = refs[-2:]
        z = parts[0][0, :, :width].astype(F32)
        for ref in parts[1:]:
            z = z + ref[0, :, :width].astype(F32)
        x = x_ref[0].astype(F32)
        inv = lax.rsqrt(jnp.mean(x * x, axis=1, keepdims=True) + EPSILON)
        inner = jnp.mean(z * x, axis=1, keepdims=True)
        dx_out[0] = dy_ref[...] + z - x * (inv * inv * inner)
        firsts = pieces_at([ref[0, :, width:].astype(F32) for ref in parts], seat_ref[0] // CORES)
        for k, value in enumerate(firsts):
            dv_out[0, :, k * lanes : (k + 1) * lanes] = value

    spec = pl.BlockSpec((1, rows, width), lambda i: (i, 0, 0))
    return pl.pallas_call(
        kernel,
        grid=(micro,),
        in_specs=[
            pl.BlockSpec(memory_space=pltpu.SMEM), spec, pl.BlockSpec((rows, width), lambda i: (i, 0)),
        ]
        + [pl.BlockSpec((1, rows, width + lanes), lambda i: (i, 0, 0))] * len(got)
        + [corner(a) for a in ready],
        out_specs=[spec, spec],
        out_shape=[pltpu.HBM(tokens.shape, F32)] * 2,
        cost_estimate=FREE,
        name="token_grads",
    )(seat, tokens, dy, *got, *ready)


def projection_grads(parts, weight, gain, wide):
    seats, depth, held, _ = parts.shape
    width = seats * wide

    def kernel(p_ref, w_ref, gain_ref, dw_out, dg_out):
        gain = gain_ref[...]
        grown = jnp.zeros((held, 1), F32)
        for s in range(seats):
            total = p_ref[s, 0].astype(F32)
            for d in range(1, depth):
                total = total + p_ref[s, d].astype(F32)
            for t in range(3):
                at = slice(t * width + s * wide, t * width + (s + 1) * wide)
                piece = total[:, t * wide : (t + 1) * wide]
                dw_out[:, at] = piece * gain
                grown = grown + jnp.sum(piece * w_ref[:, at].astype(F32), axis=1, keepdims=True)
        dg_out[...] = grown

    return pl.pallas_call(
        kernel,
        out_shape=[
            pltpu.HBM(weight.shape, F32), pltpu.HBM((held, 1), F32),
        ],
        cost_estimate=FREE,
        name="projection_grads",
    )(parts, weight, gain)


def pair_grads(parts, gate, up, gain, depth, short):
    outer, group, held, slab2 = parts.shape
    slab = slab2 // 2
    tall = slab // (OUTER * depth)
    fan = gate.shape[1]

    def kernel(p_ref, gate_ref, up_ref, gain_ref, dgate_out, dup_out, dg_out):
        for q in range(group):
            total = p_ref[0, q].astype(F32)
            for y in range(1, outer):
                total = total + p_ref[y, q].astype(F32)
            for m, out in enumerate((dgate_out, dup_out)):
                for y in range(OUTER):
                    for d in range(depth):
                        at = m * slab + (y * depth + d) * tall
                        to = ((y * group + q) * depth + d) * short
                        out[:, to : to + short] = total[:, at : at + short]
        dgate = dgate_out[...]
        dup = dup_out[...]
        dg_out[...] = jnp.sum(
            dgate * gate_ref[...].astype(F32) + dup * up_ref[...].astype(F32),
            axis=1,
            keepdims=True,
        )
        dgate_out[...] = dgate * gain_ref[...]
        dup_out[...] = dup * gain_ref[...]

    return pl.pallas_call(
        kernel,
        out_shape=[
            pltpu.HBM((held, fan), F32), pltpu.HBM((held, fan), F32), pltpu.HBM((held, 1), F32),
        ],
        cost_estimate=FREE,
        name="pair_grads",
    )(parts, gate, up, gain)


def rope_tables(total, wide):
    positions = np.arange(total, dtype=np.float32)
    inverse = np.float32(10000.0) ** (-np.arange(0, HEAD_DIM, 2, dtype=np.float32) / HEAD_DIM)
    angles = (positions[:, None] * inverse[None, :].astype(np.float32)).astype(np.float64)
    cosine, sine = np.cos(angles), np.sin(angles)
    cosine = np.tile(cosine, (1, 2 * wide // HEAD_DIM))
    sine = np.tile(np.concatenate([-sine, sine], -1), (1, wide // HEAD_DIM))
    return jnp.asarray(cosine.astype(np.float32)), jnp.asarray(sine.astype(np.float32))


def local(
    tokens, first_values, out_grad, lengths, norm1_gain, qkv_weight, out_weight, norm2_gain,
    gate_weight, up_weight, down_weight,
):
    micro, rows, width = tokens.shape
    seats, depth = lax.axis_size("seq"), lax.axis_size("dp")
    devices = seats * depth
    seat = lax.axis_index("seq")
    group = seats // OUTER
    spread = group // CORES
    outer = seat // group
    total = seats * rows
    wide = width // seats
    held = qkv_weight.shape[0]
    fan_rows = down_weight.shape[0]
    fan = fan_rows * devices
    tall = -(-fan_rows // 16) * 16
    slab = OUTER * depth * tall
    many = micro * rows
    seat_arr = jnp.reshape(seat, (1,)).astype(jnp.int32)
    level_arr = jnp.reshape(lax.axis_index("dp"), (1,)).astype(jnp.int32)

    def swap(value, mask):
        return lax.ppermute(value, "seq", [(i, i ^ mask) for i in range(seats)])

    def token(value):
        return value[(0,) * value.ndim].astype(F32) * 0.0

    def swap_depth(value, mask):
        return lax.ppermute(value, "dp", [(i, i ^ mask) for i in range(depth)])

    same_core = [[i for i in range(seats) if i % CORES == c] for c in range(CORES)]
    every = ("seq", "dp")
    core = seat % CORES
    chip = seat // CORES
    inner = [2 * j for j in range(spread)]
    across = [group + 2 * j for j in range(spread)]

    gain1 = norm1_gain.astype(F32)[:, None]
    gain2 = norm2_gain.astype(F32)[:, None]

    lanes = width + CORES * wide

    def together(part, *operands):
        shapes = jax.eval_shape(part, *operands)
        return lax.cond(
            lengths[0] > 0,
            part,
            lambda *_: jax.tree.map(lambda s: jnp.zeros(s.shape, s.dtype), shapes),
            *operands,
        )

    def to_seats(value, groups=None):
        return lax.all_to_all(
            value, "seq", split_axis=0, concat_axis=0, tiled=True, axis_index_groups=groups
        )

    def to_all(value):
        return lax.all_to_all(value, every, split_axis=0, concat_axis=0, tiled=True)

    tail = jnp.concatenate(
        [jnp.pad(down_weight, ((0, tall - fan_rows), (0, 0))), out_weight], 0
    )
    tail = lax.all_gather(tail, "dp", axis=0)

    def columns(weight):
        scaled = (weight.astype(F32) * gain2).astype(BF16)
        scaled = scaled.reshape(held, OUTER, group, depth, fan_rows).transpose(2, 0, 1, 3, 4)
        scaled = jnp.pad(scaled, ((0, 0),) * 4 + ((0, tall - fan_rows),))
        return scaled.reshape(group, held, slab)

    def weights_first():
        pair = jnp.concatenate([columns(gate_weight), columns(up_weight)], -1)
        pair = jnp.concatenate([pair] * OUTER, 0)
        wqkv = (qkv_weight.astype(F32) * gain1).astype(BF16)
        wqkv = wqkv.reshape(held, 3, seats, wide).transpose(2, 0, 1, 3).reshape(seats, held, 3 * wide)
        both = to_seats(jnp.concatenate([pair, wqkv], -1))
        return (
            both[..., : 2 * slab], both[..., 2 * slab :],
            payloads(seat_arr, tokens, first_values, spread, wide),
        )

    pair, wqkv, (own, far_own, *arrived) = together(weights_first)
    pair = lax.all_gather(pair, "dp", axis=0).reshape(depth, OUTER, group, held, 2 * slab)

    def first_leg(arrived, far_own, own, wqkv):
        return (
            [swap(v, m) for v, m in zip(arrived, inner[1:])], swap(far_own, group),
            lax.all_gather(wqkv, "dp", axis=1).reshape(width, 3 * wide),
            swap(own, 1), swap(out_grad, 1),
        )

    arrived, far_own, wqkv, own_b, grad_b = together(first_leg, arrived, far_own, own, wqkv)
    split = 128 * (lanes // 256)

    def second_leg(lower, upper, arrived, far_own, tail):
        lower = [swap(v, group) for v in lower]
        upper = [swap(v, m) for v, m in zip(upper, inner[1:])]
        wout = tail[:, tall:]
        wout = jnp.stack([wout, swap(wout, group)])
        grads = [swap(out_grad[:1], m) for m in inner[1:]]
        return lower, upper, [swap(v, 1) for v in arrived], swap(far_own, 1), wout, grads

    lower, upper = onward(arrived, far_own, width, CORES * wide, split)
    lower, upper, arrived_b, far_own_b, wout, grads_lo = together(
        second_leg, lower, upper, arrived, far_own, tail
    )
    mine = [own, *arrived, far_own, *lower, *upper]
    theirs = [own_b, *arrived_b, far_own_b, *[swap(v, 1) for v in lower + upper]]
    places = [(m, 0) for m in inner + across] + [(m, split) for m in across[1:]]
    order = tuple(places) + tuple((m + 1, lane) for m, lane in places)
    xs = mine + theirs
    near = [(own, own_b)] + list(zip(arrived, arrived_b))
    cosine, sine = rope_tables(total, wide)

    def attend(xs, wqkv, tail, wout):
        down = tail[:, :tall]
        return (
            attn_fwd(seat_arr, lengths, xs, wqkv, cosine, sine, order, []),
            down,
            swap(down, group),
            jnp.stack([wout] + [swap(wout, m) for m in inner[1:]]),
            [swap(out_grad[1:], m) for m in inner[1:]],
        )

    (qkv, ot, *sends, lse, r1), down_mine, down_far, wout, grads_hi = together(
        attend, xs, wqkv, tail, wout
    )

    def spread_out(send, wout, wqkv, *grads):
        return to_seats(send, same_core), swap(wout, 1), swap(wqkv, 1), [[swap(v, 1) for v in g] for g in grads]

    turns = list(range(1, spread)) + [0]
    o, wout_theirs, wqkv_theirs, grads_b = together(
        spread_out, sends[turns[0]], wout, wqkv, grads_lo, grads_hi
    )
    cotangents = [((out_grad,), (grad_b,))]
    cotangents += list(zip(zip(grads_lo, grads_hi), zip(*grads_b)))
    weights = (pair, down_mine, down_far, wout, wout_theirs)
    near_z, sets, near_f, z_parts = [], [], [], []
    for turn, at in enumerate(turns):

        def rows_of(o, near_z, send, weights):
            z = [swap(v, m) for v, m in near_z]
            after = [to_seats(v, same_core) for v in send]
            return (
                feed_forward(seat_arr, *near[at], *cotangents[at], *o, weights, at == 0), z, after
            )

        masks_z = [inner[j] for j in turns[turn - 1 : turn]] if turn else []
        out, z, after = together(
            lambda o, near_z, send, weights: rows_of(
                o, list(zip(near_z, masks_z)), send, weights
            ),
            (o, swap(o, 1)), near_z[-1:], [sends[j] for j in turns[turn + 1 : turn + 2]], weights,
        )
        z_parts += z
        o = after[0] if after else None
        za, zb_lo, zb_hi, fa, fb, *kept = out
        sets.append((*kept[:4], *cotangents[at][0], *cotangents[at][1]))
        if at:
            near_z.append(add_parts(za, [swap(zb_lo, 1), swap(zb_hi, 1)]))
            near_f.append((fa, fb))
    y, o_both, wout = kept[4:]
    dy, dyb, d_o = middle_back(
        y, [za] + z_parts, [swap(zb_lo, 1), swap(zb_hi, 1)], out_grad, wout, wide
    )

    near_fa = jnp.stack([v[0] for v in near_f])
    near_fb = jnp.stack([v[1] for v in near_f])

    def weight_grads(d_o, dyb, kept, near_fa, near_fb):
        return to_seats(d_o), ff_grads(
            seat_arr, kept, o_both, dyb, swap(dyb, 1), near_fa, swap(near_fb, 1),
            (depth, OUTER * group, held, 2 * slab), tall, spread,
        )

    d_o, (pair, down_mine, wout_own, *parcels) = together(
        weight_grads, d_o, dyb, sets, near_fa, near_fb
    )
    pair = lax.psum_scatter(
        pair.reshape(-1, 2 * slab), "dp", scatter_dimension=0, tiled=True
    ).reshape(OUTER * group, held, 2 * slab)

    def attend_back(parcels, d_o, xs):
        out = attn_bwd(
            seat_arr, lengths, xs, wqkv.shape, d_o, cosine, sine, qkv, ot, lse, r1, order,
            across + inner, [],
        )
        return out, [swap(v, m) for v, m in zip(parcels, inner[1:] + across[:1])]

    (e_mine, e_theirs, dwq), landed = together(attend_back, parcels[:spread], d_o, xs)

    def to_x(e_theirs, parcels, fb):
        both = back_to_x(seat_arr, e_mine, swap(e_theirs, 1), wqkv, wqkv_theirs)
        return both, [swap(v, m) for v, m in zip(parcels, across[1:])], swap(fb, 1)

    both, more, fb = together(to_x, e_theirs, parcels[spread:], fb)
    landed = landed + more
    far, close = both[:spread], both[spread:]

    def first_return(close, far, dwq, down_mine, wout_own, landed):
        got = [swap(close[j], inner[j]) for j in range(1, spread)] + [swap(far[0], across[0])]
        dwq = to_all(dwq.reshape(devices, held, 3 * wide))
        tail = plane_sums(level_arr, down_mine, wout_own, landed)
        output = y + fa.astype(F32) + fb.astype(F32)
        output = output + sum(v[:many].astype(F32) for v in landed[: spread - 1])
        return got, dwq, tail, output.astype(BF16).reshape(tokens.shape)

    got, dwq, tail, output = together(first_return, close, far, dwq, down_mine, wout_own, landed)

    def second_return(far, pair, dwq, tail):
        tail = [tail[0]] + [swap_depth(tail[k], k) for k in range(1, depth)]
        pair = to_seats(pair)
        return (
            [swap(far[j], across[j]) for j in range(1, spread)],
            pair_grads(
                pair.reshape(OUTER, group, held, 2 * slab), gate_weight, up_weight, gain2, depth,
                fan_rows,
            ),
            projection_grads(dwq.reshape(seats, depth, held, 3 * wide), qkv_weight, gain1, wide),
            tail_grads(tail, tall, fan_rows),
        )

    rest, (gate_grad, up_grad, gain2_grad), (qkv_grad, gain1_grad), (down_grad, out_grad_w) = together(
        second_return, far, pair, dwq, tail
    )
    got = [close[0]] + got + rest
    d_tokens, d_first = token_grads(seat_arr, tokens, dy, got, wide, [])
    gain1_grad, gain2_grad = gain1_grad[:, 0], gain2_grad[:, 0]
    return (
        output, d_tokens, d_first, gain1_grad, qkv_grad, out_grad_w, gain2_grad, gate_grad, up_grad,
        down_grad,
    )


def solution(mesh):
    rows = P(("seq", "dp"), None)
    acts = P("dp", "seq", None)
    gains = P(("seq", "dp"))
    return jax.shard_map(
        local,
        mesh=mesh,
        in_specs=(acts, acts, acts, P("dp"), gains, rows, rows, gains, rows, rows, rows),
        out_specs=(acts, acts, acts, gains, rows, rows, gains, rows, rows, rows),
        check_vma=False,
    )
```

```python
import functools

import jax
import jax.numpy as jnp
import numpy as np
from jax import lax
from jax.experimental import pallas as pl
from jax.experimental.pallas import tpu as pltpu
from jax.sharding import PartitionSpec as P

HEADS = 16
HEAD_DIM = 64
EPSILON = 1e-06
CORES = 2
OUTER = 2
BLOCK = 256
NEG = -1e30
F32 = jnp.float32
BF16 = jnp.bfloat16
MIB = 1024 * 1024
FREE = pl.CostEstimate(flops=0, bytes_accessed=0, transcendentals=0)


def lasting(us):
    return pl.CostEstimate(flops=0, bytes_accessed=int(us * 3.69e6), transcendentals=0)


def vmem(mib, scale=1):
    return pltpu.CompilerParams(vmem_limit_bytes=int(min(60, mib * max(scale, 1))) * MIB)


def held_in_hbm(*arrays):
    return [pltpu.with_memory_space_constraint(a, pltpu.HBM) for a in arrays]


class Copies:
    def __init__(self, sems):
        self.sems, self.used, self.waiting = sems, 0, {}

    def start(self, name, src, dst):
        copy = pltpu.make_async_copy(src, dst, self.sems.at[self.used])
        self.used += 1
        copy.start()
        self.waiting.setdefault(name, []).append(copy)

    def wait(self, *names):
        for name in names or list(self.waiting):
            for copy in self.waiting.pop(name, []):
                copy.wait()


def corner(a):
    block = (1,) * (a.ndim - 2) + (min(16, a.shape[-2]), min(128, a.shape[-1]))
    return pl.BlockSpec(block, lambda *_: (0,) * a.ndim)


def dot_nn(a, b):
    return lax.dot_general(a, b, (((1,), (0,)), ((), ())), preferred_element_type=F32)


def dot_nt(a, b):
    return lax.dot_general(a, b, (((1,), (1,)), ((), ())), preferred_element_type=F32)


def dot_tn(a, b):
    return lax.dot_general(a, b, (((0,), (0,)), ((), ())), preferred_element_type=F32)


def turned(u):
    half = HEAD_DIM // 2
    width = u.shape[1]
    if width % 128:
        parts = []
        for h in range(width // HEAD_DIM):
            lo = h * HEAD_DIM
            parts += [u[:, lo + half : lo + HEAD_DIM], u[:, lo : lo + half]]
        return jnp.concatenate(parts, axis=1)
    lane = lax.broadcasted_iota(jnp.int32, u.shape, 1) % HEAD_DIM
    return jnp.where(lane < half, pltpu.roll(u, width - half, 1), pltpu.roll(u, half, 1))


def head_mask(shape, h):
    lane = lax.broadcasted_iota(jnp.int32, shape, 1)
    return (lane >= h * HEAD_DIM) & (lane < (h + 1) * HEAD_DIM)


def own_head(u, h):
    if u.shape[1] == HEAD_DIM:
        return u
    return jnp.where(head_mask(u.shape, h), u, jnp.zeros_like(u))


def join_heads(parts):
    out = parts[0]
    for h in range(1, len(parts)):
        out = jnp.where(head_mask(out.shape, h), parts[h], out)
    return out


def fill_rows(seat, refs, order, dest):
    rows = refs[0].shape[1]
    for ref, (m, lane) in zip(refs, order):
        at = pl.multiple_of((seat ^ m) * rows, rows)
        dest[pl.ds(at, rows), lane : lane + ref.shape[2]] = ref[0]


def attn_fwd_kernel(
    order, seat_ref, len_ref, w_ref, cos_ref, sin_ref, *refs,
):
    xs = refs[: len(order)]
    spread = len(refs) - len(order) - 6
    qkv_out, ot_out = refs[len(order) : len(order) + 2]
    sends = refs[len(order) + 2 : len(order) + 2 + spread]
    lse_out, r1_out, xbuf, vt = refs[-4:]
    slot = pl.program_id(0)
    seat = seat_ref[0]
    length = len_ref[slot]
    total = xbuf.shape[0]
    width = w_ref.shape[0]
    wide = w_ref.shape[1] // 3
    heads = wide // HEAD_DIM
    blocks = total // BLOCK
    fill_rows(seat, xs, order, xbuf)
    for b in range(blocks):
        at = slice(b * BLOCK, (b + 1) * BLOCK)
        x = xbuf[at, :width]
        xf = x.astype(F32)
        r1 = lax.rsqrt(jnp.mean(xf * xf, axis=1, keepdims=True) + EPSILON)
        qkv = dot_nn(x, w_ref[...]) * r1
        cosine = cos_ref[at, :]
        sine = sin_ref[at, :]
        q = qkv[:, :wide]
        k = qkv[:, wide : 2 * wide]
        v = qkv[:, 2 * wide :]
        q = (q * cosine + turned(q) * sine) * (HEAD_DIM**-0.5)
        k = k * cosine + turned(k) * sine
        first = xbuf[at, width : width + wide]
        second = xbuf[at, width + wide :]
        v1 = jnp.where(seat % CORES == 0, first, second).astype(F32)
        vm = 0.5 * v + 0.5 * v1
        qkv_out[0, at, :wide] = q.astype(BF16)
        qkv_out[0, at, wide : 2 * wide] = k.astype(BF16)
        qkv_out[0, at, 2 * wide :] = vm.astype(BF16)
        vt[:, at] = vm.T.astype(BF16)
        r1_out[0, at, :] = jnp.broadcast_to(r1, (BLOCK, r1_out.shape[2]))
    for b in range(blocks):
        at = slice(b * BLOCK, (b + 1) * BLOCK)
        count = (b + 1) * BLOCK
        q = qkv_out[0, at, :wide]
        query = b * BLOCK + lax.broadcasted_iota(jnp.int32, (1, BLOCK), 1)
        last = jnp.minimum(query, length - 1)
        key = lax.broadcasted_iota(jnp.int32, (count, BLOCK), 0)
        allowed = key <= last
        ots = []
        for h in range(heads):
            k = own_head(qkv_out[0, :count, wide : 2 * wide], h)
            scores = jnp.where(allowed, dot_nt(k, q), NEG)
            top = jnp.max(scores, axis=0, keepdims=True)
            weights = jnp.exp(scores - top)
            total_w = jnp.sum(weights, axis=0, keepdims=True)
            ot = dot_nn(vt[h * HEAD_DIM : (h + 1) * HEAD_DIM, :count], weights.astype(BF16))
            ots.append(ot / total_w)
            lse_out[0, h : h + 1, at] = top + jnp.log(total_w)
        ot = jnp.concatenate(ots, axis=0)
        ot_out[0, :, at] = ot
        o = ot.T.astype(BF16)
        for x in range(spread):
            sends[x ^ (b % spread)][(b // spread) * spread + x, 0] = o


def chunk_specs(xs, order, lanes):
    return [
        pl.BlockSpec((1, x.shape[1], min(x.shape[2], lanes - lane)), lambda i: (i, 0, 0))
        for x, (_, lane) in zip(xs, order)
    ]


def attn_fwd(seat, lengths, xs, w, cosine, sine, order, ready):
    micro, rows, lanes = xs[0].shape
    width = w.shape[0]
    total = cosine.shape[0]
    spread = total // rows // (OUTER * CORES)
    wide = w.shape[1] // 3
    heads = wide // HEAD_DIM
    smem = pl.BlockSpec(memory_space=pltpu.SMEM)
    whole = lambda a: pl.BlockSpec(a.shape, lambda i: (0,) * a.ndim)
    pairs = total * total // 2 * micro * wide
    return pl.pallas_call(
        functools.partial(attn_fwd_kernel, order),
        grid=(micro,),
        in_specs=[smem, smem, whole(w), whole(cosine), whole(sine)]
        + chunk_specs(xs, order, lanes)
        + [corner(a) for a in ready],
        out_specs=[
            pl.BlockSpec((1, total, 3 * wide), lambda i: (i, 0, 0)),
            pl.BlockSpec((1, wide, total), lambda i: (i, 0, 0)),
        ]
        + [pl.BlockSpec((OUTER * spread, 1, BLOCK, wide), lambda i: (0, i, 0, 0))] * spread
        + [
            pl.BlockSpec((1, heads, total), lambda i: (i, 0, 0)),
            pl.BlockSpec((1, total, 128), lambda i: (i, 0, 0)),
        ],
        out_shape=[
            pltpu.HBM((micro, total, 3 * wide), BF16),
            pltpu.HBM((micro, wide, total), F32),
        ]
        + [pltpu.HBM((OUTER * spread, micro, BLOCK, wide), BF16)] * spread
        + [
            pltpu.HBM((micro, heads, total), F32),
            pltpu.HBM((micro, total, 128), F32),
        ],
        scratch_shapes=[pltpu.VMEM((total, lanes), BF16), pltpu.VMEM((wide, total), BF16)],
        compiler_params=vmem(30, total / 1024),
        cost_estimate=lasting(20),
        name="attn_fwd",
    )(seat, lengths, *held_in_hbm(w, cosine, sine, *xs), *ready)


def attn_bwd_kernel(
    order, sent, seat_ref, len_ref, do_ref, cos_ref, sin_ref, qkv_ref, ot_ref, lse_ref, r1_ref,
    *refs,
):
    xs = refs[: len(order)]
    outs = refs[-6 - CORES : -6]
    dw_out, xbuf, dobuf, dqt, ebuf, dw = refs[-6:]
    slot = pl.program_id(0)
    seat = seat_ref[0]
    rows = do_ref.shape[2]
    length = len_ref[slot]
    total = xbuf.shape[0]
    wide = do_ref.shape[3]
    heads = wide // HEAD_DIM
    blocks = total // BLOCK
    fill_rows(seat, xs, order, xbuf)
    for j in range(do_ref.shape[0]):
        dobuf[j * rows : (j + 1) * rows, :] = do_ref[j, 0]
    dot_t = dobuf[...].astype(F32).T
    deltas = []
    for h in range(heads):
        part = slice(h * HEAD_DIM, (h + 1) * HEAD_DIM)
        deltas.append(jnp.sum(dot_t[part, :] * ot_ref[0, part, :], axis=0, keepdims=True))
    dqt[...] = jnp.zeros_like(dqt)
    for b in range(blocks):
        at = slice(b * BLOCK, (b + 1) * BLOCK)
        later = slice(b * BLOCK, total)
        count = total - b * BLOCK
        k = qkv_ref[0, at, wide : 2 * wide]
        v = qkv_ref[0, at, 2 * wide :]
        kt = k.astype(F32).T.astype(BF16)
        q = qkv_ref[0, later, :wide]
        d_o = dobuf[later, :]
        query = b * BLOCK + lax.broadcasted_iota(jnp.int32, (1, count), 1)
        last = jnp.minimum(query, length - 1)
        key = b * BLOCK + lax.broadcasted_iota(jnp.int32, (BLOCK, count), 0)
        allowed = key <= last
        dks, dvs = [], []
        for h in range(heads):
            part = slice(h * HEAD_DIM, (h + 1) * HEAD_DIM)
            scores = jnp.where(allowed, dot_nt(own_head(k, h), q), NEG)
            weights = jnp.exp(scores - lse_ref[0, h : h + 1, later])
            d_weights = dot_nt(own_head(v, h), d_o)
            ds = (weights * (d_weights - deltas[h][:, later])).astype(BF16)
            dvs.append(dot_nn(weights.astype(BF16), d_o))
            dks.append(dot_nn(ds, q))
            dqt[part, later] += dot_nn(kt[part, :], ds)
        cosine = cos_ref[at, :]
        sine = sin_ref[at, :]
        r1 = r1_ref[0, at, 0:1]
        dk = join_heads(dks)
        dk = dk * cosine - turned(dk) * sine
        dv = 0.5 * join_heads(dvs)
        ebuf[at, 3 * wide :] = dv.astype(BF16)
        ebuf[at, wide : 2 * wide] = (dk * r1).astype(BF16)
        ebuf[at, 2 * wide : 3 * wide] = (dv * r1).astype(BF16)
    for b in range(blocks):
        at = slice(b * BLOCK, (b + 1) * BLOCK)
        dq = dqt[:, at].T * (HEAD_DIM**-0.5)
        dq = dq * cos_ref[at, :] - turned(dq) * sin_ref[at, :]
        ebuf[at, :wide] = (dq * r1_ref[0, at, 0:1]).astype(BF16)
    for low, out in enumerate(outs):
        for j, m in enumerate(sent):
            at = pl.multiple_of((seat ^ m ^ low) * rows, rows)
            out[j, 0] = ebuf[pl.ds(at, rows), :]
    grown = dot_tn(xbuf[...], ebuf[:, : 3 * wide])

    @pl.when(slot == 0)
    def _():
        dw[...] = grown

    @pl.when(slot > 0)
    def _():
        dw[...] += grown

    @pl.when(slot == pl.num_programs(0) - 1)
    def _():
        dw_out[...] = dw[...].astype(BF16)


def attn_bwd(seat, lengths, xs, wshape, d_o, cosine, sine, qkv, ot, lse, r1, order, sent, ready):
    micro, rows = xs[0].shape[:2]
    width = wshape[0]
    total = cosine.shape[0]
    wide = wshape[1] // 3
    heads = wide // HEAD_DIM
    smem = pl.BlockSpec(memory_space=pltpu.SMEM)
    whole = lambda a: pl.BlockSpec(a.shape, lambda i: (0,) * a.ndim)
    vspec = pl.BlockSpec((d_o.shape[0], 1, rows, wide), lambda i: (0, i, 0, 0))
    zshapes = [pltpu.HBM((len(sent), micro, rows, 4 * wide), BF16)] * CORES
    pairs = total * total // 2 * micro * wide
    return pl.pallas_call(
        functools.partial(attn_bwd_kernel, order, sent),
        grid=(micro,),
        in_specs=[
            smem, smem, vspec, whole(cosine), whole(sine),
            pl.BlockSpec((1, total, 3 * wide), lambda i: (i, 0, 0)),
            pl.BlockSpec((1, wide, total), lambda i: (i, 0, 0)),
            pl.BlockSpec((1, heads, total), lambda i: (i, 0, 0)),
            pl.BlockSpec((1, total, 128), lambda i: (i, 0, 0)),
        ]
        + chunk_specs(xs, order, width)
        + [corner(a) for a in ready],
        out_specs=[
            pl.BlockSpec((len(sent), 1, rows, 4 * wide), lambda i: (0, i, 0, 0))
        ]
        * CORES
        + [pl.BlockSpec(wshape, lambda i: (0, 0))],
        out_shape=zshapes + [pltpu.HBM(wshape, BF16)],
        scratch_shapes=[
            pltpu.VMEM((total, width), BF16),
            pltpu.VMEM((total, wide), BF16),
            pltpu.VMEM((wide, total), F32),
            pltpu.VMEM((total, 4 * wide), BF16),
            pltpu.VMEM(wshape, F32),
        ],
        compiler_params=vmem(40, total / 1024),
        cost_estimate=lasting(20),
        name="attn_bwd",
    )(seat, lengths, *held_in_hbm(d_o, cosine, sine, qkv, ot, lse, r1, *xs), *ready)


def ff_kernel(
    own, parts, seat_ref, xa, xb, oa, ob, pair, down_mine, down_far, wout_mine, wout_theirs, *refs,
):
    cotangents, refs = (refs[:parts], refs[parts : 2 * parts]), refs[2 * parts :]
    za, zb_lo, zb_hi, fa, fb, hn_out, hid_out, dgate_out, dup_out = refs[:9]
    refs = refs[9:]
    if own:
        y_out, o_out, wout_out = refs[:3]
        refs = refs[3:]
    x_buf, g_buf, oa_buf, ob_buf, wout, wg, wu, wd, z_buf, f_buf, hn, hid, dgate, dup, y_buf, o_buf, sems = refs
    seat = seat_ref[0]
    core = seat % CORES
    micro, rows = xa.shape[:2]
    width = wout.shape[0]
    many = micro * rows
    depth, outer, group, held, slab2 = pair.shape
    slab = slab2 // 2
    spread = group // CORES
    tall = down_mine.shape[1]
    half = seat // group
    copies = Copies(sems)

    for low in range(CORES):
        there = pl.ds(pl.multiple_of((core ^ low) * rows, rows), rows)
        copies.start("o", oa.at[:, :, there, :], oa_buf.at[low])
        copies.start("o", ob.at[:, :, there, :], ob_buf.at[low])
    for rc, ref in enumerate((wout_mine, wout_theirs)):
        for rx in range(spread):
            for ry in range(outer):
                other = seat ^ (ry * group + rx * CORES + rc)
                for d in range(depth):
                    to = pl.ds(pl.multiple_of((other * depth + d) * held, held), held)
                    copies.start("wout", ref.at[rx, ry, d], wout.at[to, :])
    copies.start("x", xa.at[:, :, pl.ds(0, width)], x_buf.at[0])
    copies.start("x", xb.at[:, :, pl.ds(0, width)], x_buf.at[1])
    for part, dest in ((0, wg), (1, wu)):
        for y in range(outer):
            for q in range(group):
                for d in range(depth):
                    to = ((y * group + q) * depth + d) * held
                    copies.start(
                        "wg" if part == 0 else "wu",
                        pair.at[d, y, q, :, pl.ds(part * slab, slab)],
                        dest.at[pl.ds(to, held), :],
                    )
    for low, some in enumerate(cotangents):
        base = 0
        for ref in some:
            copies.start("g", ref, g_buf.at[low, pl.ds(base, ref.shape[0])])
            base += ref.shape[0]
    for ry, ref in enumerate((down_mine, down_far)):
        for d in range(depth):
            to = pl.ds(pl.multiple_of(((half ^ ry) * depth + d) * tall, tall), tall)
            copies.start("wd", ref.at[d], wd.at[to, :])

    copies.wait("o")
    for low in range(CORES):
        for j in range(oa_buf.shape[1]):
            a = oa_buf[low, j].reshape(many, oa_buf.shape[4])
            b = ob_buf[low, j].reshape(many, oa_buf.shape[4])
            wide = a.shape[1]
            here = slice(low * many, (low + 1) * many)
            o_buf[here, (2 * j) * wide : (2 * j + 1) * wide] = jnp.where(core == 0, a, b)
            o_buf[here, (2 * j + 1) * wide : (2 * j + 2) * wide] = jnp.where(core == 0, b, a)
    copies.wait("wout", "x")
    if own:
        copies.start("out", wout, wout_out)
        copies.start("out", o_buf, o_out)
    y = x_buf[...].reshape(2 * many, width).astype(F32) + dot_nn(o_buf[...], wout[...])
    r2 = lax.rsqrt(jnp.mean(y * y, axis=1, keepdims=True) + EPSILON)
    hn[...] = (y * r2).astype(BF16)
    if own:
        y_buf[...] = y[:many]
        copies.start("out", y_buf, y_out)
    copies.start("out", hn, hn_out)
    copies.wait("wg")
    gate = dot_nn(hn[...], wg[...])
    copies.wait("wu")
    up = dot_nn(hn[...], wu[...])
    sigma = jax.nn.sigmoid(gate)
    act = gate * sigma
    hid[...] = (act * up).astype(BF16)
    copies.start("out", hid, hid_out)
    copies.wait("g", "wd")
    dhid = dot_nt(g_buf[...].reshape(2 * many, width), wd[...])
    dgate[...] = (dhid * up * (sigma + act * (1.0 - sigma))).astype(BF16)
    dup[...] = (dhid * act).astype(BF16)
    copies.start("out", dgate, dgate_out)
    copies.start("out", dup, dup_out)
    z_buf[...] = (dot_nt(dgate[...], wg[...]) + dot_nt(dup[...], wu[...])).astype(BF16)
    copies.start("out", z_buf.at[pl.ds(0, many)], za)
    copies.start("out", z_buf.at[pl.ds(many, many // 2)], zb_lo)
    copies.start("out", z_buf.at[pl.ds(many + many // 2, many // 2)], zb_hi)
    f_buf[...] = dot_nn(hid[...], wd[...]).astype(BF16)
    copies.start("out", f_buf.at[pl.ds(0, many)], fa)
    copies.start("out", f_buf.at[pl.ds(many, many)], fb)
    copies.wait()


def feed_forward(seat, xa, xb, ga, gb, oa, ob, weights, own):
    pair, down_mine, down_far, wout_mine, wout_theirs = weights
    micro, rows = xa.shape[:2]
    width = ga[0].shape[2]
    many = micro * rows
    depth, outer, group, held, slab2 = pair.shape
    fan = slab2 // 2
    wide = oa.shape[3]
    outs = [(many, width), (many // 2, width), (many // 2, width), (many, width), (many, width)]
    outs = [pltpu.HBM(s, BF16) for s in outs + [(2 * many, width)] + [(2 * many, fan)] * 3]
    if own:
        outs += [
            pltpu.HBM((many, width), F32), pltpu.HBM((2 * many, width), BF16),
            pltpu.HBM((width, width), BF16),
        ]
    o_shape = (CORES, oa.shape[0], micro, rows, wide)
    scratch = [
        ((2, micro, rows, width), BF16), ((2, micro, rows, width), BF16), (o_shape, BF16),
        (o_shape, BF16), ((width, width), BF16), ((width, fan), BF16), ((width, fan), BF16),
        ((fan, width), BF16), ((2 * many, width), BF16), ((2 * many, width), BF16),
        ((2 * many, width), BF16), ((2 * many, fan), BF16), ((2 * many, fan), BF16),
        ((2 * many, fan), BF16), ((many, width), F32), ((2 * many, width), BF16),
    ]
    many_copies = 32 + 4 * outer * group * depth
    anywhere = pl.BlockSpec(memory_space=pl.ANY)
    return pl.pallas_call(
        functools.partial(ff_kernel, own, len(ga)),
        grid=(1,),
        in_specs=[pl.BlockSpec(memory_space=pltpu.SMEM)]
        + [anywhere] * (9 + 2 * len(ga)),
        out_specs=[anywhere] * len(outs),
        out_shape=outs,
        scratch_shapes=[pltpu.VMEM(s, t) for s, t in scratch]
        + [pltpu.SemaphoreType.DMA((many_copies,))],
        compiler_params=vmem(56),
        cost_estimate=lasting(16),
        name="ff_own" if own else "ff_near",
    )(seat, *held_in_hbm(xa, xb, oa, ob, *weights, *ga, *gb))


def ff_grads_kernel(sizes, group, spread, seat_ref, *refs):
    sets = []
    for size in sizes:
        sets.append(refs[:size])
        refs = refs[size:]
    o_ref, dyb_ref, dyb_theirs, fa, fb = refs[:5]
    refs = refs[5:]
    pair_out, down_mine, wout_own = refs[:3]
    parcels = refs[3 : 2 + 2 * spread]
    dwg, dwu, dwd, dwo = refs[2 + 2 * spread :]
    seat = seat_ref[0]
    outer = seat // group
    core = seat % CORES
    chip = seat // CORES
    depth, blocks, held, slab2 = pair_out.shape
    slab = slab2 // 2
    tall = down_mine.shape[1]
    many, width = dyb_ref.shape
    for n, (hn, hid, dgate, dup, *gs) in enumerate(sets):
        g = jnp.concatenate([r[...].reshape(-1, width) for r in gs], axis=0)
        new = dot_tn(hn[...], dgate[...]), dot_tn(hn[...], dup[...]), dot_tn(hid[...], g)
        for scratch, value in zip((dwg, dwu, dwd), new):
            if n == 0:
                scratch[...] = value
            else:
                scratch[...] += value
    for k in range(blocks):
        for d in range(depth):
            at = slice((k * depth + d) * held, (k * depth + d + 1) * held)
            pair_out[d, k, :, :slab] = dwg[at, :].astype(BF16)
            pair_out[d, k, :, slab:] = dwu[at, :].astype(BF16)
    far = parcels[spread - 1]
    for d in range(depth):
        pieces = []
        for k in range(OUTER):
            at = slice((k * depth + d) * tall, (k * depth + d + 1) * tall)
            pieces.append(dwd[at, :].astype(BF16))
        down_mine[d] = jnp.where(outer == 0, pieces[0], pieces[1])
        far[d * tall : (d + 1) * tall, :] = jnp.where(outer == 0, pieces[1], pieces[0])
    dyb = jnp.concatenate([dyb_ref[...], dyb_theirs[...]], axis=0)
    rows = depth * held
    for c in range(2 * spread):
        a = o_ref[:, (2 * c) * rows : (2 * c + 1) * rows]
        b = o_ref[:, (2 * c + 1) * rows : (2 * c + 2) * rows]
        dwo[c * rows : (c + 1) * rows, :] = dot_tn(jnp.where(core == 0, a, b), dyb)
    for j in range(2 * spread):
        at = pl.ds(pl.multiple_of((chip ^ j) * rows, rows), rows)
        value = dwo[at, :].astype(BF16)
        if j == 0:
            wout_own[...] = value
        else:
            out = parcels[j - 1]
            out[out.shape[0] - rows :, :] = value
    for j in range(spread - 1):
        parcels[j][:many, :] = (fa[j].astype(F32) + fb[j].astype(F32)).astype(BF16)


def ff_grads(seat, sets, o_both, dyb, dyb_theirs, fa, fb, pair_shape, tall, spread):
    def fixed(shape):
        return pl.BlockSpec(shape, lambda i: (0,) * len(shape), pipeline_mode=pl.Buffered(1))

    args = [a for arrays in sets for a in arrays]
    last = [o_both, dyb, dyb_theirs, fa, fb]
    args += last
    specs = [fixed(a.shape) for a in args]
    depth, _, held, slab2 = pair_shape
    many, width = dyb.shape
    fan = slab2 // 2
    rows = depth * held
    parcels = [(many + rows, width)] * (spread - 1) + [(depth * tall + rows, width)]
    parcels += [(rows, width)] * (spread - 1)
    outs = [pair_shape, (depth, tall, width), (rows, width)] + parcels
    return pl.pallas_call(
        functools.partial(ff_grads_kernel, [len(s) for s in sets], spread * CORES, spread),
        grid=(1,),
        in_specs=[pl.BlockSpec(memory_space=pltpu.SMEM)] + specs,
        out_specs=[fixed(s) for s in outs],
        out_shape=[pltpu.HBM(s, BF16) for s in outs],
        scratch_shapes=[
            pltpu.VMEM((width, fan), F32), pltpu.VMEM((width, fan), F32),
            pltpu.VMEM((fan, width), F32), pltpu.VMEM((2 * spread * rows, width), F32),
        ],
        compiler_params=vmem(56),
        cost_estimate=lasting(14),
        name="ff_grads",
    )(seat, *args)


def pieces_at(values, index):
    step = 1
    while step < len(values):
        flip = (index // step) % 2 == 1
        values = [jnp.where(flip, values[k ^ step], values[k]) for k in range(len(values))]
        step *= 2
    return values


def payloads(seat, tokens, first_values, spread, wide):
    micro, rows, width = tokens.shape
    lanes = CORES * wide

    def kernel(seat_ref, x_ref, *refs):
        firsts, outs = refs[: 2 * spread], refs[2 * spread :]
        for out in outs:
            out[0, :, :width] = x_ref[0]
        for j in range(spread):
            outs[1][0, :, width + j * lanes : width + (j + 1) * lanes] = firsts[spread + j][0]
            outs[j and 1 + j][0, :, width:] = firsts[j][0]

    def part(j):
        return pl.BlockSpec((1, rows, lanes), lambda i, s: (i, 0, (s[0] // CORES) ^ j))

    sizes = [width + lanes, width + spread * lanes] + [width + lanes] * (spread - 1)
    return pl.pallas_call(
        kernel,
        grid_spec=pltpu.PrefetchScalarGridSpec(
            num_scalar_prefetch=1,
            grid=(micro,),
            in_specs=[pl.BlockSpec((1, rows, width), lambda i, s: (i, 0, 0))]
            + [part(j) for j in range(2 * spread)],
            out_specs=[pl.BlockSpec((1, rows, n), lambda i, s: (i, 0, 0)) for n in sizes],
        ),
        out_shape=[pltpu.HBM((micro, rows, n), BF16) for n in sizes],
        cost_estimate=lasting(4),
        name="payloads",
    )(seat, *held_in_hbm(tokens, *([first_values] * (2 * spread))))


def middle_back(y, parts, pieces, grad, wout, wide):
    micro, rows, width = grad.shape
    seats = width // wide
    many = micro * rows

    def kernel(y_ref, g_ref, w_ref, *refs):
        zs = refs[: len(parts)]
        z = jnp.concatenate([r[...] for r in refs[len(parts) : len(parts) + len(pieces)]], axis=0)
        dy_out, dyb_out, do_out = refs[len(parts) + len(pieces) :]
        z = z.astype(F32)
        for ref in zs:
            z = z + ref[...].astype(F32)
        y = y_ref[...]
        r2 = lax.rsqrt(jnp.mean(y * y, axis=1, keepdims=True) + EPSILON)
        inner = jnp.mean(z * y, axis=1, keepdims=True)
        g = g_ref[...].reshape(many, width).astype(F32)
        dy = g + r2 * z - y * (r2 * r2 * r2 * inner)
        dy_out[...] = dy
        dyb = dy.astype(BF16)
        dyb_out[...] = dyb
        d_o = dot_nt(dyb, w_ref[...]).astype(BF16)
        for s in range(seats):
            do_out[s] = d_o[:, s * wide : (s + 1) * wide].reshape(micro, rows, wide)

    def fixed(shape):
        return pl.BlockSpec(shape, lambda i: (0,) * len(shape), pipeline_mode=pl.Buffered(1))

    given = held_in_hbm(y, grad, wout, parts[0]) + [*parts[1:], *pieces]
    return pl.pallas_call(
        kernel,
        grid=(1,),
        in_specs=[fixed(a.shape) for a in given],
        out_specs=[
            fixed((many, width)), fixed((many, width)), fixed((seats, micro, rows, wide)),
        ],
        out_shape=[
            pltpu.HBM((many, width), F32),
            pltpu.HBM((many, width), BF16),
            pltpu.HBM((seats, micro, rows, wide), BF16),
        ],
        compiler_params=vmem(24),
        cost_estimate=FREE,
        name="middle_back",
    )(*given)


def back_to_x(seat, mine, theirs, w_mine, w_theirs):
    count, micro, rows, lanes = mine.shape
    width = w_mine.shape[0]
    wide = lanes // 4
    many = micro * rows

    def kernel(seat_ref, a_ref, b_ref, wa, wb, *refs):
        outs = refs[:count]
        buf, sems = refs[-2:]
        core = seat_ref[0] % CORES
        copies = Copies(sems)
        for j in range(count):
            a = a_ref[j].reshape(many, lanes)
            b = b_ref[j].reshape(many, lanes)
            z = dot_nt(a[:, : 3 * wide], wa[...]) + dot_nt(b[:, : 3 * wide], wb[...])
            buf[j, :, :, :width] = z.astype(BF16).reshape(micro, rows, width)
            first = jnp.where(core == 0, a[:, 3 * wide :], b[:, 3 * wide :])
            second = jnp.where(core == 0, b[:, 3 * wide :], a[:, 3 * wide :])
            buf[j, :, :, width : width + wide] = first.reshape(micro, rows, wide)
            buf[j, :, :, width + wide :] = second.reshape(micro, rows, wide)
            copies.start("out", buf.at[j], outs[j])
        copies.wait()

    anywhere = pl.BlockSpec(memory_space=pl.ANY)
    out = pltpu.HBM((micro, rows, width + CORES * wide), BF16)
    fixed = lambda shape: pl.BlockSpec(
        shape, lambda i: (0,) * len(shape), pipeline_mode=pl.Buffered(1)
    )
    given = held_in_hbm(mine) + [theirs, w_mine, w_theirs]
    return pl.pallas_call(
        kernel,
        grid=(1,),
        in_specs=[pl.BlockSpec(memory_space=pltpu.SMEM)] + [fixed(a.shape) for a in given],
        out_specs=[anywhere] * count,
        out_shape=[out] * count,
        scratch_shapes=[
            pltpu.VMEM((count, micro, rows, width + CORES * wide), BF16),
            pltpu.SemaphoreType.DMA((count,)),
        ],
        compiler_params=vmem(32),
        cost_estimate=lasting(5),
        name="back_to_x",
    )(seat, *given)


def plane_sums(level, down, wout, parcels):
    depth, tall, width = down.shape
    held = wout.shape[0] // depth
    spread = (len(parcels) + 1) // 2

    def kernel(level_ref, down_ref, wout_ref, *refs):
        parts, outs = refs[: len(parcels)], refs[len(parcels) :]
        far = parts[spread - 1]
        for k, out in enumerate(outs):
            d = level_ref[0] ^ k
            at = pl.ds(pl.multiple_of(d * tall, tall), tall)
            out[:tall, :] = (down_ref[d].astype(F32) + far[at, :].astype(F32)).astype(BF16)
            at = pl.ds(pl.multiple_of(d * held, held), held)
            total = wout_ref[at, :].astype(F32)
            for part in parts:
                base = part.shape[0] - depth * held
                at = pl.ds(pl.multiple_of(base + d * held, held), held)
                total = total + part[at, :].astype(F32)
            out[tall:, :] = total.astype(BF16)

    fixed = lambda shape: pl.BlockSpec(
        shape, lambda i: (0,) * len(shape), pipeline_mode=pl.Buffered(1)
    )
    given = [down, wout, *parcels]
    shape = (tall + held, width)
    return pl.pallas_call(
        kernel,
        grid=(1,),
        in_specs=[pl.BlockSpec(memory_space=pltpu.SMEM)] + [fixed(a.shape) for a in given],
        out_specs=[fixed(shape)] * depth,
        out_shape=[pltpu.HBM(shape, BF16)] * depth,
        compiler_params=vmem(24),
        cost_estimate=FREE,
        name="plane_sums",
    )(level, *given)


def add_parts(mine, theirs):
    def kernel(a_ref, *refs):
        b = jnp.concatenate([r[...] for r in refs[:-1]], axis=0)
        refs[-1][...] = (a_ref[...].astype(F32) + b.astype(F32)).astype(BF16)

    fixed = lambda shape: pl.BlockSpec(
        shape, lambda i: (0,) * len(shape), pipeline_mode=pl.Buffered(1)
    )
    return pl.pallas_call(
        kernel,
        grid=(1,),
        in_specs=[fixed(a.shape) for a in (mine, *theirs)],
        out_specs=fixed(mine.shape),
        out_shape=pltpu.HBM(mine.shape, BF16),
        compiler_params=vmem(16),
        cost_estimate=FREE,
        name="add_parts",
    )(*held_in_hbm(mine), *theirs)


def tail_grads(parts, tall, short):
    rows, width = parts[0].shape

    def kernel(*refs):
        *ins, down_out, wout_out = refs
        total = ins[0][...].astype(F32)
        for ref in ins[1:]:
            total = total + ref[...].astype(F32)
        down_out[...] = total[:short, :]
        wout_out[...] = total[tall:, :]

    return pl.pallas_call(
        kernel,
        out_shape=[pltpu.HBM((short, width), F32), pltpu.HBM((rows - tall, width), F32)],
        cost_estimate=FREE,
        name="tail_grads",
    )(*parts)


def fence(value, ready):
    def kernel(*_):
        pass

    return pl.pallas_call(
        kernel,
        grid=(1,),
        in_specs=[pl.BlockSpec(memory_space=pl.ANY)] + [corner(a) for a in ready],
        out_specs=pl.BlockSpec(memory_space=pl.ANY),
        out_shape=pltpu.HBM(value.shape, value.dtype),
        input_output_aliases={0: 0},
        cost_estimate=FREE,
        name="fence",
    )(value, *ready)


def token_sums(seat, dy, got, chips, wide):
    micro, rows, lanes = got[0].shape
    pair = CORES * wide
    width = lanes - pair
    many = len(got)

    def kernel(seat_ref, *refs):
        parts, (dx_out, dv_out) = refs[:many], refs[many:]
        z = parts[0][0, :, :width].astype(F32)
        for ref in parts[1:]:
            z = z + ref[0, :, :width].astype(F32)
        dx_out[0] = z
        chip = seat_ref[0] // CORES
        for ref, j in zip(parts, chips):
            at = pl.multiple_of((chip ^ j) * pair, pair)
            dv_out[0, :, pl.ds(at, pair)] = ref[0, :, width:].astype(F32)

    spec = lambda n: pl.BlockSpec((1, rows, n), lambda i: (i, 0, 0))
    return pl.pallas_call(
        kernel,
        grid=(micro,),
        in_specs=[pl.BlockSpec(memory_space=pltpu.SMEM)] + [spec(lanes)] * many,
        out_specs=[spec(width)] * 2,
        out_shape=[pltpu.HBM((micro, rows, width), F32)] * 2,
        cost_estimate=FREE,
        name="token_sums",
    )(seat, *got)


def token_grads(seat, tokens, dy, dx, dv, rest, chips, wide):
    micro, rows, width = tokens.shape
    pair = CORES * wide
    many = len(rest)

    def kernel(seat_ref, x_ref, dy_ref, dx_ref, *refs):
        parts = refs[:many]
        dx_out, dv_out, buf, sems = refs[many + 1 :]
        chip = seat_ref[0] // CORES
        copies = Copies(sems)
        for k, j in enumerate(chips):
            buf[k] = parts[k][:, :, width:].astype(F32)
            at = pl.multiple_of((chip ^ j) * pair, pair)
            copies.start("dv", buf.at[k], dv_out.at[:, :, pl.ds(at, pair)])
        z = dx_ref[...]
        for ref in parts:
            z = z + ref[:, :, :width].astype(F32)
        x = x_ref[...].astype(F32)
        inv = lax.rsqrt(jnp.mean(x * x, axis=2, keepdims=True) + EPSILON)
        inner = jnp.mean(z * x, axis=2, keepdims=True)
        dx_out[...] = dy_ref[...].reshape(micro, rows, width) + z - x * (inv * inv * inner)
        copies.wait()

    def fixed(shape):
        return pl.BlockSpec(shape, lambda i: (0,) * len(shape), pipeline_mode=pl.Buffered(1))

    anywhere = pl.BlockSpec(memory_space=pl.ANY)
    given = [tokens, dy, dx, *rest]
    return pl.pallas_call(
        kernel,
        grid=(1,),
        in_specs=[pl.BlockSpec(memory_space=pltpu.SMEM)]
        + [fixed(a.shape) for a in given]
        + [anywhere],
        out_specs=[fixed(tokens.shape), anywhere],
        out_shape=[pltpu.HBM(tokens.shape, F32)] * 2,
        scratch_shapes=[
            pltpu.VMEM((many, micro, rows, pair), F32), pltpu.SemaphoreType.DMA((many,)),
        ],
        input_output_aliases={1 + len(given): 1},
        compiler_params=vmem(24),
        cost_estimate=FREE,
        name="token_grads",
    )(seat, *given, dv)


def projection_grads(parts, weight, gain, wide):
    seats, depth, held, _ = parts.shape
    width = seats * wide

    def kernel(p_ref, w_ref, gain_ref, dw_out, dg_out):
        gain = gain_ref[...]
        grown = jnp.zeros((held, 1), F32)
        for s in range(seats):
            total = p_ref[s, 0].astype(F32)
            for d in range(1, depth):
                total = total + p_ref[s, d].astype(F32)
            for t in range(3):
                at = slice(t * width + s * wide, t * width + (s + 1) * wide)
                piece = total[:, t * wide : (t + 1) * wide]
                dw_out[:, at] = piece * gain
                grown = grown + jnp.sum(piece * w_ref[:, at].astype(F32), axis=1, keepdims=True)
        dg_out[...] = jnp.broadcast_to(grown, (held, 128)).T[:1, :]

    return pl.pallas_call(
        kernel,
        out_shape=[
            pltpu.HBM(weight.shape, F32), pltpu.HBM((1, held), F32),
        ],
        cost_estimate=FREE,
        name="projection_grads",
    )(parts, weight, gain)


def pair_grads(parts, gate, up, gain, depth, short):
    outer, group, held, slab2 = parts.shape
    slab = slab2 // 2
    tall = slab // (OUTER * depth)
    fan = gate.shape[1]

    def kernel(p_ref, gate_ref, up_ref, gain_ref, dgate_out, dup_out, dg_out):
        for q in range(group):
            total = p_ref[0, q].astype(F32)
            for y in range(1, outer):
                total = total + p_ref[y, q].astype(F32)
            for m, out in enumerate((dgate_out, dup_out)):
                for y in range(OUTER):
                    for d in range(depth):
                        at = m * slab + (y * depth + d) * tall
                        to = ((y * group + q) * depth + d) * short
                        out[:, to : to + short] = total[:, at : at + short]
        dgate = dgate_out[...]
        dup = dup_out[...]
        grown = jnp.sum(
            dgate * gate_ref[...].astype(F32) + dup * up_ref[...].astype(F32),
            axis=1,
            keepdims=True,
        )
        dg_out[...] = jnp.broadcast_to(grown, (held, 128)).T[:1, :]
        dgate_out[...] = dgate * gain_ref[...]
        dup_out[...] = dup * gain_ref[...]

    return pl.pallas_call(
        kernel,
        out_shape=[
            pltpu.HBM((held, fan), F32), pltpu.HBM((held, fan), F32), pltpu.HBM((1, held), F32),
        ],
        cost_estimate=FREE,
        name="pair_grads",
    )(parts, gate, up, gain)


def rope_tables(total, wide):
    positions = np.arange(total, dtype=np.float32)
    inverse = np.float32(10000.0) ** (-np.arange(0, HEAD_DIM, 2, dtype=np.float32) / HEAD_DIM)
    angles = (positions[:, None] * inverse[None, :].astype(np.float32)).astype(np.float64)
    cosine, sine = np.cos(angles), np.sin(angles)
    cosine = np.tile(cosine, (1, 2 * wide // HEAD_DIM))
    sine = np.tile(np.concatenate([-sine, sine], -1), (1, wide // HEAD_DIM))
    return jnp.asarray(cosine.astype(np.float32)), jnp.asarray(sine.astype(np.float32))


def local(
    tokens, first_values, out_grad, lengths, norm1_gain, qkv_weight, out_weight, norm2_gain,
    gate_weight, up_weight, down_weight,
):
    micro, rows, width = tokens.shape
    seats, depth = lax.axis_size("seq"), lax.axis_size("dp")
    devices = seats * depth
    seat = lax.axis_index("seq")
    group = seats // OUTER
    spread = group // CORES
    outer = seat // group
    total = seats * rows
    wide = width // seats
    held = qkv_weight.shape[0]
    fan_rows = down_weight.shape[0]
    fan = fan_rows * devices
    tall = -(-fan_rows // 16) * 16
    slab = OUTER * depth * tall
    many = micro * rows
    seat_arr = jnp.reshape(seat, (1,)).astype(jnp.int32)
    level_arr = jnp.reshape(lax.axis_index("dp"), (1,)).astype(jnp.int32)

    def swap(value, mask):
        return lax.ppermute(value, "seq", [(i, i ^ mask) for i in range(seats)])

    def token(value):
        return value[(0,) * value.ndim].astype(F32) * 0.0

    def swap_depth(value, mask):
        return lax.ppermute(value, "dp", [(i, i ^ mask) for i in range(depth)])

    same_core = [[i for i in range(seats) if i % CORES == c] for c in range(CORES)]
    every = ("seq", "dp")
    core = seat % CORES
    chip = seat // CORES
    inner = [2 * j for j in range(spread)]
    across = [group + 2 * j for j in range(spread)]

    gain1 = norm1_gain.astype(F32)[:, None]
    gain2 = norm2_gain.astype(F32)[:, None]

    lanes = width + CORES * wide

    def together(part, *operands):
        shapes = jax.eval_shape(part, *operands)
        return lax.cond(
            lengths[0] > 0,
            part,
            lambda *_: jax.tree.map(lambda s: jnp.zeros(s.shape, s.dtype), shapes),
            *operands,
        )

    def to_seats(value, groups=None):
        return lax.all_to_all(
            value, "seq", split_axis=0, concat_axis=0, tiled=True, axis_index_groups=groups
        )

    def to_all(value):
        return lax.all_to_all(value, every, split_axis=0, concat_axis=0, tiled=True)

    tail = jnp.concatenate(
        [jnp.pad(down_weight, ((0, tall - fan_rows), (0, 0))), out_weight], 0
    )
    tail = lax.all_gather(tail, "dp", axis=0)

    def columns(weight):
        scaled = (weight.astype(F32) * gain2).astype(BF16)
        scaled = scaled.reshape(held, OUTER, group, depth, fan_rows).transpose(2, 0, 1, 3, 4)
        scaled = jnp.pad(scaled, ((0, 0),) * 4 + ((0, tall - fan_rows),))
        return scaled.reshape(group, held, slab)

    def weights_first():
        pair = jnp.concatenate([columns(gate_weight), columns(up_weight)], -1)
        pair = jnp.concatenate([pair] * OUTER, 0)
        wqkv = (qkv_weight.astype(F32) * gain1).astype(BF16)
        wqkv = wqkv.reshape(held, 3, seats, wide).transpose(2, 0, 1, 3).reshape(seats, held, 3 * wide)
        both = to_seats(jnp.concatenate([pair, wqkv], -1))
        return (
            both[..., : 2 * slab], both[..., 2 * slab :],
            payloads(seat_arr, tokens, first_values, spread, wide),
        )

    pair, wqkv, (own, far_own, *arrived) = together(weights_first)
    pair = lax.all_gather(pair, "dp", axis=0).reshape(depth, OUTER, group, held, 2 * slab)

    def first_leg(arrived, far_own, own, wqkv):
        return (
            [swap(v, m) for v, m in zip(arrived, inner[1:])], swap(far_own, group),
            lax.all_gather(wqkv, "dp", axis=1).reshape(width, 3 * wide),
            swap(own, 1), swap(out_grad, 1),
        )

    arrived, far_own, wqkv, own_b, grad_b = together(first_leg, arrived, far_own, own, wqkv)
    split = 128 * (lanes // 256)

    def second_leg(arrived, far_own, tail):
        pair = CORES * wide
        lower, upper = [], []
        for j in range(1, spread):
            lower.append(swap(arrived[j - 1][..., :split], group))
            at = width + j * pair
            rest = jnp.concatenate([far_own[..., split:width], far_own[..., at : at + pair]], -1)
            upper.append(swap(rest, inner[j]))
        down, wout = tail[:, :tall], tail[:, tall:]
        grads = [swap(out_grad[:1], m) for m in inner[1:]]
        return (
            lower, upper, [swap(v, 1) for v in arrived], swap(far_own, 1), down,
            [wout, swap(wout, group)], grads,
        )

    lower, upper, arrived_b, far_own_b, down_mine, wout, grads_lo = together(
        second_leg, arrived, far_own, tail
    )
    mine = [own, *arrived, far_own, *lower, *upper]
    theirs = [own_b, *arrived_b, far_own_b, *[swap(v, 1) for v in lower + upper]]
    places = [(m, 0) for m in inner + across] + [(m, split) for m in across[1:]]
    order = tuple(places) + tuple((m + 1, lane) for m, lane in places)
    xs = mine + theirs
    near = [(own, own_b)] + list(zip(arrived, arrived_b))
    cosine, sine = rope_tables(total, wide)

    def attend(xs, wqkv, down, wout):
        wout = jnp.stack(wout)
        return (
            attn_fwd(seat_arr, lengths, xs, wqkv, cosine, sine, order, []),
            swap(down, group),
            jnp.stack([wout] + [swap(wout, m) for m in inner[1:]]),
            [swap(out_grad[1:], m) for m in inner[1:]],
        )

    (qkv, ot, *sends, lse, r1), down_far, wout, grads_hi = together(
        attend, xs, wqkv, down_mine, wout
    )

    def spread_out(send, wout, wqkv, *grads):
        return to_seats(send, same_core), swap(wout, 1), swap(wqkv, 1), [[swap(v, 1) for v in g] for g in grads]

    turns = list(range(1, spread)) + [0]
    o, wout_theirs, wqkv_theirs, grads_b = together(
        spread_out, sends[turns[0]], wout, wqkv, grads_lo, grads_hi
    )
    cotangents = [((out_grad,), (grad_b,))]
    cotangents += list(zip(zip(grads_lo, grads_hi), zip(*grads_b)))
    weights = (pair, down_mine, down_far, wout, wout_theirs)
    near_z, sets, near_f, z_parts = [], [], [], []
    for turn, at in enumerate(turns):

        def rows_of(o, near_z, send, weights):
            z = [swap(v, m) for v, m in near_z]
            after = [to_seats(v, same_core) for v in send]
            return (
                feed_forward(seat_arr, *near[at], *cotangents[at], *o, weights, at == 0), z, after
            )

        masks_z = [inner[j] for j in turns[turn - 1 : turn]] if turn else []
        out, z, after = together(
            lambda o, near_z, send, weights: rows_of(
                o, list(zip(near_z, masks_z)), send, weights
            ),
            (o, swap(o, 1)), near_z[-1:], [sends[j] for j in turns[turn + 1 : turn + 2]], weights,
        )
        z_parts += z
        o = after[0] if after else None
        za, zb_lo, zb_hi, fa, fb, *kept = out
        sets.append((*kept[:4], *cotangents[at][0], *cotangents[at][1]))
        if at:
            near_z.append(add_parts(za, [swap(zb_lo, 1), swap(zb_hi, 1)]))
            near_f.append((fa, fb))
    y, o_both, wout = kept[4:]
    dy, dyb, d_o = middle_back(
        y, [za] + z_parts, [swap(zb_lo, 1), swap(zb_hi, 1)], out_grad, wout, wide
    )

    near_fa = jnp.stack([v[0] for v in near_f])
    near_fb = jnp.stack([v[1] for v in near_f])

    def weight_grads(d_o, dyb, kept, near_fa, near_fb):
        return to_seats(d_o), ff_grads(
            seat_arr, kept, o_both, dyb, swap(dyb, 1), near_fa, swap(near_fb, 1),
            (depth, OUTER * group, held, 2 * slab), tall, spread,
        )

    d_o, (pair, down_mine, wout_own, *parcels) = together(
        weight_grads, d_o, dyb, sets, near_fa, near_fb
    )
    pair = lax.psum_scatter(
        pair.reshape(-1, 2 * slab), "dp", scatter_dimension=0, tiled=True
    ).reshape(OUTER * group, held, 2 * slab)

    def attend_back(parcels, d_o, xs):
        out = attn_bwd(
            seat_arr, lengths, xs, wqkv.shape, d_o, cosine, sine, qkv, ot, lse, r1, order,
            across + inner, [],
        )
        return out, [swap(v, m) for v, m in zip(parcels, inner[1:] + across[:1])]

    (e_mine, e_theirs, dwq), landed = together(attend_back, parcels[:spread], d_o, xs)

    def to_x(e_theirs, parcels, fb):
        both = back_to_x(seat_arr, e_mine, swap(e_theirs, 1), wqkv, wqkv_theirs)
        return both, [swap(v, m) for v, m in zip(parcels, across[1:])], swap(fb, 1)

    both, more, fb = together(to_x, e_theirs, parcels[spread:], fb)
    landed = landed + more
    far, close = both[:spread], both[spread:]

    def first_return(close, far, dwq, down_mine, wout_own, landed):
        got = [swap(close[j], inner[j]) for j in range(1, spread)] + [swap(far[0], across[0])]
        dwq = to_all(dwq.reshape(devices, held, 3 * wide))
        tail = plane_sums(level_arr, down_mine, wout_own, landed)
        output = y + fa.astype(F32) + fb.astype(F32)
        output = output + sum(v[:many].astype(F32) for v in landed[: spread - 1])
        return got, dwq, tail, output.astype(BF16).reshape(tokens.shape)

    got, dwq, tail, output = together(first_return, close, far, dwq, down_mine, wout_own, landed)

    def second_return(got, far, pair, dwq, tail):
        tail = [tail[0]] + [swap_depth(tail[k], k) for k in range(1, depth)]
        pair = to_seats(pair)
        return (
            [swap(far[j], across[j]) for j in range(1, spread)],
            token_sums(seat_arr, dy, got, list(range(spread + 1)), wide),
            pair_grads(
                pair.reshape(OUTER, group, held, 2 * slab), gate_weight, up_weight, gain2, depth,
                fan_rows,
            ),
            projection_grads(dwq.reshape(seats, depth, held, 3 * wide), qkv_weight, gain1, wide),
            tail_grads(tail, tall, fan_rows),
        )

    rest, (dx, dv), pair_out, projection_out, (down_grad, out_grad_w) = together(
        second_return, [close[0]] + got, far, pair, dwq, tail
    )
    gate_grad, up_grad, gain2_grad = pair_out
    qkv_grad, gain1_grad = projection_out
    d_tokens, d_first = token_grads(
        seat_arr, tokens, dy, dx, dv, rest, list(range(spread + 1, 2 * spread)), wide
    )
    gain1_grad, gain2_grad = gain1_grad.reshape(held), gain2_grad.reshape(held)
    return (
        output, d_tokens, d_first, gain1_grad, qkv_grad, out_grad_w, gain2_grad, gate_grad, up_grad,
        down_grad,
    )


def solution(mesh):
    rows = P(("seq", "dp"), None)
    acts = P("dp", "seq", None)
    gains = P(("seq", "dp"))
    return jax.shard_map(
        local,
        mesh=mesh,
        in_specs=(acts, acts, acts, P("dp"), gains, rows, rows, gains, rows, rows, rows),
        out_specs=(acts, acts, acts, gains, rows, rows, gains, rows, rows, rows),
        check_vma=False,
    )
```

```python
import functools

import jax
import jax.numpy as jnp
import numpy as np
from jax import lax
from jax.experimental import pallas as pl
from jax.experimental.pallas import tpu as pltpu
from jax.sharding import PartitionSpec as P

HEADS = 16
HEAD_DIM = 64
EPSILON = 1e-06
CORES = 2
OUTER = 2
BLOCK = 256
NEG = -1e30
F32 = jnp.float32
BF16 = jnp.bfloat16
MIB = 1024 * 1024
FREE = pl.CostEstimate(flops=0, bytes_accessed=0, transcendentals=0)


def lasting(us):
    return pl.CostEstimate(flops=0, bytes_accessed=int(us * 3.69e6), transcendentals=0)


def vmem(mib, scale=1):
    return pltpu.CompilerParams(vmem_limit_bytes=int(min(60, mib * max(scale, 1))) * MIB)


def held_in_hbm(*arrays):
    return [pltpu.with_memory_space_constraint(a, pltpu.HBM) for a in arrays]


class Copies:
    def __init__(self, sems):
        self.sems, self.used, self.waiting = sems, 0, {}

    def start(self, name, src, dst):
        copy = pltpu.make_async_copy(src, dst, self.sems.at[self.used])
        self.used += 1
        copy.start()
        self.waiting.setdefault(name, []).append(copy)

    def wait(self, *names):
        for name in names or list(self.waiting):
            for copy in self.waiting.pop(name, []):
                copy.wait()


def corner(a):
    block = (1,) * (a.ndim - 2) + (min(16, a.shape[-2]), min(128, a.shape[-1]))
    return pl.BlockSpec(block, lambda *_: (0,) * a.ndim)


def dot_nn(a, b):
    return lax.dot_general(a, b, (((1,), (0,)), ((), ())), preferred_element_type=F32)


def dot_nt(a, b):
    return lax.dot_general(a, b, (((1,), (1,)), ((), ())), preferred_element_type=F32)


def dot_tn(a, b):
    return lax.dot_general(a, b, (((0,), (0,)), ((), ())), preferred_element_type=F32)


def turned(u):
    half = HEAD_DIM // 2
    width = u.shape[1]
    if width % 128:
        parts = []
        for h in range(width // HEAD_DIM):
            lo = h * HEAD_DIM
            parts += [u[:, lo + half : lo + HEAD_DIM], u[:, lo : lo + half]]
        return jnp.concatenate(parts, axis=1)
    lane = lax.broadcasted_iota(jnp.int32, u.shape, 1) % HEAD_DIM
    return jnp.where(lane < half, pltpu.roll(u, width - half, 1), pltpu.roll(u, half, 1))


def head_mask(shape, h):
    lane = lax.broadcasted_iota(jnp.int32, shape, 1)
    return (lane >= h * HEAD_DIM) & (lane < (h + 1) * HEAD_DIM)


def own_head(u, h):
    if u.shape[1] == HEAD_DIM:
        return u
    return jnp.where(head_mask(u.shape, h), u, jnp.zeros_like(u))


def join_heads(parts):
    out = parts[0]
    for h in range(1, len(parts)):
        out = jnp.where(head_mask(out.shape, h), parts[h], out)
    return out


def fill_rows(seat, refs, order, dest):
    rows = refs[0].shape[1]
    for ref, (m, lane) in zip(refs, order):
        at = pl.multiple_of((seat ^ m) * rows, rows)
        dest[pl.ds(at, rows), lane : lane + ref.shape[2]] = ref[0]


def attn_fwd_kernel(
    order, seat_ref, len_ref, w_ref, cos_ref, sin_ref, *refs,
):
    xs = refs[: len(order)]
    spread = len(refs) - len(order) - 6
    qkv_out, ot_out = refs[len(order) : len(order) + 2]
    sends = refs[len(order) + 2 : len(order) + 2 + spread]
    lse_out, r1_out, xbuf, vt = refs[-4:]
    slot = pl.program_id(0)
    seat = seat_ref[0]
    length = len_ref[slot]
    total = xbuf.shape[0]
    width = w_ref.shape[0]
    wide = w_ref.shape[1] // 3
    heads = wide // HEAD_DIM
    blocks = total // BLOCK
    fill_rows(seat, xs, order, xbuf)
    for b in range(blocks):
        at = slice(b * BLOCK, (b + 1) * BLOCK)
        x = xbuf[at, :width]
        xf = x.astype(F32)
        r1 = lax.rsqrt(jnp.mean(xf * xf, axis=1, keepdims=True) + EPSILON)
        qkv = dot_nn(x, w_ref[...]) * r1
        cosine = cos_ref[at, :]
        sine = sin_ref[at, :]
        q = qkv[:, :wide]
        k = qkv[:, wide : 2 * wide]
        v = qkv[:, 2 * wide :]
        q = (q * cosine + turned(q) * sine) * (HEAD_DIM**-0.5)
        k = k * cosine + turned(k) * sine
        first = xbuf[at, width : width + wide]
        second = xbuf[at, width + wide :]
        v1 = jnp.where(seat % CORES == 0, first, second).astype(F32)
        vm = 0.5 * v + 0.5 * v1
        qkv_out[0, at, :wide] = q.astype(BF16)
        qkv_out[0, at, wide : 2 * wide] = k.astype(BF16)
        qkv_out[0, at, 2 * wide :] = vm.astype(BF16)
        vt[:, at] = vm.T.astype(BF16)
        r1_out[0, at, :] = jnp.broadcast_to(r1, (BLOCK, r1_out.shape[2]))
    for b in range(blocks):
        at = slice(b * BLOCK, (b + 1) * BLOCK)
        count = (b + 1) * BLOCK
        q = qkv_out[0, at, :wide]
        query = b * BLOCK + lax.broadcasted_iota(jnp.int32, (1, BLOCK), 1)
        last = jnp.minimum(query, length - 1)
        key = lax.broadcasted_iota(jnp.int32, (count, BLOCK), 0)
        allowed = key <= last
        ots = []
        for h in range(heads):
            k = own_head(qkv_out[0, :count, wide : 2 * wide], h)
            scores = jnp.where(allowed, dot_nt(k, q), NEG)
            top = jnp.max(scores, axis=0, keepdims=True)
            weights = jnp.exp(scores - top)
            total_w = jnp.sum(weights, axis=0, keepdims=True)
            ot = dot_nn(vt[h * HEAD_DIM : (h + 1) * HEAD_DIM, :count], weights.astype(BF16))
            ots.append(ot / total_w)
            lse_out[0, h : h + 1, at] = top + jnp.log(total_w)
        ot = jnp.concatenate(ots, axis=0)
        ot_out[0, :, at] = ot
        o = ot.T.astype(BF16)
        for x in range(spread):
            sends[x ^ (b % spread)][(b // spread) * spread + x, 0] = o


def chunk_specs(xs, order, lanes):
    return [
        pl.BlockSpec((1, x.shape[1], min(x.shape[2], lanes - lane)), lambda i: (i, 0, 0))
        for x, (_, lane) in zip(xs, order)
    ]


def attn_fwd(seat, lengths, xs, w, cosine, sine, order, ready):
    micro, rows, lanes = xs[0].shape
    width = w.shape[0]
    total = cosine.shape[0]
    spread = total // rows // (OUTER * CORES)
    wide = w.shape[1] // 3
    heads = wide // HEAD_DIM
    smem = pl.BlockSpec(memory_space=pltpu.SMEM)
    whole = lambda a: pl.BlockSpec(a.shape, lambda i: (0,) * a.ndim)
    pairs = total * total // 2 * micro * wide
    return pl.pallas_call(
        functools.partial(attn_fwd_kernel, order),
        grid=(micro,),
        in_specs=[smem, smem, whole(w), whole(cosine), whole(sine)]
        + chunk_specs(xs, order, lanes)
        + [corner(a) for a in ready],
        out_specs=[
            pl.BlockSpec((1, total, 3 * wide), lambda i: (i, 0, 0)),
            pl.BlockSpec((1, wide, total), lambda i: (i, 0, 0)),
        ]
        + [pl.BlockSpec((OUTER * spread, 1, BLOCK, wide), lambda i: (0, i, 0, 0))] * spread
        + [
            pl.BlockSpec((1, heads, total), lambda i: (i, 0, 0)),
            pl.BlockSpec((1, total, 128), lambda i: (i, 0, 0)),
        ],
        out_shape=[
            pltpu.HBM((micro, total, 3 * wide), BF16),
            pltpu.HBM((micro, wide, total), F32),
        ]
        + [pltpu.HBM((OUTER * spread, micro, BLOCK, wide), BF16)] * spread
        + [
            pltpu.HBM((micro, heads, total), F32),
            pltpu.HBM((micro, total, 128), F32),
        ],
        scratch_shapes=[pltpu.VMEM((total, lanes), BF16), pltpu.VMEM((wide, total), BF16)],
        compiler_params=vmem(30, total / 1024),
        cost_estimate=lasting(20),
        name="attn_fwd",
    )(seat, lengths, *held_in_hbm(w, cosine, sine, *xs), *ready)


def attn_bwd_kernel(
    order, sent, seat_ref, len_ref, do_ref, cos_ref, sin_ref, qkv_ref, ot_ref, lse_ref, r1_ref,
    *refs,
):
    xs = refs[: len(order)]
    outs = refs[-6 - CORES : -6]
    dw_out, xbuf, dobuf, dqt, ebuf, dw = refs[-6:]
    slot = pl.program_id(0)
    seat = seat_ref[0]
    rows = do_ref.shape[2]
    length = len_ref[slot]
    total = xbuf.shape[0]
    wide = do_ref.shape[3]
    heads = wide // HEAD_DIM
    blocks = total // BLOCK
    fill_rows(seat, xs, order, xbuf)
    for j in range(do_ref.shape[0]):
        dobuf[j * rows : (j + 1) * rows, :] = do_ref[j, 0]
    dot_t = dobuf[...].astype(F32).T
    deltas = []
    for h in range(heads):
        part = slice(h * HEAD_DIM, (h + 1) * HEAD_DIM)
        deltas.append(jnp.sum(dot_t[part, :] * ot_ref[0, part, :], axis=0, keepdims=True))
    dqt[...] = jnp.zeros_like(dqt)
    for b in range(blocks):
        at = slice(b * BLOCK, (b + 1) * BLOCK)
        later = slice(b * BLOCK, total)
        count = total - b * BLOCK
        k = qkv_ref[0, at, wide : 2 * wide]
        v = qkv_ref[0, at, 2 * wide :]
        kt = k.astype(F32).T.astype(BF16)
        q = qkv_ref[0, later, :wide]
        d_o = dobuf[later, :]
        query = b * BLOCK + lax.broadcasted_iota(jnp.int32, (1, count), 1)
        last = jnp.minimum(query, length - 1)
        key = b * BLOCK + lax.broadcasted_iota(jnp.int32, (BLOCK, count), 0)
        allowed = key <= last
        dks, dvs = [], []
        for h in range(heads):
            part = slice(h * HEAD_DIM, (h + 1) * HEAD_DIM)
            scores = jnp.where(allowed, dot_nt(own_head(k, h), q), NEG)
            weights = jnp.exp(scores - lse_ref[0, h : h + 1, later])
            d_weights = dot_nt(own_head(v, h), d_o)
            ds = (weights * (d_weights - deltas[h][:, later])).astype(BF16)
            dvs.append(dot_nn(weights.astype(BF16), d_o))
            dks.append(dot_nn(ds, q))
            dqt[part, later] += dot_nn(kt[part, :], ds)
        cosine = cos_ref[at, :]
        sine = sin_ref[at, :]
        r1 = r1_ref[0, at, 0:1]
        dk = join_heads(dks)
        dk = dk * cosine - turned(dk) * sine
        dv = 0.5 * join_heads(dvs)
        ebuf[at, 3 * wide :] = dv.astype(BF16)
        ebuf[at, wide : 2 * wide] = (dk * r1).astype(BF16)
        ebuf[at, 2 * wide : 3 * wide] = (dv * r1).astype(BF16)
    for b in range(blocks):
        at = slice(b * BLOCK, (b + 1) * BLOCK)
        dq = dqt[:, at].T * (HEAD_DIM**-0.5)
        dq = dq * cos_ref[at, :] - turned(dq) * sin_ref[at, :]
        ebuf[at, :wide] = (dq * r1_ref[0, at, 0:1]).astype(BF16)
    for low, out in enumerate(outs):
        for j, m in enumerate(sent):
            at = pl.multiple_of((seat ^ m ^ low) * rows, rows)
            out[j, 0] = ebuf[pl.ds(at, rows), :]
    grown = dot_tn(xbuf[...], ebuf[:, : 3 * wide])

    @pl.when(slot == 0)
    def _():
        dw[...] = grown

    @pl.when(slot > 0)
    def _():
        dw[...] += grown

    @pl.when(slot == pl.num_programs(0) - 1)
    def _():
        dw_out[...] = dw[...].astype(BF16)


def attn_bwd(seat, lengths, xs, wshape, d_o, cosine, sine, qkv, ot, lse, r1, order, sent, ready):
    micro, rows = xs[0].shape[:2]
    width = wshape[0]
    total = cosine.shape[0]
    wide = wshape[1] // 3
    heads = wide // HEAD_DIM
    smem = pl.BlockSpec(memory_space=pltpu.SMEM)
    whole = lambda a: pl.BlockSpec(a.shape, lambda i: (0,) * a.ndim)
    vspec = pl.BlockSpec((d_o.shape[0], 1, rows, wide), lambda i: (0, i, 0, 0))
    zshapes = [pltpu.HBM((len(sent), micro, rows, 4 * wide), BF16)] * CORES
    pairs = total * total // 2 * micro * wide
    return pl.pallas_call(
        functools.partial(attn_bwd_kernel, order, sent),
        grid=(micro,),
        in_specs=[
            smem, smem, vspec, whole(cosine), whole(sine),
            pl.BlockSpec((1, total, 3 * wide), lambda i: (i, 0, 0)),
            pl.BlockSpec((1, wide, total), lambda i: (i, 0, 0)),
            pl.BlockSpec((1, heads, total), lambda i: (i, 0, 0)),
            pl.BlockSpec((1, total, 128), lambda i: (i, 0, 0)),
        ]
        + chunk_specs(xs, order, width)
        + [corner(a) for a in ready],
        out_specs=[
            pl.BlockSpec((len(sent), 1, rows, 4 * wide), lambda i: (0, i, 0, 0))
        ]
        * CORES
        + [pl.BlockSpec(wshape, lambda i: (0, 0))],
        out_shape=zshapes + [pltpu.HBM(wshape, BF16)],
        scratch_shapes=[
            pltpu.VMEM((total, width), BF16),
            pltpu.VMEM((total, wide), BF16),
            pltpu.VMEM((wide, total), F32),
            pltpu.VMEM((total, 4 * wide), BF16),
            pltpu.VMEM(wshape, F32),
        ],
        compiler_params=vmem(40, total / 1024),
        cost_estimate=lasting(20),
        name="attn_bwd",
    )(seat, lengths, *held_in_hbm(d_o, cosine, sine, qkv, ot, lse, r1, *xs), *ready)


def ff_kernel(
    own, parts, seat_ref, xa, xb, oa, ob, pair, down_mine, down_far, wout_mine, wout_theirs, *refs,
):
    cotangents, refs = (refs[:parts], refs[parts : 2 * parts]), refs[2 * parts :]
    za, zb_lo, zb_hi, fa, fb, hn_out, hid_out, dgate_out, dup_out = refs[:9]
    refs = refs[9:]
    if own:
        y_out, o_out, wout_out = refs[:3]
        refs = refs[3:]
    x_buf, g_buf, oa_buf, ob_buf, wout, wg, wu, wd, z_buf, f_buf, hn, hid, dgate, dup, y_buf, o_buf, sems = refs
    seat = seat_ref[0]
    core = seat % CORES
    micro, rows = xa.shape[:2]
    width = wout.shape[0]
    many = micro * rows
    depth, outer, group, held, slab2 = pair.shape
    slab = slab2 // 2
    spread = group // CORES
    tall = down_mine.shape[1]
    half = seat // group
    copies = Copies(sems)

    for low in range(CORES):
        there = pl.ds(pl.multiple_of((core ^ low) * rows, rows), rows)
        copies.start("o", oa.at[:, :, there, :], oa_buf.at[low])
        copies.start("o", ob.at[:, :, there, :], ob_buf.at[low])
    for rc, ref in enumerate((wout_mine, wout_theirs)):
        for rx in range(spread):
            for ry in range(outer):
                other = seat ^ (ry * group + rx * CORES + rc)
                for d in range(depth):
                    to = pl.ds(pl.multiple_of((other * depth + d) * held, held), held)
                    copies.start("wout", ref.at[rx, ry, d], wout.at[to, :])
    copies.start("x", xa.at[:, :, pl.ds(0, width)], x_buf.at[0])
    copies.start("x", xb.at[:, :, pl.ds(0, width)], x_buf.at[1])
    for part, dest in ((0, wg), (1, wu)):
        for y in range(outer):
            for q in range(group):
                for d in range(depth):
                    to = ((y * group + q) * depth + d) * held
                    copies.start(
                        "wg" if part == 0 else "wu",
                        pair.at[d, y, q, :, pl.ds(part * slab, slab)],
                        dest.at[pl.ds(to, held), :],
                    )
    for low, some in enumerate(cotangents):
        base = 0
        for ref in some:
            copies.start("g", ref, g_buf.at[low, pl.ds(base, ref.shape[0])])
            base += ref.shape[0]
    for ry, ref in enumerate((down_mine, down_far)):
        for d in range(depth):
            to = pl.ds(pl.multiple_of(((half ^ ry) * depth + d) * tall, tall), tall)
            copies.start("wd", ref.at[d], wd.at[to, :])

    copies.wait("o")
    for low in range(CORES):
        for j in range(oa_buf.shape[1]):
            a = oa_buf[low, j].reshape(many, oa_buf.shape[4])
            b = ob_buf[low, j].reshape(many, oa_buf.shape[4])
            wide = a.shape[1]
            here = slice(low * many, (low + 1) * many)
            o_buf[here, (2 * j) * wide : (2 * j + 1) * wide] = jnp.where(core == 0, a, b)
            o_buf[here, (2 * j + 1) * wide : (2 * j + 2) * wide] = jnp.where(core == 0, b, a)
    copies.wait("wout", "x")
    if own:
        copies.start("out", wout, wout_out)
        copies.start("out", o_buf, o_out)
    y = x_buf[...].reshape(2 * many, width).astype(F32) + dot_nn(o_buf[...], wout[...])
    r2 = lax.rsqrt(jnp.mean(y * y, axis=1, keepdims=True) + EPSILON)
    hn[...] = (y * r2).astype(BF16)
    if own:
        y_buf[...] = y[:many]
        copies.start("out", y_buf, y_out)
    copies.start("out", hn, hn_out)
    copies.wait("wg")
    gate = dot_nn(hn[...], wg[...])
    copies.wait("wu")
    up = dot_nn(hn[...], wu[...])
    sigma = jax.nn.sigmoid(gate)
    act = gate * sigma
    hid[...] = (act * up).astype(BF16)
    copies.start("out", hid, hid_out)
    copies.wait("g", "wd")
    dhid = dot_nt(g_buf[...].reshape(2 * many, width), wd[...])
    dgate[...] = (dhid * up * (sigma + act * (1.0 - sigma))).astype(BF16)
    dup[...] = (dhid * act).astype(BF16)
    copies.start("out", dgate, dgate_out)
    copies.start("out", dup, dup_out)
    z_buf[...] = (dot_nt(dgate[...], wg[...]) + dot_nt(dup[...], wu[...])).astype(BF16)
    copies.start("out", z_buf.at[pl.ds(0, many)], za)
    copies.start("out", z_buf.at[pl.ds(many, many // 2)], zb_lo)
    copies.start("out", z_buf.at[pl.ds(many + many // 2, many // 2)], zb_hi)
    f_buf[...] = dot_nn(hid[...], wd[...]).astype(BF16)
    copies.start("out", f_buf.at[pl.ds(0, many)], fa)
    copies.start("out", f_buf.at[pl.ds(many, many)], fb)
    copies.wait()


def feed_forward(seat, xa, xb, ga, gb, oa, ob, weights, own):
    pair, down_mine, down_far, wout_mine, wout_theirs = weights
    micro, rows = xa.shape[:2]
    width = ga[0].shape[2]
    many = micro * rows
    depth, outer, group, held, slab2 = pair.shape
    fan = slab2 // 2
    wide = oa.shape[3]
    outs = [(many, width), (many // 2, width), (many // 2, width), (many, width), (many, width)]
    outs = [pltpu.HBM(s, BF16) for s in outs + [(2 * many, width)] + [(2 * many, fan)] * 3]
    if own:
        outs += [
            pltpu.HBM((many, width), F32), pltpu.HBM((2 * many, width), BF16),
            pltpu.HBM((width, width), BF16),
        ]
    o_shape = (CORES, oa.shape[0], micro, rows, wide)
    scratch = [
        ((2, micro, rows, width), BF16), ((2, micro, rows, width), BF16), (o_shape, BF16),
        (o_shape, BF16), ((width, width), BF16), ((width, fan), BF16), ((width, fan), BF16),
        ((fan, width), BF16), ((2 * many, width), BF16), ((2 * many, width), BF16),
        ((2 * many, width), BF16), ((2 * many, fan), BF16), ((2 * many, fan), BF16),
        ((2 * many, fan), BF16), ((many, width), F32), ((2 * many, width), BF16),
    ]
    many_copies = 32 + 4 * outer * group * depth
    anywhere = pl.BlockSpec(memory_space=pl.ANY)
    return pl.pallas_call(
        functools.partial(ff_kernel, own, len(ga)),
        grid=(1,),
        in_specs=[pl.BlockSpec(memory_space=pltpu.SMEM)]
        + [anywhere] * (9 + 2 * len(ga)),
        out_specs=[anywhere] * len(outs),
        out_shape=outs,
        scratch_shapes=[pltpu.VMEM(s, t) for s, t in scratch]
        + [pltpu.SemaphoreType.DMA((many_copies,))],
        compiler_params=vmem(56),
        cost_estimate=lasting(16),
        name="ff_own" if own else "ff_near",
    )(seat, *held_in_hbm(xa, xb, oa, ob, *weights, *ga, *gb))


def ff_grads_kernel(sizes, group, spread, seat_ref, *refs):
    sets = []
    for size in sizes:
        sets.append(refs[:size])
        refs = refs[size:]
    o_ref, dyb_ref, dyb_theirs, fa, fb = refs[:5]
    refs = refs[5:]
    pair_out, down_mine, wout_own = refs[:3]
    parcels = refs[3 : 2 + 2 * spread]
    dwg, dwu, dwd, dwo = refs[2 + 2 * spread :]
    seat = seat_ref[0]
    outer = seat // group
    core = seat % CORES
    chip = seat // CORES
    depth, blocks, held, slab2 = pair_out.shape
    slab = slab2 // 2
    tall = down_mine.shape[1]
    many, width = dyb_ref.shape
    for n, (hn, hid, dgate, dup, *gs) in enumerate(sets):
        g = jnp.concatenate([r[...].reshape(-1, width) for r in gs], axis=0)
        new = dot_tn(hn[...], dgate[...]), dot_tn(hn[...], dup[...]), dot_tn(hid[...], g)
        for scratch, value in zip((dwg, dwu, dwd), new):
            if n == 0:
                scratch[...] = value
            else:
                scratch[...] += value
    for k in range(blocks):
        for d in range(depth):
            at = slice((k * depth + d) * held, (k * depth + d + 1) * held)
            pair_out[d, k, :, :slab] = dwg[at, :].astype(BF16)
            pair_out[d, k, :, slab:] = dwu[at, :].astype(BF16)
    far = parcels[spread - 1]
    for d in range(depth):
        pieces = []
        for k in range(OUTER):
            at = slice((k * depth + d) * tall, (k * depth + d + 1) * tall)
            pieces.append(dwd[at, :].astype(BF16))
        down_mine[d] = jnp.where(outer == 0, pieces[0], pieces[1])
        far[d * tall : (d + 1) * tall, :] = jnp.where(outer == 0, pieces[1], pieces[0])
    dyb = jnp.concatenate([dyb_ref[...], dyb_theirs[...]], axis=0)
    rows = depth * held
    for c in range(2 * spread):
        a = o_ref[:, (2 * c) * rows : (2 * c + 1) * rows]
        b = o_ref[:, (2 * c + 1) * rows : (2 * c + 2) * rows]
        dwo[c * rows : (c + 1) * rows, :] = dot_tn(jnp.where(core == 0, a, b), dyb)
    for j in range(2 * spread):
        at = pl.ds(pl.multiple_of((chip ^ j) * rows, rows), rows)
        value = dwo[at, :].astype(BF16)
        if j == 0:
            wout_own[...] = value
        else:
            out = parcels[j - 1]
            out[out.shape[0] - rows :, :] = value
    for j in range(spread - 1):
        parcels[j][:many, :] = (fa[j].astype(F32) + fb[j].astype(F32)).astype(BF16)


def ff_grads(seat, sets, o_both, dyb, dyb_theirs, fa, fb, pair_shape, tall, spread):
    def fixed(shape):
        return pl.BlockSpec(shape, lambda i: (0,) * len(shape), pipeline_mode=pl.Buffered(1))

    args = [a for arrays in sets for a in arrays]
    last = [o_both, dyb, dyb_theirs, fa, fb]
    args += last
    specs = [fixed(a.shape) for a in args]
    depth, _, held, slab2 = pair_shape
    many, width = dyb.shape
    fan = slab2 // 2
    rows = depth * held
    parcels = [(many + rows, width)] * (spread - 1) + [(depth * tall + rows, width)]
    parcels += [(rows, width)] * (spread - 1)
    outs = [pair_shape, (depth, tall, width), (rows, width)] + parcels
    return pl.pallas_call(
        functools.partial(ff_grads_kernel, [len(s) for s in sets], spread * CORES, spread),
        grid=(1,),
        in_specs=[pl.BlockSpec(memory_space=pltpu.SMEM)] + specs,
        out_specs=[fixed(s) for s in outs],
        out_shape=[pltpu.HBM(s, BF16) for s in outs],
        scratch_shapes=[
            pltpu.VMEM((width, fan), F32), pltpu.VMEM((width, fan), F32),
            pltpu.VMEM((fan, width), F32), pltpu.VMEM((2 * spread * rows, width), F32),
        ],
        compiler_params=vmem(56),
        cost_estimate=lasting(14),
        name="ff_grads",
    )(seat, *args)


def pieces_at(values, index):
    step = 1
    while step < len(values):
        flip = (index // step) % 2 == 1
        values = [jnp.where(flip, values[k ^ step], values[k]) for k in range(len(values))]
        step *= 2
    return values


def payloads(seat, tokens, first_values, spread, wide):
    micro, rows, width = tokens.shape
    lanes = CORES * wide

    def kernel(seat_ref, x_ref, *refs):
        firsts, outs = refs[: 2 * spread], refs[2 * spread :]
        for out in outs:
            out[0, :, :width] = x_ref[0]
        for j in range(spread):
            outs[1][0, :, width + j * lanes : width + (j + 1) * lanes] = firsts[spread + j][0]
            outs[j and 1 + j][0, :, width:] = firsts[j][0]

    def part(j):
        return pl.BlockSpec((1, rows, lanes), lambda i, s: (i, 0, (s[0] // CORES) ^ j))

    sizes = [width + lanes, width + spread * lanes] + [width + lanes] * (spread - 1)
    return pl.pallas_call(
        kernel,
        grid_spec=pltpu.PrefetchScalarGridSpec(
            num_scalar_prefetch=1,
            grid=(micro,),
            in_specs=[pl.BlockSpec((1, rows, width), lambda i, s: (i, 0, 0))]
            + [part(j) for j in range(2 * spread)],
            out_specs=[pl.BlockSpec((1, rows, n), lambda i, s: (i, 0, 0)) for n in sizes],
        ),
        out_shape=[pltpu.HBM((micro, rows, n), BF16) for n in sizes],
        cost_estimate=lasting(4),
        name="payloads",
    )(seat, *held_in_hbm(tokens, *([first_values] * (2 * spread))))


def middle_back(y, parts, pieces, grad, wout, wide):
    micro, rows, width = grad.shape
    seats = width // wide
    many = micro * rows

    def kernel(y_ref, g_ref, w_ref, *refs):
        zs = refs[: len(parts)]
        z = jnp.concatenate([r[...] for r in refs[len(parts) : len(parts) + len(pieces)]], axis=0)
        dy_out, dyb_out, do_out = refs[len(parts) + len(pieces) :]
        z = z.astype(F32)
        for ref in zs:
            z = z + ref[...].astype(F32)
        y = y_ref[...]
        r2 = lax.rsqrt(jnp.mean(y * y, axis=1, keepdims=True) + EPSILON)
        inner = jnp.mean(z * y, axis=1, keepdims=True)
        g = g_ref[...].reshape(many, width).astype(F32)
        dy = g + r2 * z - y * (r2 * r2 * r2 * inner)
        dy_out[...] = dy
        dyb = dy.astype(BF16)
        dyb_out[...] = dyb
        d_o = dot_nt(dyb, w_ref[...]).astype(BF16)
        for s in range(seats):
            do_out[s] = d_o[:, s * wide : (s + 1) * wide].reshape(micro, rows, wide)

    def fixed(shape):
        return pl.BlockSpec(shape, lambda i: (0,) * len(shape), pipeline_mode=pl.Buffered(1))

    given = held_in_hbm(y, grad, wout, parts[0]) + [*parts[1:], *pieces]
    return pl.pallas_call(
        kernel,
        grid=(1,),
        in_specs=[fixed(a.shape) for a in given],
        out_specs=[
            fixed((many, width)), fixed((many, width)), fixed((seats, micro, rows, wide)),
        ],
        out_shape=[
            pltpu.HBM((many, width), F32),
            pltpu.HBM((many, width), BF16),
            pltpu.HBM((seats, micro, rows, wide), BF16),
        ],
        compiler_params=vmem(24),
        cost_estimate=FREE,
        name="middle_back",
    )(*given)


def back_to_x(seat, mine, theirs, w_mine, w_theirs, ready):
    count, micro, rows, lanes = mine.shape
    width = w_mine.shape[0]
    wide = lanes // 4
    many = micro * rows

    def kernel(seat_ref, a_ref, b_ref, wa, wb, *refs):
        outs = refs[len(ready) : len(ready) + count]
        buf, sems = refs[-2:]
        core = seat_ref[0] % CORES
        copies = Copies(sems)
        for j in range(count):
            a = a_ref[j].reshape(many, lanes)
            b = b_ref[j].reshape(many, lanes)
            z = dot_nt(a[:, : 3 * wide], wa[...]) + dot_nt(b[:, : 3 * wide], wb[...])
            buf[j, :, :, :width] = z.astype(BF16).reshape(micro, rows, width)
            first = jnp.where(core == 0, a[:, 3 * wide :], b[:, 3 * wide :])
            second = jnp.where(core == 0, b[:, 3 * wide :], a[:, 3 * wide :])
            buf[j, :, :, width : width + wide] = first.reshape(micro, rows, wide)
            buf[j, :, :, width + wide :] = second.reshape(micro, rows, wide)
            copies.start("out", buf.at[j], outs[j])
        copies.wait()

    anywhere = pl.BlockSpec(memory_space=pl.ANY)
    out = pltpu.HBM((micro, rows, width + CORES * wide), BF16)
    fixed = lambda shape: pl.BlockSpec(
        shape, lambda i: (0,) * len(shape), pipeline_mode=pl.Buffered(1)
    )
    given = held_in_hbm(mine) + [theirs, w_mine, w_theirs]
    return pl.pallas_call(
        kernel,
        grid=(1,),
        in_specs=[pl.BlockSpec(memory_space=pltpu.SMEM)] + [fixed(a.shape) for a in given]
        + [corner(a) for a in ready],
        out_specs=[anywhere] * count,
        out_shape=[out] * count,
        scratch_shapes=[
            pltpu.VMEM((count, micro, rows, width + CORES * wide), BF16),
            pltpu.SemaphoreType.DMA((count,)),
        ],
        compiler_params=vmem(32),
        cost_estimate=lasting(5),
        name="back_to_x",
    )(seat, *given, *ready)


def plane_sums(level, down, wout, parcels):
    depth, tall, width = down.shape
    held = wout.shape[0] // depth
    spread = (len(parcels) + 1) // 2

    def kernel(level_ref, down_ref, wout_ref, *refs):
        parts, outs = refs[: len(parcels)], refs[len(parcels) :]
        far = parts[spread - 1]
        for k, out in enumerate(outs):
            d = level_ref[0] ^ k
            at = pl.ds(pl.multiple_of(d * tall, tall), tall)
            out[:tall, :] = (down_ref[d].astype(F32) + far[at, :].astype(F32)).astype(BF16)
            at = pl.ds(pl.multiple_of(d * held, held), held)
            total = wout_ref[at, :].astype(F32)
            for part in parts:
                base = part.shape[0] - depth * held
                at = pl.ds(pl.multiple_of(base + d * held, held), held)
                total = total + part[at, :].astype(F32)
            out[tall:, :] = total.astype(BF16)

    fixed = lambda shape: pl.BlockSpec(
        shape, lambda i: (0,) * len(shape), pipeline_mode=pl.Buffered(1)
    )
    given = [down, wout, *parcels]
    shape = (tall + held, width)
    return pl.pallas_call(
        kernel,
        grid=(1,),
        in_specs=[pl.BlockSpec(memory_space=pltpu.SMEM)] + [fixed(a.shape) for a in given],
        out_specs=[fixed(shape)] * depth,
        out_shape=[pltpu.HBM(shape, BF16)] * depth,
        compiler_params=vmem(24),
        cost_estimate=FREE,
        name="plane_sums",
    )(level, *given)


def add_parts(mine, theirs):
    def kernel(a_ref, *refs):
        b = jnp.concatenate([r[...] for r in refs[:-1]], axis=0)
        refs[-1][...] = (a_ref[...].astype(F32) + b.astype(F32)).astype(BF16)

    fixed = lambda shape: pl.BlockSpec(
        shape, lambda i: (0,) * len(shape), pipeline_mode=pl.Buffered(1)
    )
    return pl.pallas_call(
        kernel,
        grid=(1,),
        in_specs=[fixed(a.shape) for a in (mine, *theirs)],
        out_specs=fixed(mine.shape),
        out_shape=pltpu.HBM(mine.shape, BF16),
        compiler_params=vmem(16),
        cost_estimate=FREE,
        name="add_parts",
    )(*held_in_hbm(mine), *theirs)


def tail_grads(parts, tall, short):
    rows, width = parts[0].shape

    def kernel(*refs):
        *ins, down_out, wout_out = refs
        total = ins[0][...].astype(F32)
        for ref in ins[1:]:
            total = total + ref[...].astype(F32)
        down_out[...] = total[:short, :]
        wout_out[...] = total[tall:, :]

    return pl.pallas_call(
        kernel,
        out_shape=[pltpu.HBM((short, width), F32), pltpu.HBM((rows - tall, width), F32)],
        cost_estimate=FREE,
        name="tail_grads",
    )(*parts)


def fence(value, ready):
    def kernel(*_):
        pass

    return pl.pallas_call(
        kernel,
        grid=(1,),
        in_specs=[pl.BlockSpec(memory_space=pl.ANY)] + [corner(a) for a in ready],
        out_specs=pl.BlockSpec(memory_space=pl.ANY),
        out_shape=pltpu.HBM(value.shape, value.dtype),
        input_output_aliases={0: 0},
        cost_estimate=FREE,
        name="fence",
    )(value, *ready)


def token_sums(seat, dy, got, chips, wide):
    micro, rows, lanes = got[0].shape
    pair = CORES * wide
    width = lanes - pair
    many = len(got)

    def kernel(seat_ref, *refs):
        parts, (dx_out, dv_out) = refs[:many], refs[many:]
        z = parts[0][0, :, :width].astype(F32)
        for ref in parts[1:]:
            z = z + ref[0, :, :width].astype(F32)
        dx_out[0] = z
        chip = seat_ref[0] // CORES
        for ref, j in zip(parts, chips):
            at = pl.multiple_of((chip ^ j) * pair, pair)
            dv_out[0, :, pl.ds(at, pair)] = ref[0, :, width:].astype(F32)

    spec = lambda n: pl.BlockSpec((1, rows, n), lambda i: (i, 0, 0))
    return pl.pallas_call(
        kernel,
        grid=(micro,),
        in_specs=[pl.BlockSpec(memory_space=pltpu.SMEM)] + [spec(lanes)] * many,
        out_specs=[spec(width)] * 2,
        out_shape=[pltpu.HBM((micro, rows, width), F32)] * 2,
        cost_estimate=FREE,
        name="token_sums",
    )(seat, *got)


def token_grads(seat, tokens, dy, dx, dv, rest, chips, wide):
    micro, rows, width = tokens.shape
    pair = CORES * wide
    many = len(rest)

    def kernel(seat_ref, x_ref, dy_ref, dx_ref, *refs):
        parts = refs[:many]
        dx_out, dv_out, buf, sems = refs[many + 1 :]
        chip = seat_ref[0] // CORES
        copies = Copies(sems)
        for k, j in enumerate(chips):
            buf[k] = parts[k][:, :, width:].astype(F32)
            at = pl.multiple_of((chip ^ j) * pair, pair)
            copies.start("dv", buf.at[k], dv_out.at[:, :, pl.ds(at, pair)])
        z = dx_ref[...]
        for ref in parts:
            z = z + ref[:, :, :width].astype(F32)
        x = x_ref[...].astype(F32)
        inv = lax.rsqrt(jnp.mean(x * x, axis=2, keepdims=True) + EPSILON)
        inner = jnp.mean(z * x, axis=2, keepdims=True)
        dx_out[...] = dy_ref[...].reshape(micro, rows, width) + z - x * (inv * inv * inner)
        copies.wait()

    def fixed(shape):
        return pl.BlockSpec(shape, lambda i: (0,) * len(shape), pipeline_mode=pl.Buffered(1))

    anywhere = pl.BlockSpec(memory_space=pl.ANY)
    given = [tokens, dy, dx, *rest]
    return pl.pallas_call(
        kernel,
        grid=(1,),
        in_specs=[pl.BlockSpec(memory_space=pltpu.SMEM)]
        + [fixed(a.shape) for a in given]
        + [anywhere],
        out_specs=[fixed(tokens.shape), anywhere],
        out_shape=[pltpu.HBM(tokens.shape, F32)] * 2,
        scratch_shapes=[
            pltpu.VMEM((many, micro, rows, pair), F32), pltpu.SemaphoreType.DMA((many,)),
        ],
        input_output_aliases={1 + len(given): 1},
        compiler_params=vmem(24),
        cost_estimate=FREE,
        name="token_grads",
    )(seat, *given, dv)


def projection_grads(parts, weight, gain, wide):
    seats, depth, held, _ = parts.shape
    width = seats * wide

    def kernel(p_ref, w_ref, gain_ref, dw_out, dg_out):
        gain = gain_ref[...]
        grown = jnp.zeros((held, 1), F32)
        for s in range(seats):
            total = p_ref[s, 0].astype(F32)
            for d in range(1, depth):
                total = total + p_ref[s, d].astype(F32)
            for t in range(3):
                at = slice(t * width + s * wide, t * width + (s + 1) * wide)
                piece = total[:, t * wide : (t + 1) * wide]
                dw_out[:, at] = piece * gain
                grown = grown + jnp.sum(piece * w_ref[:, at].astype(F32), axis=1, keepdims=True)
        dg_out[...] = jnp.broadcast_to(grown, (held, 128)).T[:1, :]

    return pl.pallas_call(
        kernel,
        out_shape=[
            pltpu.HBM(weight.shape, F32), pltpu.HBM((1, held), F32),
        ],
        cost_estimate=FREE,
        name="projection_grads",
    )(parts, weight, gain)


def pair_grads(parts, gate, up, gain, depth, short):
    outer, group, held, slab2 = parts.shape
    slab = slab2 // 2
    tall = slab // (OUTER * depth)
    fan = gate.shape[1]

    def kernel(p_ref, gate_ref, up_ref, gain_ref, dgate_out, dup_out, dg_out):
        for q in range(group):
            total = p_ref[0, q].astype(F32)
            for y in range(1, outer):
                total = total + p_ref[y, q].astype(F32)
            for m, out in enumerate((dgate_out, dup_out)):
                for y in range(OUTER):
                    for d in range(depth):
                        at = m * slab + (y * depth + d) * tall
                        to = ((y * group + q) * depth + d) * short
                        out[:, to : to + short] = total[:, at : at + short]
        dgate = dgate_out[...]
        dup = dup_out[...]
        grown = jnp.sum(
            dgate * gate_ref[...].astype(F32) + dup * up_ref[...].astype(F32),
            axis=1,
            keepdims=True,
        )
        dg_out[...] = jnp.broadcast_to(grown, (held, 128)).T[:1, :]
        dgate_out[...] = dgate * gain_ref[...]
        dup_out[...] = dup * gain_ref[...]

    return pl.pallas_call(
        kernel,
        out_shape=[
            pltpu.HBM((held, fan), F32), pltpu.HBM((held, fan), F32), pltpu.HBM((1, held), F32),
        ],
        cost_estimate=FREE,
        name="pair_grads",
    )(parts, gate, up, gain)


def rope_tables(total, wide):
    positions = np.arange(total, dtype=np.float32)
    inverse = np.float32(10000.0) ** (-np.arange(0, HEAD_DIM, 2, dtype=np.float32) / HEAD_DIM)
    angles = (positions[:, None] * inverse[None, :].astype(np.float32)).astype(np.float64)
    cosine, sine = np.cos(angles), np.sin(angles)
    cosine = np.tile(cosine, (1, 2 * wide // HEAD_DIM))
    sine = np.tile(np.concatenate([-sine, sine], -1), (1, wide // HEAD_DIM))
    return jnp.asarray(cosine.astype(np.float32)), jnp.asarray(sine.astype(np.float32))


def local(
    tokens, first_values, out_grad, lengths, norm1_gain, qkv_weight, out_weight, norm2_gain,
    gate_weight, up_weight, down_weight,
):
    micro, rows, width = tokens.shape
    seats, depth = lax.axis_size("seq"), lax.axis_size("dp")
    devices = seats * depth
    seat = lax.axis_index("seq")
    group = seats // OUTER
    spread = group // CORES
    outer = seat // group
    total = seats * rows
    wide = width // seats
    held = qkv_weight.shape[0]
    fan_rows = down_weight.shape[0]
    fan = fan_rows * devices
    tall = -(-fan_rows // 16) * 16
    slab = OUTER * depth * tall
    many = micro * rows
    seat_arr = jnp.reshape(seat, (1,)).astype(jnp.int32)
    level_arr = jnp.reshape(lax.axis_index("dp"), (1,)).astype(jnp.int32)

    def swap(value, mask):
        return lax.ppermute(value, "seq", [(i, i ^ mask) for i in range(seats)])

    def token(value):
        return value[(0,) * value.ndim].astype(F32) * 0.0

    def swap_depth(value, mask):
        return lax.ppermute(value, "dp", [(i, i ^ mask) for i in range(depth)])

    same_core = [[i for i in range(seats) if i % CORES == c] for c in range(CORES)]
    every = ("seq", "dp")
    core = seat % CORES
    chip = seat // CORES
    inner = [2 * j for j in range(spread)]
    across = [group + 2 * j for j in range(spread)]

    gain1 = norm1_gain.astype(F32)[:, None]
    gain2 = norm2_gain.astype(F32)[:, None]

    lanes = width + CORES * wide

    def together(part, *operands):
        shapes = jax.eval_shape(part, *operands)
        return lax.cond(
            lengths[0] > 0,
            part,
            lambda *_: jax.tree.map(lambda s: jnp.zeros(s.shape, s.dtype), shapes),
            *operands,
        )

    def to_seats(value, groups=None):
        return lax.all_to_all(
            value, "seq", split_axis=0, concat_axis=0, tiled=True, axis_index_groups=groups
        )

    def to_all(value):
        return lax.all_to_all(value, every, split_axis=0, concat_axis=0, tiled=True)

    tail = jnp.concatenate(
        [jnp.pad(down_weight, ((0, tall - fan_rows), (0, 0))), out_weight], 0
    )
    tail = lax.all_gather(tail, "dp", axis=0)

    def columns(weight):
        scaled = (weight.astype(F32) * gain2).astype(BF16)
        scaled = scaled.reshape(held, OUTER, group, depth, fan_rows).transpose(2, 0, 1, 3, 4)
        scaled = jnp.pad(scaled, ((0, 0),) * 4 + ((0, tall - fan_rows),))
        return scaled.reshape(group, held, slab)

    def weights_first():
        pair = jnp.concatenate([columns(gate_weight), columns(up_weight)], -1)
        pair = jnp.concatenate([pair] * OUTER, 0)
        wqkv = (qkv_weight.astype(F32) * gain1).astype(BF16)
        wqkv = wqkv.reshape(held, 3, seats, wide).transpose(2, 0, 1, 3).reshape(seats, held, 3 * wide)
        both = to_seats(jnp.concatenate([pair, wqkv], -1))
        return (
            both[..., : 2 * slab], both[..., 2 * slab :],
            payloads(seat_arr, tokens, first_values, spread, wide),
        )

    pair, wqkv, (own, far_own, *arrived) = together(weights_first)
    pair = lax.all_gather(pair, "dp", axis=0).reshape(depth, OUTER, group, held, 2 * slab)

    def first_leg(arrived, far_own, own, wqkv):
        return (
            [swap(v, m) for v, m in zip(arrived, inner[1:])], swap(far_own, group),
            lax.all_gather(wqkv, "dp", axis=1).reshape(width, 3 * wide),
            swap(own, 1), swap(out_grad, 1),
        )

    arrived, far_own, wqkv, own_b, grad_b = together(first_leg, arrived, far_own, own, wqkv)
    split = 128 * (lanes // 256)

    def second_leg(arrived, far_own, tail):
        pair = CORES * wide
        lower, upper = [], []
        for j in range(1, spread):
            lower.append(swap(arrived[j - 1][..., :split], group))
            at = width + j * pair
            rest = jnp.concatenate([far_own[..., split:width], far_own[..., at : at + pair]], -1)
            upper.append(swap(rest, inner[j]))
        down, wout = tail[:, :tall], tail[:, tall:]
        grads = [swap(out_grad[:1], m) for m in inner[1:]]
        return (
            lower, upper, [swap(v, 1) for v in arrived], swap(far_own, 1), down,
            [wout, swap(wout, group)], grads,
        )

    lower, upper, arrived_b, far_own_b, down_mine, wout, grads_lo = together(
        second_leg, arrived, far_own, tail
    )
    mine = [own, *arrived, far_own, *lower, *upper]
    theirs = [own_b, *arrived_b, far_own_b, *[swap(v, 1) for v in lower + upper]]
    places = [(m, 0) for m in inner + across] + [(m, split) for m in across[1:]]
    order = tuple(places) + tuple((m + 1, lane) for m, lane in places)
    xs = mine + theirs
    near = [(own, own_b)] + list(zip(arrived, arrived_b))
    cosine, sine = rope_tables(total, wide)

    def attend(xs, wqkv, down, wout):
        wout = jnp.stack(wout)
        return (
            attn_fwd(seat_arr, lengths, xs, wqkv, cosine, sine, order, []),
            swap(down, group),
            jnp.stack([wout] + [swap(wout, m) for m in inner[1:]]),
            [swap(out_grad[1:], m) for m in inner[1:]],
        )

    (qkv, ot, *sends, lse, r1), down_far, wout, grads_hi = together(
        attend, xs, wqkv, down_mine, wout
    )

    def spread_out(send, wout, wqkv, *grads):
        return to_seats(send, same_core), swap(wout, 1), swap(wqkv, 1), [[swap(v, 1) for v in g] for g in grads]

    turns = list(range(1, spread)) + [0]
    o, wout_theirs, wqkv_theirs, grads_b = together(
        spread_out, sends[turns[0]], wout, wqkv, grads_lo, grads_hi
    )
    cotangents = [((out_grad,), (grad_b,))]
    cotangents += list(zip(zip(grads_lo, grads_hi), zip(*grads_b)))
    weights = (pair, down_mine, down_far, wout, wout_theirs)
    near_z, sets, near_f, z_parts = [], [], [], []
    for turn, at in enumerate(turns):

        def rows_of(o, near_z, send, weights):
            z = [swap(v, m) for v, m in near_z]
            after = [to_seats(v, same_core) for v in send]
            return (
                feed_forward(seat_arr, *near[at], *cotangents[at], *o, weights, at == 0), z, after
            )

        masks_z = [inner[j] for j in turns[turn - 1 : turn]] if turn else []
        out, z, after = together(
            lambda o, near_z, send, weights: rows_of(
                o, list(zip(near_z, masks_z)), send, weights
            ),
            (o, swap(o, 1)), near_z[-1:], [sends[j] for j in turns[turn + 1 : turn + 2]], weights,
        )
        z_parts += z
        o = after[0] if after else None
        za, zb_lo, zb_hi, fa, fb, *kept = out
        sets.append((*kept[:4], *cotangents[at][0], *cotangents[at][1]))
        if at:
            near_z.append(add_parts(za, [swap(zb_lo, 1), swap(zb_hi, 1)]))
            near_f.append((fa, fb))
    y, o_both, wout = kept[4:]
    dy, dyb, d_o = middle_back(
        y, [za] + z_parts, [swap(zb_lo, 1), swap(zb_hi, 1)], out_grad, wout, wide
    )

    near_fa = jnp.stack([v[0] for v in near_f])
    near_fb = jnp.stack([v[1] for v in near_f])

    def weight_grads(d_o, dyb, kept, near_fa, near_fb):
        return to_seats(d_o), ff_grads(
            seat_arr, kept, o_both, dyb, swap(dyb, 1), near_fa, swap(near_fb, 1),
            (depth, OUTER * group, held, 2 * slab), tall, spread,
        )

    d_o, (pair, down_mine, wout_own, *parcels) = together(
        weight_grads, d_o, dyb, sets, near_fa, near_fb
    )
    pair = lax.psum_scatter(
        pair.reshape(-1, 2 * slab), "dp", scatter_dimension=0, tiled=True
    ).reshape(OUTER * group, held, 2 * slab)

    def attend_back(parcels, d_o, xs):
        out = attn_bwd(
            seat_arr, lengths, xs, wqkv.shape, d_o, cosine, sine, qkv, ot, lse, r1, order,
            across + inner, [],
        )
        return out, [swap(v, m) for v, m in zip(parcels, inner[1:] + across)]

    (e_mine, e_theirs, dwq), landed = together(attend_back, parcels, d_o, xs)

    def first_return(e_theirs, fb, dwq, down_mine, wout_own, landed):
        dwq = to_all(dwq.reshape(devices, held, 3 * wide))
        both = back_to_x(seat_arr, e_mine, swap(e_theirs, 1), wqkv, wqkv_theirs, [])
        far, close = both[:spread], both[spread:]
        got = [swap(close[j], inner[j]) for j in range(1, spread)] + [swap(far[0], across[0])]
        tail = plane_sums(level_arr, down_mine, wout_own, landed)
        output = y + fa.astype(F32) + swap(fb, 1).astype(F32)
        output = output + sum(v[:many].astype(F32) for v in landed[: spread - 1])
        return [close[0]] + got, far, dwq, tail, output.astype(BF16).reshape(tokens.shape)

    got, far, dwq, tail, output = together(
        first_return, e_theirs, fb, dwq, down_mine, wout_own, landed
    )

    def second_return(got, far, pair, dwq, tail):
        tail = [tail[0]] + [swap_depth(tail[k], k) for k in range(1, depth)]
        pair = to_seats(pair)
        return (
            [swap(far[j], across[j]) for j in range(1, spread)],
            token_sums(seat_arr, dy, got, list(range(spread + 1)), wide),
            pair_grads(
                pair.reshape(OUTER, group, held, 2 * slab), gate_weight, up_weight, gain2, depth,
                fan_rows,
            ),
            projection_grads(dwq.reshape(seats, depth, held, 3 * wide), qkv_weight, gain1, wide),
            tail_grads(tail, tall, fan_rows),
        )

    rest, (dx, dv), pair_out, projection_out, (down_grad, out_grad_w) = together(
        second_return, got, far, pair, dwq, tail
    )
    gate_grad, up_grad, gain2_grad = pair_out
    qkv_grad, gain1_grad = projection_out
    d_tokens, d_first = token_grads(
        seat_arr, tokens, dy, dx, dv, rest, list(range(spread + 1, 2 * spread)), wide
    )
    gain1_grad, gain2_grad = gain1_grad.reshape(held), gain2_grad.reshape(held)
    return (
        output, d_tokens, d_first, gain1_grad, qkv_grad, out_grad_w, gain2_grad, gate_grad, up_grad,
        down_grad,
    )


def solution(mesh):
    rows = P(("seq", "dp"), None)
    acts = P("dp", "seq", None)
    gains = P(("seq", "dp"))
    return jax.shard_map(
        local,
        mesh=mesh,
        in_specs=(acts, acts, acts, P("dp"), gains, rows, rows, gains, rows, rows, rows),
        out_specs=(acts, acts, acts, gains, rows, rows, gains, rows, rows, rows),
        check_vma=False,
    )
```
